128 devices in a mesh: tm: 16 (over x, y), rows: 8 (over z, core).
Axes of the slice: x: 4, y: 4, z: 4, core: 2. Of those that a mesh axis runs over, the one named last changes fastest.
Arguments:
- inputs: bfloat16 [32, 32, 128, 256], P('tm', 'rows'), may hold values from -6 to 6
- in_weight: bfloat16 [3, 3, 256, 256], replicated, may hold values from -0.125 to 0.125
- out_weight: bfloat16 [3, 3, 256, 256], replicated, may hold values from -0.0625 to 0.0625
- skip_gain: float32 [256], replicated, may hold values from 0.5 to 1.5
- rates: float32 [256], replicated, may hold values from 0.002 to 1
- step_sizes: float32 [32], P('tm'), may hold values from 0.25 to 4
- cotangent: bfloat16 [32, 32, 128, 256], P('tm', 'rows'), may hold values from -6 to 6
Outputs:
- outputs: bfloat16 [32, 32, 128, 256], P('tm', 'rows')
- grad_inputs: bfloat16 [32, 32, 128, 256], P('tm', 'rows')
- grad_in_weight: float32 [3, 3, 256, 256], replicated
- grad_out_weight: float32 [3, 3, 256, 256], replicated
- grad_skip: float32 [256], replicated
- grad_rates: float32 [256], replicated
- grad_steps: float32 [32], P('tm')
The draws below stay inside these ranges and needn't reach their ends.
All inputs are finite; a program needn't handle non-finite values.
Results may differ from the reference program's by a relative error of at most 0.015.
Values may be sent and summed in bfloat16 or wider, within the bound.
No kernel may reach another device: no remote copies, remote signals or barrier semaphores. Data moves between devices by JAX's collectives and lax.ppermute only.
A program may use at most 128 MiB of HBM per device.

```python
import math
import jax
import jax.numpy as jnp
from jax import lax

C = 256
P_SIZE = 256
W = 128
FRAMES = 32
HEIGHT = 32


def block_levels(own_key, extent, split, low, high):
    def one(dim, shards_of):
        heights = jax.random.uniform(jax.random.fold_in(jax.random.fold_in(own_key, 6), dim), (shards_of,), jnp.float32, low / len(split), high / len(split))
        return jnp.repeat(jnp.exp(heights), extent[dim] // shards_of).reshape((-1,) + (1,) * (len(extent) - dim - 1))

    gain = one(*split[0])
    for cut in split[1:]:
        gain = gain * one(*cut)
    return gain


def scatter_about(key, extent, deviation, limit, shards=(), dtype=jnp.bfloat16):
    entries = deviation * jax.random.normal(key, extent, jnp.float32)
    if shards:
        entries = entries * block_levels(key, extent, shards, -0.22, 0.18)
    return jnp.clip(entries, -limit, limit).astype(dtype)


def setup_inputs(seed: int = 0) -> dict:
    seeds = jax.random.split(jax.random.key(seed), 8)
    inputs = scatter_about(seeds[0], (FRAMES, HEIGHT, W, C), 1.0, 6.0, ((0, 16), (1, 8)))
    in_weight = scatter_about(seeds[1], (3, 3, C, P_SIZE), (9 * C) ** -0.5, 0.125)
    out_weight = scatter_about(seeds[2], (3, 3, P_SIZE, C), (36 * P_SIZE) ** -0.5, 0.0625)
    skip_gain = jnp.clip(jax.random.uniform(seeds[3], (C,), jnp.float32, 0.5, 1.5), 0.5, 1.5)
    rates = jnp.clip(jnp.exp(jax.random.uniform(seeds[4], (P_SIZE,), jnp.float32, math.log(0.002), math.log(1.0))), 0.002, 1.0)
    step_sizes = jnp.clip(jnp.exp(math.log(4.0) - 2.7725887 * jax.random.uniform(seeds[5], (FRAMES,), jnp.float32) ** block_levels(seeds[5], (FRAMES,), ((0, 16),), -0.2, 0.2)), 0.25, 4.0)
    cotangent = scatter_about(seeds[6], (FRAMES, HEIGHT, W, C), 1.0, 6.0, ((0, 16), (1, 8)))
    return {"inputs": inputs, "in_weight": in_weight, "out_weight": out_weight, "skip_gain": skip_gain, "rates": rates, "step_sizes": step_sizes, "cotangent": cotangent}


def shifted(padded, row_tap, col_tap, height, width):
    return padded[:, row_tap:row_tap + height, col_tap:col_tap + width, :]

def pad_all(field):
    return jnp.pad(field, ((0, 0), (1, 1), (1, 1), (0, 0)))

def conv_taps(padded, weight, flipped):
    frames, rows_pad, cols_pad, chans = padded.shape
    height = rows_pad - 2
    width = cols_pad - 2
    result = None
    for row_tap in range(3):
        for col_tap in range(3):
            if flipped:
                window = shifted(padded, 2 - row_tap, 2 - col_tap, height, width)
                matrix = weight[row_tap, col_tap].T
            else:
                window = shifted(padded, row_tap, col_tap, height, width)
                matrix = weight[row_tap, col_tap]
            term = jnp.dot(window.reshape(-1, chans), matrix, preferred_element_type=jnp.float32)
            result = term if result is None else result + term
    return result.reshape(frames, height, width, -1)

def weight_taps(plain, padded_out):
    frames, height, width, chans = plain.shape
    flat = plain.reshape(-1, chans)
    grid_rows = []
    for row_tap in range(3):
        grid_cols = []
        for col_tap in range(3):
            window = shifted(padded_out, 2 - row_tap, 2 - col_tap, height, width).reshape(-1, padded_out.shape[3])
            grid_cols.append(lax.dot_general(flat, window, (((0,), (0,)), ((), ())), preferred_element_type=jnp.float32))
        grid_rows.append(jnp.stack(grid_cols))
    return jnp.stack(grid_rows)

def reference(inputs, in_weight, out_weight, skip_gain, rates, step_sizes, cotangent):
    frames, height, width, chans = inputs.shape
    states_ch = in_weight.shape[3]
    scale = 1.0 / math.sqrt(frames * height * width)
    driven = conv_taps(pad_all(inputs), in_weight, False)
    decays = jnp.exp(-rates[None, :] * step_sizes[:, None])

    def forward_step(carried, pieces):
        drive_now, decay_now = pieces
        fresh = decay_now * carried + drive_now
        return (fresh, (fresh, carried))
    start = jnp.zeros((height, width, states_ch), jnp.float32)
    _, (states, earlier) = lax.scan(forward_step, start, (driven, decays))
    state_bf = states.astype(jnp.bfloat16)
    pre_act = conv_taps(pad_all(state_bf), out_weight, False) + skip_gain * inputs.astype(jnp.float32)
    outputs = jax.nn.gelu(pre_act).astype(jnp.bfloat16)
    grad_z = jax.vjp(jax.nn.gelu, pre_act)[1](cotangent.astype(jnp.float32))[0]
    gz_pad = pad_all(grad_z.astype(jnp.bfloat16))
    grad_out_weight = weight_taps(state_bf, gz_pad) * scale
    grad_state = conv_taps(gz_pad, out_weight, True)

    def backward_step(carried, pieces):
        grad_now, decay_now = pieces
        adjoint_now = grad_now + carried
        return (decay_now * adjoint_now, adjoint_now)
    _, adjoint = lax.scan(backward_step, start, (grad_state, decays), reverse=True)
    adj_pad = pad_all(adjoint.astype(jnp.bfloat16))
    grad_inputs = (conv_taps(adj_pad, in_weight, True) + skip_gain * grad_z).astype(jnp.bfloat16)
    grad_in_weight = weight_taps(inputs, adj_pad) * scale
    grad_skip = lax.optimization_barrier(jnp.sum(grad_z * inputs.astype(jnp.float32), axis=(0, 1, 2))) * scale
    coupling = lax.optimization_barrier(jnp.sum(adjoint * earlier, axis=(1, 2)))
    grad_rates = -lax.optimization_barrier(jnp.sum(coupling * step_sizes[:, None] * decays, axis=0)) * scale
    grad_steps = -lax.optimization_barrier(jnp.sum(coupling * rates[None, :] * decays, axis=1)) / math.sqrt(height * width * states_ch)
    return (outputs, grad_inputs, grad_in_weight, grad_out_weight, grad_skip, grad_rates, grad_steps)
```

```python
import functools
import math

import jax
import jax.numpy as jnp
from jax import lax
from jax.experimental import pallas as pl
from jax.experimental.pallas import tpu as pltpu
from jax.sharding import Mesh, PartitionSpec as P

BF, F32 = jnp.bfloat16, jnp.float32
VM = pl.BlockSpec(memory_space=pltpu.VMEM)
SM = pl.BlockSpec(memory_space=pltpu.SMEM)
FRAMES, HEIGHT, WIDTH, CHANS = 2, 4, 128, 256
BLOCKS = 16
PLACES = HEIGHT * WIDTH // BLOCKS
CHIPS = 64


def sds(shape, dtype):
    return jax.ShapeDtypeStruct(shape, dtype)


def call(body, outs, ins, flops=0):
    nbytes = sum(math.prod(o.shape) * o.dtype.itemsize for o in outs)
    nbytes += sum(math.prod(i.shape) * i.dtype.itemsize for i in ins)
    specs = [SM if i.ndim == 1 else VM for i in ins]
    return pl.pallas_call(
        body,
        out_shape=outs,
        in_specs=specs,
        out_specs=[VM] * len(outs),
        compiler_params=pltpu.CompilerParams(vmem_limit_bytes=40 << 20),
        cost_estimate=pl.CostEstimate(flops=flops, bytes_accessed=nbytes, transcendentals=0),
    )(*ins)


CONV_FLOPS = 2 * 9 * FRAMES * HEIGHT * WIDTH * CHANS * CHANS


def col_shift(v, by):
    turned = pltpu.roll(v, by % WIDTH, 1)
    at = lax.broadcasted_iota(jnp.int32, v.shape, 1)
    return jnp.where(at == (0 if by == 1 else WIDTH - 1), 0.0, turned)


def padded(t, above, mid, below):
    return jnp.concatenate([above[t], mid[t], below[t]], axis=0)


def conv(rows, weight, flipped):
    lhs = jnp.concatenate([rows[a : a + HEIGHT] for a in range(3)], axis=-1)
    lhs = lhs.reshape(HEIGHT * WIDTH, 3 * CHANS)
    parts = []
    for b in range(3):
        if flipped:
            rhs = jnp.concatenate([weight[2 - a, 2 - b] for a in range(3)], axis=1)
            y = lax.dot_general(lhs, rhs, (((1,), (1,)), ((), ())), preferred_element_type=F32)
        else:
            rhs = jnp.concatenate([weight[a, b] for a in range(3)], axis=0)
            y = jnp.dot(lhs, rhs, preferred_element_type=F32)
        parts.append(y.reshape(HEIGHT, WIDTH, CHANS))
    return parts[1] + col_shift(parts[0], 1) + col_shift(parts[2], -1)


def transposed_body(v_ref, out_ref):
    lane = lax.broadcasted_iota(jnp.int32, (CHANS, WIDTH), 1)
    for t in range(FRAMES):
        for h in range(HEIGHT):
            flat = v_ref[t, h].astype(F32).T
            at = pl.ds((t * HEIGHT + h) * WIDTH, WIDTH)
            left = jnp.where(lane == 0, 0.0, pltpu.roll(flat, 1, 1))
            right = jnp.where(lane == WIDTH - 1, 0.0, pltpu.roll(flat, WIDTH - 1, 1))
            out_ref[0:CHANS, at] = left.astype(BF)
            out_ref[CHANS : 2 * CHANS, at] = flat.astype(BF)
            out_ref[2 * CHANS : 3 * CHANS, at] = right.astype(BF)


def transposed(v):
    return call(transposed_body, [sds((3 * CHANS, FRAMES * HEIGHT * WIDTH), BF)], [v])[0]


def decay(rates_ref, step):
    return jnp.exp(-rates_ref[...] * step)


def drive_body(steps, x, above, below, weight, rates, local, send):
    d1 = decay(rates, steps[1])
    first = conv(padded(0, above, x, below), weight, False)
    local[0] = first
    last = d1 * first + conv(padded(1, above, x, below), weight, False)
    local[1] = last
    send[:, 0:PLACES, :] = last.reshape(BLOCKS, PLACES, CHANS).astype(BF)
    total = jnp.full((BLOCKS, 16, CHANS), steps[0] + steps[1], F32)
    row = lax.broadcasted_iota(jnp.int32, total.shape, 1)
    one = total.astype(BF).astype(F32)
    two = (total - one).astype(BF).astype(F32)
    three = total - one - two
    send[:, PLACES : PLACES + 16, :] = jnp.where(
        row == 0, one, jnp.where(row == 1, two, jnp.where(row == 2, three, 0.0))
    ).astype(BF)


def forward_scan_body(got, rates, send, block_decays):
    carry = jnp.zeros((PLACES, CHANS), F32)
    for k in range(BLOCKS):
        send[k] = carry.astype(BF)
        span = jnp.sum(got[k, PLACES : PLACES + 16, :].astype(F32), axis=0, keepdims=True)
        d = jnp.exp(-rates[...] * span)
        block_decays[pl.ds(k, 1), :] = d
        carry = d * carry + got[k, 0:PLACES, :].astype(F32)


def backward_scan_body(got, block_decays, send):
    carry = jnp.zeros((PLACES, CHANS), F32)
    for k in reversed(range(BLOCKS)):
        send[k] = carry.astype(BF)
        carry = block_decays[pl.ds(k, 1), :] * carry + got[k].astype(F32)


def states_body(steps, local, carry, rates, state, first, last, state_f):
    d0, d1 = decay(rates, steps[0]), decay(rates, steps[1])
    c = carry[...].reshape(HEIGHT, WIDTH, CHANS).astype(F32)
    s0 = local[0] + d0 * c
    s1 = local[1] + (d0 * d1) * c
    state_f[...] = s0
    for t, s in enumerate((s0, s1)):
        s = s.astype(BF)
        state[t] = s
        first[t] = s[0:1]
        last[t] = s[HEIGHT - 1 :]


GELU_A = math.sqrt(2 / math.pi)


def output_body(state, above, below, x, cot, weight, gain, out, gz_f, gz, first, last, skip):
    total = jnp.zeros((1, CHANS), F32)
    for t in range(FRAMES):
        xt = x[t].astype(F32)
        z = conv(padded(t, above, state, below), weight, False) + gain[...] * xt
        th = jnp.tanh(GELU_A * (z + 0.044715 * (z * z * z)))
        half = 0.5 * (1.0 + th)
        out[t] = (z * half).astype(BF)
        slope = half + 0.5 * z * (1.0 - th * th) * (GELU_A * (1.0 + 3 * 0.044715 * (z * z)))
        g = cot[t].astype(F32) * slope
        gz_f[t] = g
        gb = g.astype(BF)
        gz[t] = gb
        first[t] = gb[0:1]
        last[t] = gb[HEIGHT - 1 :]
        total += jnp.sum((g * xt).reshape(-1, CHANS), axis=0, keepdims=True)
    skip[...] = spread(total, None)


def spread(vector, extra):
    row = lax.broadcasted_iota(jnp.int32, (8, 128), 0) % 4
    low = jnp.broadcast_to(vector[:, 0:128], (8, 128))
    high = jnp.broadcast_to(vector[:, 128:256], (8, 128))
    out = jnp.where(row == 0, low, jnp.where(row == 1, high, 0.0))
    if extra is not None:
        out = jnp.where(row == 2, extra, out)
    return out


def split_pairs(both):
    row = lax.broadcasted_iota(jnp.int32, (8, 128), 0)
    top = both.astype(BF).astype(F32)
    return jnp.where(row < 4, top, both - top)


def joined(pairs):
    return pairs + pltpu.roll(pairs, 4, 0)


def adjoint_body(steps, gz, above, below, weight, rates, local, send):
    d0, d1 = decay(rates, steps[0]), decay(rates, steps[1])
    a1 = conv(padded(1, above, gz, below), weight, True)
    local[1] = a1
    a0 = conv(padded(0, above, gz, below), weight, True) + d1 * a1
    local[0] = a0
    send[...] = (d0 * a0).reshape(BLOCKS, PLACES, CHANS).astype(BF)


def adjoints_body(scale, steps, place, local, incoming, state_f, carry, rates, adj, first, last, small):
    d0, d1 = decay(rates, steps[0]), decay(rates, steps[1])
    c = incoming[...].reshape(HEIGHT, WIDTH, CHANS).astype(F32)
    a0 = local[0] + d1 * c
    a1 = local[1] + c
    earlier = carry[...].reshape(HEIGHT, WIDTH, CHANS).astype(F32)
    for t, s in enumerate((a0, a1)):
        s = s.astype(BF)
        adj[t] = s
        first[t] = s[0:1]
        last[t] = s[HEIGHT - 1 :]
    k0 = jnp.sum((a0 * earlier).reshape(-1, CHANS), axis=0, keepdims=True) * d0
    k1 = jnp.sum((a1 * state_f[...]).reshape(-1, CHANS), axis=0, keepdims=True) * d1
    rate_part = (k0 * steps[0] + k1 * steps[1]) * (-scale[0])
    s0 = jnp.sum(k0 * rates[...], axis=1, keepdims=True) * (-scale[1])
    s1 = jnp.sum(k1 * rates[...], axis=1, keepdims=True) * (-scale[1])
    lane = lax.broadcasted_iota(jnp.int32, (8, 128), 1)
    at = place[0] * FRAMES
    extra = jnp.where(lane == at, s0, jnp.where(lane == at + 1, s1, 0.0))
    small[...] = spread(rate_part, extra)


def grad_inputs_body(adj, above, below, weight, gain, gz_f, out):
    for t in range(FRAMES):
        out[t] = (conv(padded(t, above, adj, below), weight, True) + gain[...] * gz_f[t]).astype(BF)


def weight_grad_body(scale, flat, field, above, below, small, out):
    for a in range(3):
        rhs = jnp.concatenate(
            [padded(t, above, field, below)[2 - a : 2 - a + HEIGHT] for t in range(FRAMES)], axis=0
        ).reshape(FRAMES * HEIGHT * WIDTH, CHANS)
        for b in range(3):
            g = jnp.dot(flat[b * CHANS : (b + 1) * CHANS, :], rhs, preferred_element_type=F32)
            g = g * scale[0]
            tap = 3 * a + b
            for lg in range(2):
                part = g[:, lg * 128 : (lg + 1) * 128].reshape(32, 8, 128)
                out[:, lg, tap * 8 : tap * 8 + 8, :] = part.astype(BF)
    out[:, :, 72:80, :] = jnp.zeros((32, 2, 8, 128), BF)
    out[0, 0, 72:80, :] = split_pairs(small[...] * scale[1]).astype(BF)


def pair_sum_body(core, out_own, out_got, in_own, in_got, send):
    def add(own, got):
        send[...] = (own[...].astype(F32) + got[...].astype(F32)).astype(BF)
        pairs = own[0, 0, 72:80, :].astype(F32) + got[0, 0, 72:80, :].astype(F32)
        send[0, 0, 72:80, :] = split_pairs(joined(pairs)).astype(BF)

    @pl.when(core[0] == 0)
    def _():
        add(out_own, out_got)

    @pl.when(core[0] == 1)
    def _():
        add(in_own, in_got)


def all_sum_body(got, send):
    total = jnp.zeros((80, 128), F32)
    for k in range(CHIPS):
        total = total + got[k].astype(F32)
    extras = split_pairs(joined(total[72:80]))
    total = jnp.concatenate([total[0:72], extras], axis=0).astype(BF)
    send[...] = jnp.broadcast_to(total[None], (CHIPS, 80, 128))


def unpack_body(core, own, got, grad_in, grad_out, small_in, small_out):
    def write(src, grad, small):
        for tap in range(9):
            for lg in range(2):
                part = src[:, lg, tap * 8 : tap * 8 + 8, :].astype(F32).reshape(CHANS, 128)
                grad[tap // 3, tap % 3, :, lg * 128 : (lg + 1) * 128] = part
        small[...] = joined(src[0, 0, 72:80, :].astype(F32))

    @pl.when(core[0] == 0)
    def _():
        write(own, grad_out, small_out)
        write(got, grad_in, small_in)

    @pl.when(core[0] == 1)
    def _():
        write(own, grad_in, small_in)
        write(got, grad_out, small_out)


ROWS_AXES = ("z", "core")
TM_AXES = ("x", "y")


def halos(first, last):
    count = 8
    up = [(i, i + 1) for i in range(count - 1)]
    down = [(i + 1, i) for i in range(count - 1)]
    above = lax.ppermute(last, ROWS_AXES, up)
    below = lax.ppermute(first, ROWS_AXES, down)
    return above, below


def swap(chunks, axes):
    return lax.all_to_all(chunks, axes, 0, 0)


def on_device(inputs, in_weight, out_weight, skip_gain, rates, step_sizes, cotangent):
    scale = 1.0 / math.sqrt(32 * 32 * 128)
    step_scale = 1.0 / math.sqrt(1048576)
    gain, rates = skip_gain[None, :], rates[None, :]
    place = (lax.axis_index("x") * 4 + lax.axis_index("y")).astype(jnp.int32)[None]
    core = lax.axis_index("core").astype(jnp.int32)[None]
    field = (FRAMES, HEIGHT, WIDTH, CHANS)
    edge = sds((FRAMES, 1, WIDTH, CHANS), BF)
    chunk = sds((BLOCKS, PLACES, CHANS), BF)
    packed = sds((32, 2, 80, 128), BF)
    small = sds((8, 128), F32)

    x_above, x_below = halos(inputs[:, 0:1], inputs[:, HEIGHT - 1 :])
    inputs_t = transposed(inputs)
    local, send = call(
        drive_body,
        [sds(field, F32), sds((BLOCKS, PLACES + 16, CHANS), BF)],
        [step_sizes, inputs, x_above, x_below, in_weight, rates],
        CONV_FLOPS,
    )
    got = swap(send, TM_AXES)
    send, block_decays = call(forward_scan_body, [chunk, sds((BLOCKS, CHANS), F32)], [got, rates])
    carry = swap(send, TM_AXES)
    state, first, last, state_f = call(
        states_body,
        [sds(field, BF), edge, edge, sds(field[1:], F32)],
        [step_sizes, local, carry, rates],
    )
    s_above, s_below = halos(first, last)
    state_t = transposed(state)
    outputs, gz_f, gz, first, last, skip_part = call(
        output_body,
        [sds(field, BF), sds(field, F32), sds(field, BF), edge, edge, small],
        [state, s_above, s_below, inputs, cotangent, out_weight, gain],
        CONV_FLOPS,
    )
    g_above, g_below = halos(first, last)
    local_adj, send = call(
        adjoint_body,
        [sds(field, F32), chunk],
        [step_sizes, gz, g_above, g_below, out_weight, rates],
        CONV_FLOPS,
    )
    got = swap(send, TM_AXES)
    (out_part,) = call(
        weight_grad_body,
        [packed],
        [jnp.array([scale, scale], F32), state_t, gz, g_above, g_below, skip_part],
        CONV_FLOPS,
    )
    to_first = [(2 * k + 1, 2 * k) for k in range(4)]
    to_second = [(2 * k, 2 * k + 1) for k in range(4)]
    out_got = lax.ppermute(out_part, ROWS_AXES, to_first)
    (send,) = call(backward_scan_body, [chunk], [got, block_decays])
    incoming = swap(send, TM_AXES)
    adj, first, last, small_part = call(
        adjoints_body,
        [sds(field, BF), edge, edge, small],
        [
            jnp.array([scale, step_scale], F32),
            step_sizes,
            place,
            local_adj,
            incoming,
            state_f,
            carry,
            rates,
        ],
    )
    a_above, a_below = halos(first, last)
    (in_part,) = call(
        weight_grad_body,
        [packed],
        [jnp.array([scale, 1.0], F32), inputs_t, adj, a_above, a_below, small_part],
        CONV_FLOPS,
    )
    in_got = lax.ppermute(in_part, ROWS_AXES, to_second)
    (grad_inputs,) = call(
        grad_inputs_body,
        [sds(field, BF)],
        [adj, a_above, a_below, in_weight, gain, gz_f],
        CONV_FLOPS,
    )
    (send,) = call(pair_sum_body, [packed], [core, out_part, out_got, in_part, in_got])
    got = swap(send.reshape(CHIPS, 80, 128), ("x", "y", "z"))
    (send,) = call(all_sum_body, [sds((CHIPS, 80, 128), BF)], [got])
    own = swap(send, ("x", "y", "z")).reshape(packed.shape)
    other = lax.ppermute(own, "core", [(0, 1), (1, 0)])
    weights = sds((3, 3, CHANS, CHANS), F32)
    grad_in_weight, grad_out_weight, small_in, small_out = call(
        unpack_body, [weights, weights, small, small], [core, own, other]
    )
    grad_skip = small_out[0:2].reshape(CHANS)
    grad_rates = small_in[0:2].reshape(CHANS)
    grad_steps = lax.dynamic_slice(small_in[2], (place[0] * FRAMES,), (FRAMES,))
    return (
        outputs,
        grad_inputs,
        grad_in_weight,
        grad_out_weight,
        grad_skip,
        grad_rates,
        grad_steps,
    )


def solution(mesh):
    fine = Mesh(mesh.devices.reshape(4, 4, 4, 2), ("x", "y", "z", "core"))
    spread_out = P(TM_AXES, ROWS_AXES, None, None)
    placed = (spread_out, P(), P(), P(), P(), P(TM_AXES), spread_out)
    return jax.shard_map(
        on_device,
        mesh=fine,
        in_specs=placed,
        out_specs=(spread_out, spread_out, P(), P(), P(), P(), P(TM_AXES)),
        check_vma=False,
    )
```

```python
import math

import jax
import jax.numpy as jnp
from jax import lax
from jax.experimental import pallas as pl
from jax.experimental.pallas import tpu as pltpu
from jax.sharding import Mesh, PartitionSpec as P

BF, F32 = jnp.bfloat16, jnp.float32
VM = pl.BlockSpec(memory_space=pltpu.VMEM)
SM = pl.BlockSpec(memory_space=pltpu.SMEM)
FRAMES, HEIGHT, WIDTH, CHANS = 2, 4, 128, 256
WIDE, WIDER = HEIGHT + 2, HEIGHT + 4
BLOCKS = 16
PLACES = WIDE * WIDTH // BLOCKS
NOTE = 8
CHIPS = 64
GROUPS = 32
TAPS = 72
PACK = TAPS + 8


def sds(shape, dtype):
    return jax.ShapeDtypeStruct(shape, dtype)


def call(body, outs, ins, flops=0, scratch=()):
    nbytes = sum(math.prod(o.shape) * o.dtype.itemsize for o in outs)
    nbytes += sum(math.prod(i.shape) * i.dtype.itemsize for i in ins)
    specs = [SM if i.ndim == 1 else VM for i in ins]
    return pl.pallas_call(
        body,
        out_shape=outs,
        in_specs=specs,
        out_specs=[VM] * len(outs),
        scratch_shapes=list(scratch),
        compiler_params=pltpu.CompilerParams(vmem_limit_bytes=40 << 20),
        cost_estimate=pl.CostEstimate(flops=flops, bytes_accessed=nbytes, transcendentals=0),
    )(*ins)


ROW_FLOPS = 2 * 9 * FRAMES * WIDTH * CHANS * CHANS


def col_shift(v, by):
    turned = pltpu.roll(v, by % WIDTH, 1)
    at = lax.broadcasted_iota(jnp.int32, v.shape, 1)
    return jnp.where(at == (0 if by == 1 else WIDTH - 1), 0.0, turned)


def conv(rows, weight, flipped):
    height = rows.shape[0] - 2
    lhs = jnp.concatenate([rows[a : a + height] for a in range(3)], axis=-1)
    lhs = lhs.reshape(height * WIDTH, 3 * CHANS)
    parts = []
    for b in range(3):
        if flipped:
            rhs = jnp.concatenate([weight[2 - a, 2 - b] for a in range(3)], axis=1)
            y = lax.dot_general(lhs, rhs, (((1,), (1,)), ((), ())), preferred_element_type=F32)
        else:
            rhs = jnp.concatenate([weight[a, b] for a in range(3)], axis=0)
            y = jnp.dot(lhs, rhs, preferred_element_type=F32)
        parts.append(y.reshape(height, WIDTH, CHANS))
    return parts[1] + col_shift(parts[0], 1) + col_shift(parts[2], -1)


def inside(spot, rows):
    top = jnp.where(spot[1] == 1, 0.0, rows[0:1])
    bottom = jnp.where(spot[2] == 1, 0.0, rows[WIDE - 1 :])
    return jnp.concatenate([top, rows[1 : WIDE - 1], bottom], axis=0)


def transpose_rows(v_ref, out_ref, rows):
    lane = lax.broadcasted_iota(jnp.int32, (CHANS, WIDTH), 1)
    for t in range(FRAMES):
        for h in range(rows):
            flat = v_ref[t, h].astype(F32).T
            at = pl.ds((t * rows + h) * WIDTH, WIDTH)
            left = jnp.where(lane == 0, 0.0, pltpu.roll(flat, 1, 1))
            right = jnp.where(lane == WIDTH - 1, 0.0, pltpu.roll(flat, WIDTH - 1, 1))
            out_ref[0:CHANS, at] = left.astype(BF)
            out_ref[CHANS : 2 * CHANS, at] = flat.astype(BF)
            out_ref[2 * CHANS : 3 * CHANS, at] = right.astype(BF)


def transposed_body(v_ref, out_ref):
    transpose_rows(v_ref, out_ref, WIDER)


def decay(rates_ref, step):
    return jnp.exp(-rates_ref[...] * step)


def place_halos(spot, from_core, from_chip, above, below):
    @pl.when(spot[0] == 0)
    def _():
        above[...] = from_chip[...]
        below[...] = from_core[...]

    @pl.when(spot[0] == 1)
    def _():
        above[...] = from_core[...]
        below[...] = from_chip[...]

    @pl.when(spot[1] == 1)
    def _():
        above[...] = jnp.zeros_like(above)

    @pl.when(spot[2] == 1)
    def _():
        below[...] = jnp.zeros_like(below)


def drive_body(spot, steps, x, from_core, from_chip, weight, rates, local, send, wider):
    place_halos(spot, from_core, from_chip, wider.at[:, 0:2], wider.at[:, WIDER - 2 :])
    wider[:, 2 : WIDER - 2] = x[...]
    d1 = decay(rates, steps[1])
    first = inside(spot, conv(wider[0], weight, False))
    local[0] = first
    last = d1 * first + inside(spot, conv(wider[1], weight, False))
    local[1] = last
    send[:, 0:PLACES, :] = last.reshape(BLOCKS, PLACES, CHANS).astype(BF)
    total = jnp.full((BLOCKS, NOTE, CHANS), steps[0] + steps[1], F32)
    row = lax.broadcasted_iota(jnp.int32, total.shape, 1)
    one = total.astype(BF).astype(F32)
    two = (total - one).astype(BF).astype(F32)
    three = total - one - two
    send[:, PLACES : PLACES + NOTE, :] = jnp.where(
        row == 0, one, jnp.where(row == 1, two, jnp.where(row == 2, three, 0.0))
    ).astype(BF)


def forward_scan_body(got, rates, send, block_decays):
    carry = jnp.zeros((PLACES, CHANS), F32)
    for k in range(BLOCKS):
        send[k] = carry.astype(BF)
        span = jnp.sum(got[k, PLACES : PLACES + NOTE, :].astype(F32), axis=0, keepdims=True)
        d = jnp.exp(-rates[...] * span)
        block_decays[pl.ds(k, 1), :] = d
        carry = d * carry + got[k, 0:PLACES, :].astype(F32)


def backward_scan_body(got, block_decays, send):
    carry = jnp.zeros((PLACES, CHANS), F32)
    for k in reversed(range(BLOCKS)):
        send[k] = carry.astype(BF)
        carry = block_decays[pl.ds(k, 1), :] * carry + got[k].astype(F32)


GELU_A = math.sqrt(2 / math.pi)


def spread(vector, extra):
    row = lax.broadcasted_iota(jnp.int32, (8, 128), 0) % 4
    low = jnp.broadcast_to(vector[:, 0:128], (8, 128))
    high = jnp.broadcast_to(vector[:, 128:256], (8, 128))
    low, high = (jnp.where(row == 0, v, 0.0) for v in (low, high))
    if extra is not None:
        low = jnp.where(row == 1, extra, low)
    return low, high


def split_pairs(both):
    row = lax.broadcasted_iota(jnp.int32, (8, 128), 0)
    top = both.astype(BF).astype(F32)
    return jnp.where(row < 4, top, both - top)


def joined(pairs):
    return pairs + pltpu.roll(pairs, 4, 0)


def middle_body(
    spot, steps, local, carry, x, cot, weight, gain, rates,
    out, gz_f, gz, state, state_f, local_adj, send, small,
):
    d0, d1 = decay(rates, steps[0]), decay(rates, steps[1])
    c = carry[...].reshape(WIDE, WIDTH, CHANS).astype(F32)
    s0 = local[0] + d0 * c
    state_f[...] = s0
    state[0] = s0.astype(BF)
    state[1] = (local[1] + (d0 * d1) * c).astype(BF)
    total = jnp.zeros((1, CHANS), F32)
    later = None
    for t in (1, 0):
        xt = x[t].astype(F32)
        z = conv(state[t], weight, False) + gain[...] * xt
        th = jnp.tanh(GELU_A * (z + 0.044715 * (z * z * z)))
        half = 0.5 * (1.0 + th)
        out[t] = (z * half).astype(BF)
        slope = half + 0.5 * z * (1.0 - th * th) * (GELU_A * (1.0 + 3 * 0.044715 * (z * z)))
        g = cot[t].astype(F32) * slope
        gz_f[t] = g
        gb = g.astype(BF)
        gz[t] = gb
        total += jnp.sum((g * xt).reshape(-1, CHANS), axis=0, keepdims=True)
        blank = jnp.zeros((2, WIDTH, CHANS), BF)
        grad = inside(spot, conv(jnp.concatenate([blank, gb, blank], axis=0), weight, True))
        later = grad if later is None else grad + d1 * later
        local_adj[t] = later
    send[...] = (d0 * later).reshape(BLOCKS, PLACES, CHANS).astype(BF)
    small[0], small[1] = spread(total, None)


def pack_grad(core, g, a, scale, mine, theirs):
    for b in range(3):
        tap = (3 * a + b) * 8
        low = g[b * CHANS : (b + 1) * CHANS, 0:128] * scale
        high = g[b * CHANS : (b + 1) * CHANS, 128:256] * scale
        mine[:, tap : tap + 8, :] = (
            jnp.where(core == 0, low, high).astype(BF).reshape(GROUPS, 8, 128)
        )
        theirs[:, tap : tap + 8, :] = (
            jnp.where(core == 0, high, low).astype(BF).reshape(GROUPS, 8, 128)
        )


def pack_small(core, low, high, scale, mine, theirs):
    blank = jnp.zeros((GROUPS, 8, 128), BF)
    for ref, half in (
        (mine, jnp.where(core == 0, low, high)),
        (theirs, jnp.where(core == 0, high, low)),
    ):
        ref[:, TAPS:PACK, :] = blank
        ref[0, TAPS:PACK, :] = split_pairs(half * scale).astype(BF)


def out_grad_body(spot, scale, state, gz, small, mine, theirs, flat):
    transpose_rows(state, flat, WIDE)
    rhs = gz[...].reshape(FRAMES * HEIGHT * WIDTH, CHANS)
    for a in range(3):
        lhs = jnp.concatenate(
            [flat[:, pl.ds((t * WIDE + a) * WIDTH, HEIGHT * WIDTH)] for t in range(FRAMES)], axis=1
        )
        g = jnp.dot(lhs, rhs, preferred_element_type=F32)
        pack_grad(spot[0], g, a, scale[0], mine, theirs)
    pack_small(spot[0], small[0], small[1], scale[0], mine, theirs)


def in_grad_body(
    spot, scale, steps, local, incoming, state_f, carry, rates, flat,
    mine, theirs, adj, to_core, to_chip,
):
    d0, d1 = decay(rates, steps[0]), decay(rates, steps[1])
    c = incoming[...].reshape(WIDE, WIDTH, CHANS).astype(F32)
    a0 = local[0] + d1 * c
    a1 = local[1] + c
    earlier = carry[...].reshape(WIDE, WIDTH, CHANS).astype(F32)
    for t, s in enumerate((a0, a1)):
        adj[t] = s.astype(BF)

    @pl.when(spot[0] == 0)
    def _():
        to_chip[...] = adj[:, 0:2]
        to_core[...] = adj[:, WIDE - 2 :]

    @pl.when(spot[0] == 1)
    def _():
        to_core[...] = adj[:, 0:2]
        to_chip[...] = adj[:, WIDE - 2 :]

    rhs = adj[...].reshape(FRAMES * WIDE * WIDTH, CHANS)
    for a in range(3):
        lhs = jnp.concatenate(
            [flat[:, pl.ds((t * WIDER + a) * WIDTH, WIDE * WIDTH)] for t in range(FRAMES)], axis=1
        )
        g = jnp.dot(lhs, rhs, preferred_element_type=F32)
        pack_grad(spot[0], g, a, scale[0], mine, theirs)
    k0 = jnp.sum((a0 * earlier).reshape(-1, CHANS), axis=0, keepdims=True) * d0
    k1 = jnp.sum((a1 * state_f[...]).reshape(-1, CHANS), axis=0, keepdims=True) * d1
    rate_part = (k0 * steps[0] + k1 * steps[1]) * (-scale[0])
    s0 = jnp.sum(k0 * rates[...], axis=1, keepdims=True) * (-scale[1])
    s1 = jnp.sum(k1 * rates[...], axis=1, keepdims=True) * (-scale[1])
    lane = lax.broadcasted_iota(jnp.int32, (8, 128), 1)
    at = spot[3] * FRAMES
    low, high = spread(rate_part, jnp.where(lane == at, s0, jnp.where(lane == at + 1, s1, 0.0)))
    pack_small(spot[0], low, high, 1.0, mine, theirs)


def grad_inputs_body(spot, adj, from_core, from_chip, weight, gain, gz_f, out, above, below):
    place_halos(spot, from_core, from_chip, above, below)
    for t in range(FRAMES):
        up = (adj[t, 0:2].astype(F32) + above[t].astype(F32)).astype(BF)
        down = (adj[t, WIDE - 2 :].astype(F32) + below[t].astype(F32)).astype(BF)
        rows = jnp.concatenate([up, adj[t, 2 : WIDE - 2], down], axis=0)
        out[t] = (conv(rows, weight, True) + gain[...] * gz_f[t]).astype(BF)


def pair_sum_body(out_own, out_got, in_own, in_got, send):
    for g, (own, got) in enumerate(((out_own, out_got), (in_own, in_got))):
        send[g] = (own[...].astype(F32) + got[...].astype(F32)).astype(BF)
        pairs = own[0, TAPS:PACK, :].astype(F32) + got[0, TAPS:PACK, :].astype(F32)
        send[g, 0, TAPS:PACK, :] = split_pairs(joined(pairs)).astype(BF)


def all_sum_body(got, send):
    total = jnp.zeros((PACK, 128), F32)
    for k in range(CHIPS):
        total = total + got[k].astype(F32)
    extras = split_pairs(joined(total[TAPS:PACK]))
    total = jnp.concatenate([total[0:TAPS], extras], axis=0).astype(BF)
    send[...] = jnp.broadcast_to(total[None], (CHIPS, PACK, 128))


def unpack_body(spot, own, got, grad_in, grad_out, skip, rate, step):
    def write(src, lg):
        for g, grad, vector in ((0, grad_out, skip), (1, grad_in, rate)):
            for tap in range(9):
                part = src[g, :, tap * 8 : tap * 8 + 8, :].astype(F32).reshape(CHANS, 128)
                grad[tap // 3, tap % 3, :, lg * 128 : (lg + 1) * 128] = part
            extras = joined(src[g, 0, TAPS:PACK, :].astype(F32))
            vector[lg : lg + 1, :] = extras[0:1]
            if g == 1 and lg == 0:
                turned = pltpu.roll(extras, (128 - spot[3] * FRAMES) % 128, 1)
                step[...] = turned[1:2, 0:FRAMES]

    @pl.when(spot[0] == 0)
    def _():
        write(own, 0)
        write(got, 1)

    @pl.when(spot[0] == 1)
    def _():
        write(own, 1)
        write(got, 0)


ROWS_AXES = ("z", "core")
TM_AXES = ("x", "y")
CORE_PAIRS = [(i, i ^ 1) for i in range(8)]
CHIP_PAIRS = [(i, (i + 1) % 8 if i % 2 else (i - 1) % 8) for i in range(8)]


def halos(to_core, to_chip):
    from_chip = lax.ppermute(to_chip, ROWS_AXES, CHIP_PAIRS)
    from_core = lax.ppermute(to_core, ROWS_AXES, CORE_PAIRS)
    return from_core, from_chip


def swap(chunks, axes):
    return lax.all_to_all(chunks, axes, 0, 0)


def on_device(inputs, in_weight, out_weight, skip_gain, rates, step_sizes, cotangent):
    scale = 1.0 / math.sqrt(32 * 32 * 128)
    step_scale = 1.0 / math.sqrt(1048576)
    scales = jnp.array([scale, step_scale], F32)
    gain, rates = skip_gain[None, :], rates[None, :]
    core, z = lax.axis_index("core"), lax.axis_index("z")
    place = lax.axis_index("x") * 4 + lax.axis_index("y")
    top, bottom = (z == 0) & (core == 0), (z == 3) & (core == 1)
    spot = jnp.stack([core, top, bottom, place]).astype(jnp.int32)
    field = (FRAMES, HEIGHT, WIDTH, CHANS)
    wide = (FRAMES, WIDE, WIDTH, CHANS)
    edge = sds((FRAMES, 2, WIDTH, CHANS), BF)
    chunk = sds((BLOCKS, PLACES, CHANS), BF)
    packed = sds((GROUPS, PACK, 128), BF)

    to_core = lax.dynamic_slice(inputs, (0, 2 - 2 * core, 0, 0), edge.shape)
    to_chip = lax.dynamic_slice(inputs, (0, 2 * core, 0, 0), edge.shape)
    from_core, from_chip = halos(to_core, to_chip)
    local, send, wider = call(
        drive_body,
        [
            sds(wide, F32),
            sds((BLOCKS, PLACES + NOTE, CHANS), BF),
            sds((FRAMES, WIDER, WIDTH, CHANS), BF),
        ],
        [spot, step_sizes, inputs, from_core, from_chip, in_weight, rates],
        WIDE * ROW_FLOPS,
    )
    got = swap(send, TM_AXES)
    (flat,) = call(
        transposed_body, [sds((3 * CHANS, FRAMES * WIDER * WIDTH), BF)], [wider], 4 * ROW_FLOPS
    )
    send, block_decays = call(forward_scan_body, [chunk, sds((BLOCKS, CHANS), F32)], [got, rates])
    carry = swap(send, TM_AXES)
    outputs, gz_f, gz, state, state_f, local_adj, send, small = call(
        middle_body,
        [
            sds(field, BF),
            sds(field, F32),
            sds(field, BF),
            sds(wide, BF),
            sds(wide[1:], F32),
            sds(wide, F32),
            chunk,
            sds((2, 8, 128), F32),
        ],
        [spot, step_sizes, local, carry, inputs, cotangent, out_weight, gain, rates],
        (HEIGHT + WIDE) * ROW_FLOPS,
    )
    got = swap(send, TM_AXES)
    out_mine, out_theirs = call(
        out_grad_body,
        [packed, packed],
        [spot, scales, state, gz, small],
        HEIGHT * ROW_FLOPS,
        [pltpu.VMEM((3 * CHANS, FRAMES * WIDE * WIDTH), BF)],
    )
    out_got = lax.ppermute(out_theirs, ROWS_AXES, CORE_PAIRS)
    (send,) = call(backward_scan_body, [chunk], [got, block_decays])
    incoming = swap(send, TM_AXES)
    in_mine, in_theirs, adj, to_core, to_chip = call(
        in_grad_body,
        [packed, packed, sds(wide, BF), edge, edge],
        [spot, scales, step_sizes, local_adj, incoming, state_f, carry, rates, flat],
        WIDE * ROW_FLOPS,
    )
    in_got = lax.ppermute(in_theirs, ROWS_AXES, CORE_PAIRS)
    (send,) = call(
        pair_sum_body, [sds((2, GROUPS, PACK, 128), BF)], [out_mine, out_got, in_mine, in_got]
    )
    got = swap(send.reshape(CHIPS, PACK, 128), ("x", "y", "z"))
    from_core, from_chip = halos(to_core, to_chip)
    (grad_inputs,) = call(
        grad_inputs_body,
        [sds(field, BF)],
        [spot, adj, from_core, from_chip, in_weight, gain, gz_f],
        HEIGHT * ROW_FLOPS,
        [pltpu.VMEM(edge.shape, BF), pltpu.VMEM(edge.shape, BF)],
    )
    (send,) = call(all_sum_body, [sds((CHIPS, PACK, 128), BF)], [got])
    own = swap(send, ("x", "y", "z")).reshape(2, GROUPS, PACK, 128)
    other = lax.ppermute(own, ROWS_AXES, CORE_PAIRS)
    weights = sds((3, 3, CHANS, CHANS), F32)
    half = sds((2, 128), F32)
    grad_in_weight, grad_out_weight, grad_skip, grad_rates, grad_steps = call(
        unpack_body, [weights, weights, half, half, sds((1, FRAMES), F32)], [spot, own, other]
    )
    return (
        outputs,
        grad_inputs,
        grad_in_weight,
        grad_out_weight,
        grad_skip.reshape(CHANS),
        grad_rates.reshape(CHANS),
        grad_steps.reshape(FRAMES),
    )


def solution(mesh):
    fine = Mesh(mesh.devices.reshape(4, 4, 4, 2), ("x", "y", "z", "core"))
    spread_out = P(TM_AXES, ROWS_AXES, None, None)
    placed = (spread_out, P(), P(), P(), P(), P(TM_AXES), spread_out)
    return jax.shard_map(
        on_device,
        mesh=fine,
        in_specs=placed,
        out_specs=(spread_out, spread_out, P(), P(), P(), P(), P(TM_AXES)),
        check_vma=False,
    )
```

```python
import functools
import math

import jax
import jax.numpy as jnp
from jax import lax
from jax.experimental import pallas as pl
from jax.experimental.pallas import tpu as pltpu
from jax.sharding import Mesh, PartitionSpec as P

BF, F32 = jnp.bfloat16, jnp.float32
VM = pl.BlockSpec(memory_space=pltpu.VMEM)
HB = pl.BlockSpec(memory_space=pltpu.HBM)
GRANT = 24 << 20
FRAMES, HEIGHT, WIDTH, CHANS = 2, 4, 128, 256
WIDE, WIDER = HEIGHT + 2, HEIGHT + 4
BLOCKS = 16
PLACES = WIDE * WIDTH // BLOCKS
NOTE = 8
CHIPS = 64
GROUPS = 32
TAPS = 72
PACK = TAPS + 8


def sds(shape, dtype):
    return jax.ShapeDtypeStruct(shape, dtype)


def call(body, outs, ins, flops=0, scratch=(), aliases=None):
    ins = [i if isinstance(i, tuple) else (i, VM) for i in ins]
    outs = [o if isinstance(o, tuple) else (o, VM) for o in outs]
    nbytes = sum(math.prod(a.shape) * a.dtype.itemsize for a, _ in ins + outs)
    return pl.pallas_call(
        body,
        out_shape=[o for o, _ in outs],
        in_specs=[s for _, s in ins],
        out_specs=[s for _, s in outs],
        scratch_shapes=list(scratch),
        input_output_aliases=aliases or {},
        compiler_params=pltpu.CompilerParams(vmem_limit_bytes=GRANT),
        cost_estimate=pl.CostEstimate(flops=flops, bytes_accessed=nbytes, transcendentals=0),
    )(*[i for i, _ in ins])


def far(array):
    return array, HB


def fetch_wait(sems, *pairs):
    for i, (s, d) in enumerate(pairs):
        pltpu.make_async_copy(s, d, sems.at[i]).wait()


def fetch(sems, *pairs):
    copies = [pltpu.make_async_copy(s, d, sems.at[i]) for i, (s, d) in enumerate(pairs)]
    for copy in copies:
        copy.start()
    return copies


class Spot:
    def __init__(self):
        z = lax.axis_index("z")
        self.core = lax.axis_index("core")
        self.top = jnp.logical_and(z == 0, self.core == 0)
        self.bottom = jnp.logical_and(z == 3, self.core == 1)
        self.place = lax.axis_index("x") * 4 + lax.axis_index("y")


ROW_FLOPS = 2 * 9 * FRAMES * WIDTH * CHANS * CHANS


def col_shift(v, by):
    turned = pltpu.roll(v, by % WIDTH, 0)
    at = lax.broadcasted_iota(jnp.int32, v.shape, 0)
    return jnp.where(at == (0 if by == 1 else WIDTH - 1), 0.0, turned)


HALVES = [slice(0, 128), slice(128, 256)]


def conv(rows, weight, flipped):
    height = rows.shape[0] - 2
    lhs = jnp.concatenate([rows[a : a + height] for a in range(3)], axis=-1)
    lhs = lhs.reshape(height * WIDTH, 3 * CHANS)
    parts = []
    for b in range(3):
        if flipped:
            rhs = jnp.concatenate([weight[2 - a, 2 - b] for a in range(3)], axis=1)
            y = lax.dot_general(lhs, rhs, (((1,), (1,)), ((), ())), preferred_element_type=F32)
        else:
            rhs = jnp.concatenate([weight[a, b] for a in range(3)], axis=0)
            y = jnp.dot(lhs, rhs, preferred_element_type=F32)
        parts.append(y.reshape(height, WIDTH, CHANS))

    def block(h, half):
        left, mid, right = (part[h, :, half] for part in parts)
        return mid + col_shift(left, 1) + col_shift(right, -1)

    return block


def blocks(height):
    return [(h, half) for h in range(height) for half in HALVES]


def outer(spot, h, v):
    if h == 0:
        return jnp.where(spot.top, 0.0, v)
    if h == WIDE - 1:
        return jnp.where(spot.bottom, 0.0, v)
    return v


def put_chunks(send, h, half, v):
    for k in range(WIDTH // 16):
        place = h * WIDTH + k * 16
        send[place // PLACES, place % PLACES : place % PLACES + 16, half] = v[
            k * 16 : (k + 1) * 16
        ].astype(BF)


def take_chunks(ref, h, half):
    pieces = []
    for k in range(WIDTH // 16):
        place = h * WIDTH + k * 16
        pieces.append(ref[place // PLACES, place % PLACES : place % PLACES + 16, half])
    return jnp.concatenate(pieces, axis=0).astype(F32)


def transpose_rows(v_ref, out_ref, rows, at_row):
    lane = lax.broadcasted_iota(jnp.int32, (CHANS, WIDTH), 1)
    for t in range(FRAMES):
        for h in range(rows):
            flat = v_ref[t, h].astype(F32).T
            at = pl.ds(at_row(t, h) * WIDTH, WIDTH)
            left = jnp.where(lane == 0, 0.0, pltpu.roll(flat, 1, 1))
            right = jnp.where(lane == WIDTH - 1, 0.0, pltpu.roll(flat, WIDTH - 1, 1))
            out_ref[0:CHANS, at] = left.astype(BF)
            out_ref[CHANS : 2 * CHANS, at] = flat.astype(BF)
            out_ref[2 * CHANS : 3 * CHANS, at] = right.astype(BF)


def ready_body(
    x_far, in_far, steps_far, rates_far, gain_far,
    x, in_weight, table, flat_mid, steps, rates, gain, sems,
):
    copies = fetch(
        sems,
        (x_far, x),
        (steps_far, steps),
        (rates_far, rates),
        (gain_far, gain),
        (in_far, in_weight),
    )
    for copy in copies[:4]:
        copy.wait()
    s0 = jnp.broadcast_to(steps[:, 0:1], (1, CHANS))
    s1 = jnp.broadcast_to(steps[:, 1:2], (1, CHANS))
    r = rates[...]
    lines = [jnp.exp(-r * s0), jnp.exp(-r * s1), s0, s1, r, gain[...], s0 + s1, r]
    for k, line in enumerate(lines):
        table[k : k + 1, :] = line
    transpose_rows(x, flat_mid, HEIGHT, lambda t, h: t * HEIGHT + h)
    copies[4].wait()


def place_halos(spot, from_core, from_chip, above, below):
    @pl.when(spot.core == 0)
    def _():
        above[...] = from_chip[...]
        below[...] = from_core[...]

    @pl.when(spot.core == 1)
    def _():
        above[...] = from_core[...]
        below[...] = from_chip[...]

    @pl.when(spot.top)
    def _():
        above[...] = jnp.zeros_like(above)

    @pl.when(spot.bottom)
    def _():
        below[...] = jnp.zeros_like(below)


def drive_body(
    x, from_core, from_chip, weight, table, local, send, flat_edge, above, below, edges
):
    spot = Spot()
    place_halos(spot, from_core, from_chip, above, below)
    for t in range(FRAMES):
        rows = jnp.concatenate([above[t], x[t], below[t]], axis=0)
        drive = conv(rows, weight, False)
        for h, half in blocks(WIDE):
            v = outer(spot, h, drive(h, half))
            if t == 1:
                v = table[1:2, half] * local[0, h, :, half] + v
                put_chunks(send, h, half, v)
            local[t, h, :, half] = v
    total = jnp.broadcast_to(table[6:7, :][None], (BLOCKS, NOTE, CHANS))
    row = lax.broadcasted_iota(jnp.int32, total.shape, 1)
    one = total.astype(BF).astype(F32)
    two = (total - one).astype(BF).astype(F32)
    three = total - one - two
    send[:, PLACES : PLACES + NOTE, :] = jnp.where(
        row == 0, one, jnp.where(row == 1, two, jnp.where(row == 2, three, 0.0))
    ).astype(BF)
    edges[:, 0:2] = above[...]
    edges[:, 2:4] = below[...]
    transpose_rows(edges, flat_edge, 4, lambda t, h: t * 4 + h)


def forward_scan_body(got, table, send, block_decays):
    carry = jnp.zeros((PLACES, CHANS), F32)
    for k in range(BLOCKS):
        send[k] = carry.astype(BF)
        span = jnp.sum(got[k, PLACES : PLACES + NOTE, :].astype(F32), axis=0, keepdims=True)
        d = jnp.exp(-table[4:5, :] * span)
        block_decays[pl.ds(k, 1), :] = d
        carry = d * carry + got[k, 0:PLACES, :].astype(F32)


def backward_scan_body(got, block_decays, send):
    carry = jnp.zeros((PLACES, CHANS), F32)
    for k in reversed(range(BLOCKS)):
        send[k] = carry.astype(BF)
        carry = block_decays[pl.ds(k, 1), :] * carry + got[k].astype(F32)


GELU_A = math.sqrt(2 / math.pi)


def spread(vector, extra):
    row = lax.broadcasted_iota(jnp.int32, (8, 128), 0) % 4
    low = jnp.broadcast_to(vector[:, 0:128], (8, 128))
    high = jnp.broadcast_to(vector[:, 128:256], (8, 128))
    low, high = (jnp.where(row == 0, v, 0.0) for v in (low, high))
    if extra is not None:
        low = jnp.where(row == 1, extra, low)
    return low, high


def split_pairs(both):
    row = lax.broadcasted_iota(jnp.int32, (8, 128), 0)
    top = both.astype(BF).astype(F32)
    return jnp.where(row < 4, top, both - top)


def joined(pairs):
    return pairs + pltpu.roll(pairs, 4, 0)


def middle_body(
    local, carry, x, cot, weight, table,
    out_far, gz_far, gz, state, state_f, local_adj, send, small, out, sems,
):
    spot = Spot()
    d0, d1 = table[0:1, :], table[1:2, :]
    for h, half in blocks(WIDE):
        c = take_chunks(carry, h, half)
        s0 = local[0, h, :, half] + d0[:, half] * c
        state_f[h, :, half] = s0
        state[0, h, :, half] = s0.astype(BF)
        s1 = local[1, h, :, half] + (d0 * d1)[:, half] * c
        state[1, h, :, half] = s1.astype(BF)
    totals = [jnp.zeros((8, 128), F32) for _ in HALVES]
    copies = []
    for t in (1, 0):
        pre_act = conv(state[t], weight, False)
        for h, half in blocks(HEIGHT):
            xt = x[t, h, :, half].astype(F32)
            z = pre_act(h, half) + table[5:6, half] * xt
            zz = z * z
            th = jnp.tanh(GELU_A * (z + 0.044715 * (zz * z)))
            gate = 0.5 * (1.0 + th)
            out[t, h, :, half] = (z * gate).astype(BF)
            slope = gate + 0.5 * z * (1.0 - th * th) * (GELU_A * (1.0 + 3 * 0.044715 * zz))
            g = cot[t, h, :, half].astype(F32) * slope
            gz[t, h, :, half] = g.astype(BF)
            k = HALVES.index(half)
            totals[k] = totals[k] + jnp.sum((g * xt).reshape(WIDTH // 8, 8, 128), axis=0)
        copies += fetch(sems.at[t], (out.at[t], out_far.at[t]), (gz.at[t], gz_far.at[t]))
        blank = jnp.zeros((2, WIDTH, CHANS), BF)
        grad = conv(jnp.concatenate([blank, gz[t], blank], axis=0), weight, True)
        for h, half in blocks(WIDE):
            v = outer(spot, h, grad(h, half))
            if t == 0:
                v = v + d1[:, half] * local_adj[1, h, :, half]
                put_chunks(send, h, half, d0[:, half] * v)
            local_adj[t, h, :, half] = v
    total = jnp.concatenate([jnp.sum(v, axis=0, keepdims=True) for v in totals], axis=1)
    small[0], small[1] = spread(total, None)
    for copy in copies:
        copy.wait()


def pack_grad(core, g, a, scale, mine, theirs):
    for b in range(3):
        tap = (3 * a + b) * 8
        low = g[b * CHANS : (b + 1) * CHANS, 0:128] * scale
        high = g[b * CHANS : (b + 1) * CHANS, 128:256] * scale
        mine[:, tap : tap + 8, :] = (
            jnp.where(core == 0, low, high).astype(BF).reshape(GROUPS, 8, 128)
        )
        theirs[:, tap : tap + 8, :] = (
            jnp.where(core == 0, high, low).astype(BF).reshape(GROUPS, 8, 128)
        )


def pack_small(core, low, high, scale, mine, theirs):
    blank = jnp.zeros((GROUPS, 8, 128), BF)
    for ref, half in (
        (mine, jnp.where(core == 0, low, high)),
        (theirs, jnp.where(core == 0, high, low)),
    ):
        ref[:, TAPS:PACK, :] = blank
        ref[0, TAPS:PACK, :] = split_pairs(half * scale).astype(BF)


def out_grad_body(scale, state, gz, small, mine, theirs, flat):
    spot = Spot()
    transpose_rows(state, flat, WIDE, lambda t, h: t * WIDE + h)
    rhs = gz[...].reshape(FRAMES * HEIGHT * WIDTH, CHANS)
    for a in range(3):
        lhs = jnp.concatenate(
            [flat[:, pl.ds((t * WIDE + a) * WIDTH, HEIGHT * WIDTH)] for t in range(FRAMES)], axis=1
        )
        g = jnp.dot(lhs, rhs, preferred_element_type=F32)
        pack_grad(spot.core, g, a, scale, mine, theirs)
    pack_small(spot.core, small[0], small[1], scale, mine, theirs)


def in_grad_body(
    scale, step_scale, local, incoming, state_f, carry, table, flat_mid, flat_edge, out_theirs,
    mine, theirs, adj_far, to_core, to_chip, adj, sems,
):
    spot = Spot()
    d0, d1 = table[0:1, :], table[1:2, :]
    sums = [[jnp.zeros((8, 128), F32) for _ in HALVES] for _ in range(FRAMES)]
    for h, half in blocks(WIDE):
        c = take_chunks(incoming, h, half)
        a0 = local[0, h, :, half] + d1[:, half] * c
        a1 = local[1, h, :, half] + c
        adj[0, h, :, half] = a0.astype(BF)
        adj[1, h, :, half] = a1.astype(BF)
        k = HALVES.index(half)
        pairs = ((a0, take_chunks(carry, h, half)), (a1, state_f[h, :, half]))
        for t, (a, earlier) in enumerate(pairs):
            sums[t][k] = sums[t][k] + jnp.sum((a * earlier).reshape(WIDTH // 8, 8, 128), axis=0)
    up, down = adj.at[:, 0:2], adj.at[:, WIDE - 2 :]

    @pl.when(spot.core == 0)
    def _():
        fetch(sems, (up, to_chip), (down, to_core))

    @pl.when(spot.core == 1)
    def _():
        fetch(sems, (down, to_chip), (up, to_core))

    others = fetch(sems.at[2:4], (adj, adj_far), (out_theirs, theirs.at[0]))
    rhs = adj[...].reshape(FRAMES * WIDE * WIDTH, CHANS)
    for a in range(3):
        pieces = []
        for t in range(FRAMES):
            at = t * 4 * WIDTH
            if a < 2:
                pieces.append(flat_edge[:, at + a * WIDTH : at + 2 * WIDTH])
            pieces.append(flat_mid[:, at : at + 4 * WIDTH])
            if a > 0:
                pieces.append(flat_edge[:, at + 2 * WIDTH : at + (2 + a) * WIDTH])
        g = jnp.dot(jnp.concatenate(pieces, axis=1), rhs, preferred_element_type=F32)
        pack_grad(spot.core, g, a, scale, mine, theirs.at[1])
    k0, k1 = (
        jnp.concatenate([jnp.sum(v, axis=0, keepdims=True) for v in pair], axis=1) * d
        for pair, d in zip(sums, (d0, d1))
    )
    rate_part = (k0 * table[2:3, :] + k1 * table[3:4, :]) * (-scale)
    s0 = jnp.sum(k0 * table[4:5, :], axis=1, keepdims=True) * (-step_scale)
    s1 = jnp.sum(k1 * table[4:5, :], axis=1, keepdims=True) * (-step_scale)
    lane = lax.broadcasted_iota(jnp.int32, (8, 128), 1)
    at = spot.place * FRAMES
    low, high = spread(rate_part, jnp.where(lane == at, s0, jnp.where(lane == at + 1, s1, 0.0)))
    pack_small(spot.core, low, high, 1.0, mine, theirs.at[1])
    fetch_wait(sems, (up, to_chip), (down, to_core))
    for copy in others:
        copy.wait()


def grad_inputs_body(
    adj_far, core_far, chip_far, weight_far, gain_far, gz_far,
    out, adj, from_core, from_chip, weight, gain, gz, above, below, sems,
):
    spot = Spot()
    copies = fetch(
        sems,
        (core_far, from_core),
        (chip_far, from_chip),
        (adj_far, adj),
        (weight_far, weight),
        (gain_far, gain),
        (gz_far, gz),
    )
    for copy in copies:
        copy.wait()
    place_halos(spot, from_core, from_chip, above, below)
    for t in range(FRAMES):
        up = (adj[t, 0:2].astype(F32) + above[t].astype(F32)).astype(BF)
        down = (adj[t, WIDE - 2 :].astype(F32) + below[t].astype(F32)).astype(BF)
        rows = jnp.concatenate([up, adj[t, 2 : WIDE - 2], down], axis=0)
        grad = conv(rows, weight, True)
        for h, half in blocks(HEIGHT):
            direct = gain[:, half] * gz[t, h, :, half].astype(F32)
            out[t, h, :, half] = (grad(h, half) + direct).astype(BF)


def pair_sum_body(out_own, in_own, both_got, send):
    for g, own in enumerate((out_own, in_own)):
        got = both_got.at[g]
        for k in range(GROUPS):
            send[g, k] = (own[k].astype(F32) + got[k].astype(F32)).astype(BF)
        pairs = own[0, TAPS:PACK, :].astype(F32) + got[0, TAPS:PACK, :].astype(F32)
        send[g, 0, TAPS:PACK, :] = split_pairs(joined(pairs)).astype(BF)


def all_sum_body(got, send):
    total = jnp.zeros((PACK, 128), F32)
    for k in range(CHIPS):
        total = total + got[k].astype(F32)
    extras = split_pairs(joined(total[TAPS:PACK]))
    total = jnp.concatenate([total[0:TAPS], extras], axis=0).astype(BF)
    send[...] = jnp.broadcast_to(total[None], (CHIPS, PACK, 128))


def write_half(src, lane_half, grads, stage, sems):
    lanes = pl.ds(pl.multiple_of(lane_half * 128, 128), 128)
    copies = []
    for g, grad in enumerate(grads):
        for a in range(3):
            for b in range(3):
                tap = (3 * a + b) * 8
                part = src[g, :, tap : tap + 8, :].astype(F32)
                stage[g, a, b] = part.reshape(CHANS, 128)
            copy = pltpu.make_async_copy(
                stage.at[g, a], grad.at[a, :, :, lanes], sems.at[3 * g + a]
            )
            copy.start()
            copies.append(copy)
    return copies


def unpack_own_body(own, grad_out, grad_in, stage, sems):
    for copy in write_half(own, Spot().core, (grad_out, grad_in), stage, sems):
        copy.wait()


def unpack_other_body(
    own, got, out_half, in_half, grad_out, grad_in, skip, rate, step, stage, sems
):
    del out_half, in_half
    spot = Spot()
    copies = write_half(got, 1 - spot.core, (grad_out, grad_in), stage, sems)

    def smalls(low, high):
        for g, vector in enumerate((skip, rate)):
            for lg, src in enumerate((low, high)):
                extras = joined(src[g, 0, TAPS:PACK, :].astype(F32))
                vector[lg : lg + 1, :] = extras[0:1]
                if g == 1 and lg == 0:
                    turned = pltpu.roll(extras, (128 - spot.place * FRAMES) % 128, 1)
                    step[...] = turned[1:2, 0:FRAMES]

    @pl.when(spot.core == 0)
    def _():
        smalls(own, got)

    @pl.when(spot.core == 1)
    def _():
        smalls(got, own)

    for copy in copies:
        copy.wait()


ROWS_AXES = ("z", "core")
TM_AXES = ("x", "y")
CORE_PAIRS = [(i, i ^ 1) for i in range(8)]
CHIP_PAIRS = [(i, (i + 1) % 8 if i % 2 else (i - 1) % 8) for i in range(8)]


def halos(to_core, to_chip):
    from_chip = lax.ppermute(to_chip, ROWS_AXES, CHIP_PAIRS)
    from_core = lax.ppermute(to_core, ROWS_AXES, CORE_PAIRS)
    return from_core, from_chip


def swap(chunks, axes):
    return lax.all_to_all(chunks, axes, 0, 0)


def vmem(shape, dtype=BF):
    return pltpu.VMEM(shape, dtype)


def sems(*shape):
    return pltpu.SemaphoreType.DMA(shape)


def on_device(inputs, in_weight, out_weight, skip_gain, rates, step_sizes, cotangent):
    scale = 1.0 / math.sqrt(32 * 32 * 128)
    step_scale = 1.0 / math.sqrt(1048576)
    core = lax.axis_index("core")
    field = (FRAMES, HEIGHT, WIDTH, CHANS)
    wide = (FRAMES, WIDE, WIDTH, CHANS)
    edge = (FRAMES, 2, WIDTH, CHANS)
    kernel = (3, 3, CHANS, CHANS)
    chunk = sds((BLOCKS, PLACES, CHANS), BF)
    packed = sds((GROUPS, PACK, 128), BF)
    flat = sds((3 * CHANS, FRAMES * 4 * WIDTH), BF)
    gain = skip_gain[None, :]

    to_core = lax.dynamic_slice(inputs, (0, 2 - 2 * core, 0, 0), edge)
    to_chip = lax.dynamic_slice(inputs, (0, 2 * core, 0, 0), edge)
    from_core, from_chip = halos(to_core, to_chip)
    x, in_w, table, flat_mid = call(
        ready_body,
        [sds(field, BF), sds(kernel, BF), sds((8, CHANS), F32), flat],
        [far(a) for a in (inputs, in_weight, step_sizes[None, :], rates[None, :], gain)],
        2 * ROW_FLOPS,
        [vmem((1, FRAMES), F32), vmem((1, CHANS), F32), vmem((1, CHANS), F32), sems(5)],
    )
    local, send, flat_edge = call(
        drive_body,
        [sds(wide, F32), sds((BLOCKS, PLACES + NOTE, CHANS), BF), flat],
        [x, from_core, from_chip, in_w, table],
        WIDE * ROW_FLOPS,
        [vmem(edge), vmem(edge), vmem(field)],
    )
    got = swap(send, TM_AXES)
    send, block_decays = call(forward_scan_body, [chunk, sds((BLOCKS, CHANS), F32)], [got, table])
    carry = swap(send, TM_AXES)
    outputs, gz_far, gz, state, state_f, local_adj, send, small = call(
        middle_body,
        [
            far(sds(field, BF)),
            far(sds(field, BF)),
            sds(field, BF),
            sds(wide, BF),
            sds(wide[1:], F32),
            sds(wide, F32),
            chunk,
            sds((2, 8, 128), F32),
        ],
        [local, carry, x, cotangent, out_weight, table],
        (HEIGHT + WIDE) * ROW_FLOPS,
        [vmem(field), sems(FRAMES, 2)],
    )
    out_mine, out_theirs = call(
        functools.partial(out_grad_body, scale),
        [packed, packed],
        [state, gz, small],
        HEIGHT * ROW_FLOPS,
        [vmem((3 * CHANS, FRAMES * WIDE * WIDTH))],
    )
    send, out_mine, out_theirs = lax.optimization_barrier((send, out_mine, out_theirs))
    got = swap(send, TM_AXES)
    (send,) = call(backward_scan_body, [chunk], [got, block_decays])
    incoming = swap(send, TM_AXES)
    in_mine, theirs, adj_far, to_core, to_chip = call(
        functools.partial(in_grad_body, scale, step_scale),
        [
            packed,
            sds((2, GROUPS, PACK, 128), BF),
            far(sds(wide, BF)),
            far(sds(edge, BF)),
            far(sds(edge, BF)),
        ],
        [local_adj, incoming, state_f, carry, table, flat_mid, flat_edge, out_theirs],
        WIDE * ROW_FLOPS,
        [vmem(wide), sems(4)],
    )
    both_got = lax.ppermute(theirs, ROWS_AXES, CORE_PAIRS)
    from_core, from_chip = halos(to_core, to_chip)
    (send,) = call(
        pair_sum_body, [sds((2, GROUPS, PACK, 128), BF)], [out_mine, in_mine, both_got]
    )
    got = swap(send.reshape(CHIPS, PACK, 128), ("x", "y", "z"))
    (send,) = call(all_sum_body, [sds((CHIPS, PACK, 128), BF)], [got])
    send, from_core, from_chip = lax.optimization_barrier((send, from_core, from_chip))
    own = swap(send, ("x", "y", "z"))
    (grad_inputs,) = call(
        grad_inputs_body,
        [sds(field, BF)],
        [far(a) for a in (adj_far, from_core, from_chip, in_weight, gain, gz_far)],
        HEIGHT * ROW_FLOPS,
        [
            vmem(wide),
            vmem(edge),
            vmem(edge),
            vmem(kernel),
            vmem((1, CHANS), F32),
            vmem(field),
            vmem(edge),
            vmem(edge),
            sems(6),
        ],
    )
    own, grad_inputs = lax.optimization_barrier((own, grad_inputs))
    own = own.reshape(2, GROUPS, PACK, 128)
    other = lax.ppermute(own, ROWS_AXES, CORE_PAIRS)
    weights = sds(kernel, F32)
    half = sds((2, 128), F32)
    stage = vmem((2, 3, 3, CHANS, 128), F32)
    grad_out_weight, grad_in_weight = call(
        unpack_own_body, [far(weights), far(weights)], [own], 0, [stage, sems(6)]
    )
    grad_out_weight, grad_in_weight, grad_skip, grad_rates, grad_steps = call(
        unpack_other_body,
        [far(weights), far(weights), half, half, sds((1, FRAMES), F32)],
        [own, other, far(grad_out_weight), far(grad_in_weight)],
        0,
        [stage, sems(6)],
        {2: 0, 3: 1},
    )
    return (
        outputs,
        grad_inputs,
        grad_in_weight,
        grad_out_weight,
        grad_skip.reshape(CHANS),
        grad_rates.reshape(CHANS),
        grad_steps.reshape(FRAMES),
    )


def solution(mesh):
    fine = Mesh(mesh.devices.reshape(4, 4, 4, 2), ("x", "y", "z", "core"))
    spread_out = P(TM_AXES, ROWS_AXES, None, None)
    placed = (spread_out, P(), P(), P(), P(), P(TM_AXES), spread_out)
    return jax.shard_map(
        on_device,
        mesh=fine,
        in_specs=placed,
        out_specs=(spread_out, spread_out, P(), P(), P(), P(), P(TM_AXES)),
        check_vma=False,
    )
```

```python
import functools
import math

import jax
import jax.numpy as jnp
from jax import lax
from jax.experimental import pallas as pl
from jax.experimental.pallas import tpu as pltpu
from jax.sharding import Mesh, PartitionSpec as P

BF, F32 = jnp.bfloat16, jnp.float32
VM = pl.BlockSpec(memory_space=pltpu.VMEM)
HB = pl.BlockSpec(memory_space=pltpu.HBM)
GRANT = 24 << 20
FRAMES, HEIGHT, WIDTH, CHANS = 2, 4, 128, 256
WIDE, WIDER = HEIGHT + 2, HEIGHT + 4
BLOCKS = 16
PLACES = WIDE * WIDTH // BLOCKS
NOTE = 8
CHIPS = 64
GROUPS = 32
TAPS = 72
PACK = TAPS + 8


def sds(shape, dtype):
    return jax.ShapeDtypeStruct(shape, dtype)


def call(body, outs, ins, flops=0, scratch=(), aliases=None):
    ins = [i if isinstance(i, tuple) else (i, VM) for i in ins]
    outs = [o if isinstance(o, tuple) else (o, VM) for o in outs]
    nbytes = sum(math.prod(a.shape) * a.dtype.itemsize for a, _ in ins + outs)
    return pl.pallas_call(
        body,
        out_shape=[o for o, _ in outs],
        in_specs=[s for _, s in ins],
        out_specs=[s for _, s in outs],
        scratch_shapes=list(scratch),
        input_output_aliases=aliases or {},
        compiler_params=pltpu.CompilerParams(vmem_limit_bytes=GRANT),
        cost_estimate=pl.CostEstimate(flops=flops, bytes_accessed=nbytes, transcendentals=0),
    )(*[i for i, _ in ins])


def far(array):
    return array, HB


def fetch_wait(sems, *pairs):
    for i, (s, d) in enumerate(pairs):
        pltpu.make_async_copy(s, d, sems.at[i]).wait()


def fetch(sems, *pairs):
    copies = [pltpu.make_async_copy(s, d, sems.at[i]) for i, (s, d) in enumerate(pairs)]
    for copy in copies:
        copy.start()
    return copies


class Spot:
    def __init__(self):
        z = lax.axis_index("z")
        self.core = lax.axis_index("core")
        self.top = jnp.logical_and(z == 0, self.core == 0)
        self.bottom = jnp.logical_and(z == 3, self.core == 1)
        self.place = lax.axis_index("x") * 4 + lax.axis_index("y")


ROW_FLOPS = 2 * 9 * FRAMES * WIDTH * CHANS * CHANS


def col_shift(v, by):
    turned = pltpu.roll(v, by % WIDTH, 0)
    at = lax.broadcasted_iota(jnp.int32, v.shape, 0)
    return jnp.where(at == (0 if by == 1 else WIDTH - 1), 0.0, turned)


HALVES = [slice(0, 128), slice(128, 256)]


def conv(rows, weight, flipped):
    height = rows.shape[0] - 2
    lhs = jnp.concatenate([rows[a : a + height] for a in range(3)], axis=-1)
    lhs = lhs.reshape(height * WIDTH, 3 * CHANS)
    parts = []
    for b in range(3):
        if flipped:
            rhs = jnp.concatenate([weight[2 - a, 2 - b] for a in range(3)], axis=1)
            y = lax.dot_general(lhs, rhs, (((1,), (1,)), ((), ())), preferred_element_type=F32)
        else:
            rhs = jnp.concatenate([weight[a, b] for a in range(3)], axis=0)
            y = jnp.dot(lhs, rhs, preferred_element_type=F32)
        parts.append(y.reshape(height, WIDTH, CHANS))

    def block(h, half):
        left, mid, right = (part[h, :, half] for part in parts)
        return mid + col_shift(left, 1) + col_shift(right, -1)

    return block


def spread_conv(field, weight):
    pieces = []
    for first, count, taps in ((0, 1, (2,)), (1, 1, (1, 2)), (2, 2, (0, 1, 2)), (4, 1, (0, 1)), (5, 1, (0,))):
        lhs = jnp.concatenate(
            [field[:, first + a - 2 : first + a - 2 + count] for a in taps], axis=-1
        ).reshape(FRAMES * count * WIDTH, len(taps) * CHANS)
        parts = []
        for b in range(3):
            rhs = jnp.concatenate([weight[2 - a, 2 - b] for a in taps], axis=1)
            y = lax.dot_general(lhs, rhs, (((1,), (1,)), ((), ())), preferred_element_type=F32)
            parts.append(y.reshape(FRAMES, count, WIDTH, CHANS))
        pieces += [(parts, k) for k in range(count)]

    def block(t, h, half):
        parts, k = pieces[h]
        left, mid, right = (part[t, k, :, half] for part in parts)
        return mid + col_shift(left, 1) + col_shift(right, -1)

    return block


def blocks(height):
    return [(h, half) for h in range(height) for half in HALVES]


def outer(spot, h, v):
    if h == 0:
        return jnp.where(spot.top, 0.0, v)
    if h == WIDE - 1:
        return jnp.where(spot.bottom, 0.0, v)
    return v


def put_chunks(send, h, half, v):
    for k in range(WIDTH // 16):
        place = h * WIDTH + k * 16
        send[place // PLACES, place % PLACES : place % PLACES + 16, half] = v[
            k * 16 : (k + 1) * 16
        ].astype(BF)


def take_chunks(ref, h, half):
    pieces = []
    for k in range(WIDTH // 16):
        place = h * WIDTH + k * 16
        pieces.append(ref[place // PLACES, place % PLACES : place % PLACES + 16, half])
    return jnp.concatenate(pieces, axis=0).astype(F32)


def transpose_rows(v_ref, out_ref, rows, at_row):
    lane = lax.broadcasted_iota(jnp.int32, (CHANS, WIDTH), 1)
    for t in range(FRAMES):
        for h in range(rows):
            flat = v_ref[t, h].astype(F32).T
            at = pl.ds(at_row(t, h) * WIDTH, WIDTH)
            left = jnp.where(lane == 0, 0.0, pltpu.roll(flat, 1, 1))
            right = jnp.where(lane == WIDTH - 1, 0.0, pltpu.roll(flat, WIDTH - 1, 1))
            out_ref[0:CHANS, at] = left.astype(BF)
            out_ref[CHANS : 2 * CHANS, at] = flat.astype(BF)
            out_ref[2 * CHANS : 3 * CHANS, at] = right.astype(BF)


def ready_body(x_far, in_far, params, x, in_weight, table, flat_mid, sems):
    copies = fetch(sems, (x_far, x), (in_far, in_weight))
    r = params[0:1, :]
    s0 = jnp.broadcast_to(params[2:3, 0:1], (1, CHANS))
    s1 = jnp.broadcast_to(params[2:3, 1:2], (1, CHANS))
    lines = [jnp.exp(-r * s0), jnp.exp(-r * s1), s0, s1, r, params[1:2, :], s0 + s1, r]
    for k, line in enumerate(lines):
        table[k : k + 1, :] = line
    copies[0].wait()
    transpose_rows(x, flat_mid, HEIGHT, lambda t, h: t * HEIGHT + h)
    copies[1].wait()


def place_halos(spot, from_core, from_chip, above, below):
    @pl.when(spot.core == 0)
    def _():
        above[...] = from_chip[...]
        below[...] = from_core[...]

    @pl.when(spot.core == 1)
    def _():
        above[...] = from_core[...]
        below[...] = from_chip[...]

    @pl.when(spot.top)
    def _():
        above[...] = jnp.zeros_like(above)

    @pl.when(spot.bottom)
    def _():
        below[...] = jnp.zeros_like(below)


def drive_body(
    x, from_core, from_chip, weight, table, local, send, flat_edge, above, below, edges
):
    spot = Spot()
    place_halos(spot, from_core, from_chip, above, below)
    for t in range(FRAMES):
        rows = jnp.concatenate([above[t], x[t], below[t]], axis=0)
        drive = conv(rows, weight, False)
        for h, half in blocks(WIDE):
            v = outer(spot, h, drive(h, half))
            if t == 1:
                v = table[1:2, half] * local[0, h, :, half] + v
                put_chunks(send, h, half, v)
            local[t, h, :, half] = v
    total = jnp.broadcast_to(table[6:7, :][None], (BLOCKS, NOTE, CHANS))
    row = lax.broadcasted_iota(jnp.int32, total.shape, 1)
    one = total.astype(BF).astype(F32)
    two = (total - one).astype(BF).astype(F32)
    three = total - one - two
    send[:, PLACES : PLACES + NOTE, :] = jnp.where(
        row == 0, one, jnp.where(row == 1, two, jnp.where(row == 2, three, 0.0))
    ).astype(BF)
    edges[:, 0:2] = above[...]
    edges[:, 2:4] = below[...]
    transpose_rows(edges, flat_edge, 4, lambda t, h: t * 4 + h)


def forward_scan_body(got, table, send, block_decays):
    carry = jnp.zeros((PLACES, CHANS), F32)
    for k in range(BLOCKS):
        send[k] = carry.astype(BF)
        span = jnp.sum(got[k, PLACES : PLACES + NOTE, :].astype(F32), axis=0, keepdims=True)
        d = jnp.exp(-table[4:5, :] * span)
        block_decays[pl.ds(k, 1), :] = d
        carry = d * carry + got[k, 0:PLACES, :].astype(F32)


def backward_scan_body(got, block_decays, send):
    carry = jnp.zeros((PLACES, CHANS), F32)
    for k in reversed(range(BLOCKS)):
        send[k] = carry.astype(BF)
        carry = block_decays[pl.ds(k, 1), :] * carry + got[k].astype(F32)


GELU_A = math.sqrt(2 / math.pi)


def spread(vector, extra):
    row = lax.broadcasted_iota(jnp.int32, (8, 128), 0) % 4
    low = jnp.broadcast_to(vector[:, 0:128], (8, 128))
    high = jnp.broadcast_to(vector[:, 128:256], (8, 128))
    low, high = (jnp.where(row == 0, v, 0.0) for v in (low, high))
    if extra is not None:
        low = jnp.where(row == 1, extra, low)
    return low, high


def split_pairs(both):
    row = lax.broadcasted_iota(jnp.int32, (8, 128), 0)
    top = both.astype(BF).astype(F32)
    return jnp.where(row < 4, top, both - top)


def joined(pairs):
    return pairs + pltpu.roll(pairs, 4, 0)


def middle_body(
    local, carry, x, cot, weight, table,
    out_far, direct_far, gz, state, state_f, local_adj, send, small, out, direct, sems,
):
    spot = Spot()
    d0, d1 = table[0:1, :], table[1:2, :]
    for h, half in blocks(WIDE):
        c = take_chunks(carry, h, half)
        s0 = local[0, h, :, half] + d0[:, half] * c
        state_f[h, :, half] = s0
        state[0, h, :, half] = s0.astype(BF)
        s1 = local[1, h, :, half] + (d0 * d1)[:, half] * c
        state[1, h, :, half] = s1.astype(BF)
    totals = [jnp.zeros((8, 128), F32) for _ in HALVES]
    copies = []
    for t in (1, 0):
        pre_act = conv(state[t], weight, False)
        for h, half in blocks(HEIGHT):
            xt = x[t, h, :, half].astype(F32)
            z = pre_act(h, half) + table[5:6, half] * xt
            zz = z * z
            th = jnp.tanh(GELU_A * (z + 0.044715 * (zz * z)))
            gate = 0.5 * (1.0 + th)
            out[t, h, :, half] = (z * gate).astype(BF)
            slope = gate + 0.5 * z * (1.0 - th * th) * (GELU_A * (1.0 + 3 * 0.044715 * zz))
            g = cot[t, h, :, half].astype(F32) * slope
            gz[t, h, :, half] = g.astype(BF)
            direct[t, h, :, half] = (table[5:6, half] * g).astype(BF)
            k = HALVES.index(half)
            totals[k] = totals[k] + jnp.sum((g * xt).reshape(WIDTH // 8, 8, 128), axis=0)
        copies += fetch(sems.at[t], (out.at[t], out_far.at[t]), (direct.at[t], direct_far.at[t]))
    grad = spread_conv(gz, weight)
    for t in (1, 0):
        for h, half in blocks(WIDE):
            v = outer(spot, h, grad(t, h, half))
            if t == 0:
                v = v + d1[:, half] * local_adj[1, h, :, half]
                put_chunks(send, h, half, d0[:, half] * v)
            local_adj[t, h, :, half] = v
    total = jnp.concatenate([jnp.sum(v, axis=0, keepdims=True) for v in totals], axis=1)
    small[0], small[1] = spread(total, None)
    for copy in copies:
        copy.wait()


def pack_grad(core, g, a, scale, mine, theirs):
    for b in range(3):
        tap = (3 * a + b) * 8
        low = g[b * CHANS : (b + 1) * CHANS, 0:128] * scale
        high = g[b * CHANS : (b + 1) * CHANS, 128:256] * scale
        mine[:, tap : tap + 8, :] = (
            jnp.where(core == 0, low, high).astype(BF).reshape(GROUPS, 8, 128)
        )
        theirs[:, tap : tap + 8, :] = (
            jnp.where(core == 0, high, low).astype(BF).reshape(GROUPS, 8, 128)
        )


def pack_small(core, low, high, scale, mine, theirs):
    blank = jnp.zeros((GROUPS, 8, 128), BF)
    for ref, half in (
        (mine, jnp.where(core == 0, low, high)),
        (theirs, jnp.where(core == 0, high, low)),
    ):
        ref[:, TAPS:PACK, :] = blank
        ref[0, TAPS:PACK, :] = split_pairs(half * scale).astype(BF)


def out_grad_body(scale, state, gz, small, mine, theirs, flat):
    spot = Spot()
    transpose_rows(state, flat, WIDE, lambda t, h: t * WIDE + h)
    rhs = gz[...].reshape(FRAMES * HEIGHT * WIDTH, CHANS)
    for a in range(3):
        lhs = jnp.concatenate(
            [flat[:, pl.ds((t * WIDE + a) * WIDTH, HEIGHT * WIDTH)] for t in range(FRAMES)], axis=1
        )
        g = jnp.dot(lhs, rhs, preferred_element_type=F32)
        pack_grad(spot.core, g, a, scale, mine, theirs)
    pack_small(spot.core, small[0], small[1], scale, mine, theirs)


def in_grad_body(
    scale, step_scale, local, incoming, state_f, carry, table, flat_mid, flat_edge, out_theirs,
    mine, theirs, adj_far, to_core, to_chip, adj, sems,
):
    spot = Spot()
    d0, d1 = table[0:1, :], table[1:2, :]
    sums = [[jnp.zeros((8, 128), F32) for _ in HALVES] for _ in range(FRAMES)]
    for h, half in blocks(WIDE):
        c = take_chunks(incoming, h, half)
        a0 = local[0, h, :, half] + d1[:, half] * c
        a1 = local[1, h, :, half] + c
        adj[0, h, :, half] = a0.astype(BF)
        adj[1, h, :, half] = a1.astype(BF)
        k = HALVES.index(half)
        pairs = ((a0, take_chunks(carry, h, half)), (a1, state_f[h, :, half]))
        for t, (a, earlier) in enumerate(pairs):
            sums[t][k] = sums[t][k] + jnp.sum((a * earlier).reshape(WIDTH // 8, 8, 128), axis=0)
    up, down = adj.at[:, 0:2], adj.at[:, WIDE - 2 :]

    @pl.when(spot.core == 0)
    def _():
        fetch(sems, (up, to_chip), (down, to_core))

    @pl.when(spot.core == 1)
    def _():
        fetch(sems, (down, to_chip), (up, to_core))

    others = fetch(sems.at[2:4], (adj, adj_far), (out_theirs, theirs.at[0]))
    rhs = adj[...].reshape(FRAMES * WIDE * WIDTH, CHANS)
    for a in range(3):
        pieces = []
        for t in range(FRAMES):
            at = t * 4 * WIDTH
            if a < 2:
                pieces.append(flat_edge[:, at + a * WIDTH : at + 2 * WIDTH])
            pieces.append(flat_mid[:, at : at + 4 * WIDTH])
            if a > 0:
                pieces.append(flat_edge[:, at + 2 * WIDTH : at + (2 + a) * WIDTH])
        g = jnp.dot(jnp.concatenate(pieces, axis=1), rhs, preferred_element_type=F32)
        pack_grad(spot.core, g, a, scale, mine, theirs.at[1])
    k0, k1 = (
        jnp.concatenate([jnp.sum(v, axis=0, keepdims=True) for v in pair], axis=1) * d
        for pair, d in zip(sums, (d0, d1))
    )
    rate_part = (k0 * table[2:3, :] + k1 * table[3:4, :]) * (-scale)
    s0 = jnp.sum(k0 * table[4:5, :], axis=1, keepdims=True) * (-step_scale)
    s1 = jnp.sum(k1 * table[4:5, :], axis=1, keepdims=True) * (-step_scale)
    lane = lax.broadcasted_iota(jnp.int32, (8, 128), 1)
    at = spot.place * FRAMES
    low, high = spread(rate_part, jnp.where(lane == at, s0, jnp.where(lane == at + 1, s1, 0.0)))
    pack_small(spot.core, low, high, 1.0, mine, theirs.at[1])
    fetch_wait(sems, (up, to_chip), (down, to_core))
    for copy in others:
        copy.wait()


def grad_inputs_body(
    adj_far, core_far, chip_far, weight_far, direct_far,
    out_far, adj, from_core, from_chip, weight, direct, out, above, below, sems,
):
    spot = Spot()
    copies = fetch(
        sems,
        (core_far, from_core),
        (chip_far, from_chip),
        (adj_far, adj),
        (weight_far, weight),
        (direct_far, direct),
    )
    for copy in copies:
        copy.wait()
    place_halos(spot, from_core, from_chip, above, below)
    for t in range(FRAMES):
        up = (adj[t, 0:2].astype(F32) + above[t].astype(F32)).astype(BF)
        down = (adj[t, WIDE - 2 :].astype(F32) + below[t].astype(F32)).astype(BF)
        rows = jnp.concatenate([up, adj[t, 2 : WIDE - 2], down], axis=0)
        grad = conv(rows, weight, True)
        for h, half in blocks(HEIGHT):
            own = direct[t, h, :, half].astype(F32)
            out[t, h, :, half] = (grad(h, half) + own).astype(BF)
    (copy,) = fetch(sems, (out, out_far))
    copy.wait()


def pair_sum_body(out_own, in_own, both_got, send_far, send, sems):
    copies = []
    for g, own in enumerate((out_own, in_own)):
        got = both_got.at[g]
        for k in range(GROUPS):
            send[g, k] = (own[k].astype(F32) + got[k].astype(F32)).astype(BF)
            if k == 0:
                pairs = own[0, TAPS:PACK, :].astype(F32) + got[0, TAPS:PACK, :].astype(F32)
                send[g, 0, TAPS:PACK, :] = split_pairs(joined(pairs)).astype(BF)
            if k % 8 == 7:
                part = slice(k - 7, k + 1)
                copies += fetch(
                    sems.at[g, k // 8 : k // 8 + 1], (send.at[g, part], send_far.at[g, part])
                )
    for copy in copies:
        copy.wait()


def all_sum_body(got, send_far, send, sems):
    total = jnp.zeros((PACK, 128), F32)
    for k in range(CHIPS):
        total = total + got[k].astype(F32)
    extras = split_pairs(joined(total[TAPS:PACK]))
    total = jnp.concatenate([total[0:TAPS], extras], axis=0).astype(BF)
    send[...] = jnp.broadcast_to(total[None], send.shape)
    pairs = [(send, send_far.at[8 * k : 8 * k + 8]) for k in range(8)]
    for copy in fetch(sems, *pairs):
        copy.wait()


def write_half(src, lane_half, grads, stage, sems):
    lanes = pl.ds(pl.multiple_of(lane_half * 128, 128), 128)
    copies = []
    for g, grad in enumerate(grads):
        for a in range(3):
            for b in range(3):
                tap = (3 * a + b) * 8
                part = src[g, :, tap : tap + 8, :].astype(F32)
                stage[g, a, b] = part.reshape(CHANS, 128)
            copy = pltpu.make_async_copy(
                stage.at[g, a], grad.at[a, :, :, lanes], sems.at[3 * g + a]
            )
            copy.start()
            copies.append(copy)
    return copies


def unpack_own_body(own, grad_out, grad_in, stage, sems):
    for copy in write_half(own, Spot().core, (grad_out, grad_in), stage, sems):
        copy.wait()


def unpack_other_body(
    own, got, out_half, in_half, grad_out, grad_in, skip, rate, step, stage, sems
):
    del out_half, in_half
    spot = Spot()
    copies = write_half(got, 1 - spot.core, (grad_out, grad_in), stage, sems)

    def smalls(low, high):
        for g, vector in enumerate((skip, rate)):
            for lg, src in enumerate((low, high)):
                extras = joined(src[g, 0, TAPS:PACK, :].astype(F32))
                vector[lg : lg + 1, :] = extras[0:1]
                if g == 1 and lg == 0:
                    turned = pltpu.roll(extras, (128 - spot.place * FRAMES) % 128, 1)
                    step[...] = turned[1:2, 0:FRAMES]

    @pl.when(spot.core == 0)
    def _():
        smalls(own, got)

    @pl.when(spot.core == 1)
    def _():
        smalls(got, own)

    for copy in copies:
        copy.wait()


ROWS_AXES = ("z", "core")
TM_AXES = ("x", "y")
CORE_PAIRS = [(i, i ^ 1) for i in range(8)]
CHIP_PAIRS = [(i, (i + 1) % 8 if i % 2 else (i - 1) % 8) for i in range(8)]


def halos(to_core, to_chip):
    from_chip = lax.ppermute(to_chip, ROWS_AXES, CHIP_PAIRS)
    from_core = lax.ppermute(to_core, ROWS_AXES, CORE_PAIRS)
    return from_core, from_chip


def swap(chunks, axes):
    return lax.all_to_all(chunks, axes, 0, 0)


def vmem(shape, dtype=BF):
    return pltpu.VMEM(shape, dtype)


def sems(*shape):
    return pltpu.SemaphoreType.DMA(shape)


def on_device(inputs, in_weight, out_weight, skip_gain, rates, step_sizes, cotangent):
    scale = 1.0 / math.sqrt(32 * 32 * 128)
    step_scale = 1.0 / math.sqrt(1048576)
    core = lax.axis_index("core")
    field = (FRAMES, HEIGHT, WIDTH, CHANS)
    wide = (FRAMES, WIDE, WIDTH, CHANS)
    edge = (FRAMES, 2, WIDTH, CHANS)
    kernel = (3, 3, CHANS, CHANS)
    chunk = sds((BLOCKS, PLACES, CHANS), BF)
    packed = sds((GROUPS, PACK, 128), BF)
    flat = sds((3 * CHANS, FRAMES * 4 * WIDTH), BF)
    params = jnp.concatenate([rates, skip_gain, jnp.pad(step_sizes, (0, CHANS - FRAMES))])
    params = params.reshape(3, CHANS)

    to_core = lax.dynamic_slice(inputs, (0, 2 - 2 * core, 0, 0), edge)
    to_chip = lax.dynamic_slice(inputs, (0, 2 * core, 0, 0), edge)
    from_core, from_chip = halos(to_core, to_chip)
    x, in_w, table, flat_mid = call(
        ready_body,
        [sds(field, BF), sds(kernel, BF), sds((8, CHANS), F32), flat],
        [far(inputs), far(in_weight), params],
        2 * ROW_FLOPS,
        [sems(2)],
    )
    local, send, flat_edge = call(
        drive_body,
        [sds(wide, F32), sds((BLOCKS, PLACES + NOTE, CHANS), BF), flat],
        [x, from_core, from_chip, in_w, table],
        WIDE * ROW_FLOPS,
        [vmem(edge), vmem(edge), vmem(field)],
    )
    got = swap(send, TM_AXES)
    send, block_decays = call(forward_scan_body, [chunk, sds((BLOCKS, CHANS), F32)], [got, table])
    carry = swap(send, TM_AXES)
    outputs, direct, gz, state, state_f, local_adj, send, small = call(
        middle_body,
        [
            far(sds(field, BF)),
            far(sds(field, BF)),
            sds(field, BF),
            sds(wide, BF),
            sds(wide[1:], F32),
            sds(wide, F32),
            chunk,
            sds((2, 8, 128), F32),
        ],
        [local, carry, x, cotangent, out_weight, table],
        (HEIGHT + WIDE) * ROW_FLOPS,
        [vmem(field), vmem(field), sems(FRAMES, 2)],
    )
    out_mine, out_theirs = call(
        functools.partial(out_grad_body, scale),
        [packed, packed],
        [state, gz, small],
        HEIGHT * ROW_FLOPS,
        [vmem((3 * CHANS, FRAMES * WIDE * WIDTH))],
    )
    send, out_mine, out_theirs = lax.optimization_barrier((send, out_mine, out_theirs))
    got = swap(send, TM_AXES)
    (send,) = call(backward_scan_body, [chunk], [got, block_decays])
    incoming = swap(send, TM_AXES)
    in_mine, theirs, adj_far, to_core, to_chip = call(
        functools.partial(in_grad_body, scale, step_scale),
        [
            packed,
            sds((2, GROUPS, PACK, 128), BF),
            far(sds(wide, BF)),
            far(sds(edge, BF)),
            far(sds(edge, BF)),
        ],
        [local_adj, incoming, state_f, carry, table, flat_mid, flat_edge, out_theirs],
        WIDE * ROW_FLOPS,
        [vmem(wide), sems(4)],
    )
    both_got = lax.ppermute(theirs, ROWS_AXES, CORE_PAIRS)
    from_core, from_chip = halos(to_core, to_chip)
    (send,) = call(
        pair_sum_body,
        [far(sds((2, GROUPS, PACK, 128), BF))],
        [out_mine, in_mine, both_got],
        0,
        [vmem((2, GROUPS, PACK, 128)), sems(2, 4)],
    )
    got = swap(send.reshape(CHIPS, PACK, 128), ("x", "y", "z"))
    (send,) = call(
        all_sum_body,
        [far(sds((CHIPS, PACK, 128), BF))],
        [got],
        0,
        [vmem((8, PACK, 128)), sems(8)],
    )
    send, from_core, from_chip = lax.optimization_barrier((send, from_core, from_chip))
    own = swap(send, ("x", "y", "z"))
    (grad_inputs,) = call(
        grad_inputs_body,
        [far(sds(field, BF))],
        [far(a) for a in (adj_far, from_core, from_chip, in_weight, direct)],
        HEIGHT * ROW_FLOPS,
        [
            vmem(wide),
            vmem(edge),
            vmem(edge),
            vmem(kernel),
            vmem(field),
            vmem(field),
            vmem(edge),
            vmem(edge),
            sems(5),
        ],
        {4: 0},
    )
    own, grad_inputs = lax.optimization_barrier((own, grad_inputs))
    own = own.reshape(2, GROUPS, PACK, 128)
    other = lax.ppermute(own, ROWS_AXES, CORE_PAIRS)
    weights = sds(kernel, F32)
    half = sds((2, 128), F32)
    stage = vmem((2, 3, 3, CHANS, 128), F32)
    grad_out_weight, grad_in_weight = call(
        unpack_own_body, [far(weights), far(weights)], [own], 0, [stage, sems(6)]
    )
    grad_out_weight, grad_in_weight, grad_skip, grad_rates, grad_steps = call(
        unpack_other_body,
        [far(weights), far(weights), half, half, sds((1, FRAMES), F32)],
        [own, other, far(grad_out_weight), far(grad_in_weight)],
        0,
        [stage, sems(6)],
        {2: 0, 3: 1},
    )
    return (
        outputs,
        grad_inputs,
        grad_in_weight,
        grad_out_weight,
        grad_skip.reshape(CHANS),
        grad_rates.reshape(CHANS),
        grad_steps.reshape(FRAMES),
    )


def solution(mesh):
    fine = Mesh(mesh.devices.reshape(4, 4, 4, 2), ("x", "y", "z", "core"))
    spread_out = P(TM_AXES, ROWS_AXES, None, None)
    placed = (spread_out, P(), P(), P(), P(), P(TM_AXES), spread_out)
    return jax.shard_map(
        on_device,
        mesh=fine,
        in_specs=placed,
        out_specs=(spread_out, spread_out, P(), P(), P(), P(), P(TM_AXES)),
        check_vma=False,
    )
```

```python
import functools
import math

import jax
import jax.numpy as jnp
from jax import lax
from jax.experimental import pallas as pl
from jax.experimental.pallas import tpu as pltpu
from jax.sharding import Mesh, PartitionSpec as P

BF, F32 = jnp.bfloat16, jnp.float32
VM = pl.BlockSpec(memory_space=pltpu.VMEM)
HB = pl.BlockSpec(memory_space=pltpu.HBM)
GRANT = 24 << 20
FRAMES, HEIGHT, WIDTH, CHANS = 2, 4, 128, 256
WIDE, WIDER = HEIGHT + 2, HEIGHT + 4
BLOCKS = 16
PLACES = WIDE * WIDTH // BLOCKS
NOTE = 8
CHIPS = 64
GROUPS = 32
TAPS = 72
PACK = TAPS + 8


def sds(shape, dtype):
    return jax.ShapeDtypeStruct(shape, dtype)


def call(body, outs, ins, flops=0, scratch=(), aliases=None):
    ins = [i if isinstance(i, tuple) else (i, VM) for i in ins]
    outs = [o if isinstance(o, tuple) else (o, VM) for o in outs]
    nbytes = sum(math.prod(a.shape) * a.dtype.itemsize for a, _ in ins + outs)
    return pl.pallas_call(
        body,
        out_shape=[o for o, _ in outs],
        in_specs=[s for _, s in ins],
        out_specs=[s for _, s in outs],
        scratch_shapes=list(scratch),
        input_output_aliases=aliases or {},
        compiler_params=pltpu.CompilerParams(vmem_limit_bytes=GRANT),
        cost_estimate=pl.CostEstimate(flops=flops, bytes_accessed=nbytes, transcendentals=0),
    )(*[i for i, _ in ins])


def far(array):
    return array, HB


def fetch_wait(sems, *pairs):
    for i, (s, d) in enumerate(pairs):
        pltpu.make_async_copy(s, d, sems.at[i]).wait()


def fetch(sems, *pairs):
    copies = [pltpu.make_async_copy(s, d, sems.at[i]) for i, (s, d) in enumerate(pairs)]
    for copy in copies:
        copy.start()
    return copies


class Spot:
    def __init__(self):
        z = lax.axis_index("z")
        self.core = lax.axis_index("core")
        self.top = jnp.logical_and(z == 0, self.core == 0)
        self.bottom = jnp.logical_and(z == 3, self.core == 1)
        self.place = lax.axis_index("x") * 4 + lax.axis_index("y")


ROW_FLOPS = 2 * 9 * FRAMES * WIDTH * CHANS * CHANS


def col_shift(v, by):
    turned = pltpu.roll(v, by % WIDTH, 0)
    at = lax.broadcasted_iota(jnp.int32, v.shape, 0)
    return jnp.where(at == (0 if by == 1 else WIDTH - 1), 0.0, turned)


HALVES = [slice(0, 128), slice(128, 256)]


def conv(rows, weight, flipped):
    height = rows.shape[0] - 2
    lhs = jnp.concatenate([rows[a : a + height] for a in range(3)], axis=-1)
    lhs = lhs.reshape(height * WIDTH, 3 * CHANS)
    parts = []
    for b in range(3):
        if flipped:
            rhs = jnp.concatenate([weight[2 - a, 2 - b] for a in range(3)], axis=1)
            y = lax.dot_general(lhs, rhs, (((1,), (1,)), ((), ())), preferred_element_type=F32)
        else:
            rhs = jnp.concatenate([weight[a, b] for a in range(3)], axis=0)
            y = jnp.dot(lhs, rhs, preferred_element_type=F32)
        parts.append(y.reshape(height, WIDTH, CHANS))

    def block(h, half):
        left, mid, right = (part[h, :, half] for part in parts)
        return mid + col_shift(left, 1) + col_shift(right, -1)

    return block


def spread_conv(field, weight):
    pieces = []
    for first, count, taps in ((0, 1, (2,)), (1, 1, (1, 2)), (2, 2, (0, 1, 2)), (4, 1, (0, 1)), (5, 1, (0,))):
        lhs = jnp.concatenate(
            [field[:, first + a - 2 : first + a - 2 + count] for a in taps], axis=-1
        ).reshape(FRAMES * count * WIDTH, len(taps) * CHANS)
        parts = []
        for b in range(3):
            rhs = jnp.concatenate([weight[2 - a, 2 - b] for a in taps], axis=1)
            y = lax.dot_general(lhs, rhs, (((1,), (1,)), ((), ())), preferred_element_type=F32)
            parts.append(y.reshape(FRAMES, count, WIDTH, CHANS))
        pieces += [(parts, k) for k in range(count)]

    def block(t, h, half):
        parts, k = pieces[h]
        left, mid, right = (part[t, k, :, half] for part in parts)
        return mid + col_shift(left, 1) + col_shift(right, -1)

    return block


def blocks(height):
    return [(h, half) for h in range(height) for half in HALVES]


def outer(spot, h, v):
    if h == 0:
        return jnp.where(spot.top, 0.0, v)
    if h == WIDE - 1:
        return jnp.where(spot.bottom, 0.0, v)
    return v


def put_chunks(send, h, half, v):
    for k in range(WIDTH // 16):
        place = h * WIDTH + k * 16
        send[place // PLACES, place % PLACES : place % PLACES + 16, half] = v[
            k * 16 : (k + 1) * 16
        ].astype(BF)


def take_chunks(ref, h, half):
    pieces = []
    for k in range(WIDTH // 16):
        place = h * WIDTH + k * 16
        pieces.append(ref[place // PLACES, place % PLACES : place % PLACES + 16, half])
    return jnp.concatenate(pieces, axis=0).astype(F32)


def transpose_rows(v_ref, out_ref, rows, at_row):
    lane = lax.broadcasted_iota(jnp.int32, (CHANS, WIDTH), 1)
    for t in range(FRAMES):
        for h in range(rows):
            flat = v_ref[t, h].astype(F32).T
            at = pl.ds(at_row(t, h) * WIDTH, WIDTH)
            left = jnp.where(lane == 0, 0.0, pltpu.roll(flat, 1, 1))
            right = jnp.where(lane == WIDTH - 1, 0.0, pltpu.roll(flat, WIDTH - 1, 1))
            out_ref[0:CHANS, at] = left.astype(BF)
            out_ref[CHANS : 2 * CHANS, at] = flat.astype(BF)
            out_ref[2 * CHANS : 3 * CHANS, at] = right.astype(BF)


def ready_body(x_far, in_far, params, x, in_weight, table, flat_mid, sems):
    copies = fetch(sems, (x_far, x), (in_far, in_weight))
    r = params[0:1, :]
    s0 = jnp.broadcast_to(params[2:3, 0:1], (1, CHANS))
    s1 = jnp.broadcast_to(params[2:3, 1:2], (1, CHANS))
    lines = [jnp.exp(-r * s0), jnp.exp(-r * s1), s0, s1, r, params[1:2, :], s0 + s1, r]
    for k, line in enumerate(lines):
        table[k : k + 1, :] = line
    copies[0].wait()
    transpose_rows(x, flat_mid, HEIGHT, lambda t, h: t * HEIGHT + h)
    copies[1].wait()


def place_halos(spot, from_core, from_chip, above, below):
    @pl.when(spot.core == 0)
    def _():
        above[...] = from_chip[...]
        below[...] = from_core[...]

    @pl.when(spot.core == 1)
    def _():
        above[...] = from_core[...]
        below[...] = from_chip[...]

    @pl.when(spot.top)
    def _():
        above[...] = jnp.zeros_like(above)

    @pl.when(spot.bottom)
    def _():
        below[...] = jnp.zeros_like(below)


def drive_body(
    x, from_core, from_chip, weight, table, local, send, flat_edge, above, below, edges
):
    spot = Spot()
    place_halos(spot, from_core, from_chip, above, below)
    for t in range(FRAMES):
        rows = jnp.concatenate([above[t], x[t], below[t]], axis=0)
        drive = conv(rows, weight, False)
        for h, half in blocks(WIDE):
            v = outer(spot, h, drive(h, half))
            if t == 1:
                v = table[1:2, half] * local[0, h, :, half] + v
                put_chunks(send, h, half, v)
            local[t, h, :, half] = v
    total = jnp.broadcast_to(table[6:7, :][None], (BLOCKS, NOTE, CHANS))
    row = lax.broadcasted_iota(jnp.int32, total.shape, 1)
    one = total.astype(BF).astype(F32)
    two = (total - one).astype(BF).astype(F32)
    three = total - one - two
    send[:, PLACES : PLACES + NOTE, :] = jnp.where(
        row == 0, one, jnp.where(row == 1, two, jnp.where(row == 2, three, 0.0))
    ).astype(BF)
    edges[:, 0:2] = above[...]
    edges[:, 2:4] = below[...]
    transpose_rows(edges, flat_edge, 4, lambda t, h: t * 4 + h)


def forward_scan_body(got, table, send, block_decays):
    carry = jnp.zeros((PLACES, CHANS), F32)
    for k in range(BLOCKS):
        send[k] = carry.astype(BF)
        span = jnp.sum(got[k, PLACES : PLACES + NOTE, :].astype(F32), axis=0, keepdims=True)
        d = jnp.exp(-table[4:5, :] * span)
        block_decays[pl.ds(k, 1), :] = d
        carry = d * carry + got[k, 0:PLACES, :].astype(F32)


def backward_scan_body(got, block_decays, send):
    carry = jnp.zeros((PLACES, CHANS), F32)
    for k in reversed(range(BLOCKS)):
        send[k] = carry.astype(BF)
        carry = block_decays[pl.ds(k, 1), :] * carry + got[k].astype(F32)


GELU_A = math.sqrt(2 / math.pi)


def spread(*vectors):
    row = lax.broadcasted_iota(jnp.int32, (8, 128), 0) % 4
    halves = []
    for half in HALVES:
        out = jnp.zeros((8, 128), F32)
        for k, vector in enumerate(vectors):
            out = jnp.where(row == k, jnp.broadcast_to(vector[:, half], (8, 128)), out)
        halves.append(out)
    return halves


def split_pairs(both):
    row = lax.broadcasted_iota(jnp.int32, (8, 128), 0)
    top = both.astype(BF).astype(F32)
    return jnp.where(row < 4, top, both - top)


def joined(pairs):
    return pairs + pltpu.roll(pairs, 4, 0)


def middle_body(
    local, carry, x, cot, weight, table,
    out_far, direct_far, gz, state, state_f, local_adj, send, skip, out, direct, sems,
):
    spot = Spot()
    d0, d1 = table[0:1, :], table[1:2, :]
    for h, half in blocks(WIDE):
        c = take_chunks(carry, h, half)
        s0 = local[0, h, :, half] + d0[:, half] * c
        state_f[h, :, half] = s0
        state[0, h, :, half] = s0.astype(BF)
        s1 = local[1, h, :, half] + (d0 * d1)[:, half] * c
        state[1, h, :, half] = s1.astype(BF)
    totals = [jnp.zeros((8, 128), F32) for _ in HALVES]
    copies = []
    for t in (1, 0):
        pre_act = conv(state[t], weight, False)
        for h, half in blocks(HEIGHT):
            xt = x[t, h, :, half].astype(F32)
            z = pre_act(h, half) + table[5:6, half] * xt
            zz = z * z
            th = jnp.tanh(GELU_A * (z + 0.044715 * (zz * z)))
            gate = 0.5 * (1.0 + th)
            out[t, h, :, half] = (z * gate).astype(BF)
            slope = gate + 0.5 * z * (1.0 - th * th) * (GELU_A * (1.0 + 3 * 0.044715 * zz))
            g = cot[t, h, :, half].astype(F32) * slope
            gz[t, h, :, half] = g.astype(BF)
            direct[t, h, :, half] = (table[5:6, half] * g).astype(BF)
            k = HALVES.index(half)
            totals[k] = totals[k] + jnp.sum((g * xt).reshape(WIDTH // 8, 8, 128), axis=0)
        copies += fetch(sems.at[t], (out.at[t], out_far.at[t]), (direct.at[t], direct_far.at[t]))
    grad = spread_conv(gz, weight)
    for t in (1, 0):
        for h, half in blocks(WIDE):
            v = outer(spot, h, grad(t, h, half))
            if t == 0:
                v = v + d1[:, half] * local_adj[1, h, :, half]
                put_chunks(send, h, half, d0[:, half] * v)
            local_adj[t, h, :, half] = v
    total = jnp.concatenate([jnp.sum(v, axis=0, keepdims=True) for v in totals], axis=1)
    skip[...] = total
    for copy in copies:
        copy.wait()


def pack_grad(g, a, scale, out):
    for b in range(3):
        tap = (3 * a + b) * 8
        for lg, half in enumerate(HALVES):
            part = g[b * CHANS : (b + 1) * CHANS, half] * scale
            out[:, lg, tap : tap + 8, :] = part.astype(BF).reshape(GROUPS, 8, 128)


def out_grad_body(scale, state, gz, out, flat):
    transpose_rows(state, flat, WIDE, lambda t, h: t * WIDE + h)
    rhs = gz[...].reshape(FRAMES * HEIGHT * WIDTH, CHANS)
    for a in range(3):
        lhs = jnp.concatenate(
            [flat[:, pl.ds((t * WIDE + a) * WIDTH, HEIGHT * WIDTH)] for t in range(FRAMES)], axis=1
        )
        pack_grad(jnp.dot(lhs, rhs, preferred_element_type=F32), a, scale, out)
    out[:, :, TAPS:PACK, :] = jnp.zeros((GROUPS, 2, 8, 128), BF)


def in_grad(scale, adj, small, flat_mid, flat_edge, out):
    rhs = adj[...].reshape(FRAMES * WIDE * WIDTH, CHANS)
    for a in range(3):
        pieces = []
        for t in range(FRAMES):
            at = t * 4 * WIDTH
            if a < 2:
                pieces.append(flat_edge[:, at + a * WIDTH : at + 2 * WIDTH])
            pieces.append(flat_mid[:, at : at + 4 * WIDTH])
            if a > 0:
                pieces.append(flat_edge[:, at + 2 * WIDTH : at + (2 + a) * WIDTH])
        g = jnp.dot(jnp.concatenate(pieces, axis=1), rhs, preferred_element_type=F32)
        pack_grad(g, a, scale, out)
    out[:, :, TAPS:PACK, :] = jnp.zeros((GROUPS, 2, 8, 128), BF)
    for lg in range(2):
        out[0, lg, TAPS:PACK, :] = split_pairs(small[lg]).astype(BF)


def odd_grad_body(
    scale, step_scale, local, incoming, state_f, carry, table, skip, flat_mid, flat_edge, out_part,
    payload, small, adj, adj_far, to_core, to_chip, sems,
):
    spot = Spot()
    d0, d1 = table[0:1, :], table[1:2, :]
    sums = [[jnp.zeros((8, 128), F32) for _ in HALVES] for _ in range(FRAMES)]
    for h, half in blocks(WIDE):
        c = take_chunks(incoming, h, half)
        a0 = local[0, h, :, half] + d1[:, half] * c
        a1 = local[1, h, :, half] + c
        adj[0, h, :, half] = a0.astype(BF)
        adj[1, h, :, half] = a1.astype(BF)
        k = HALVES.index(half)
        pairs = ((a0, take_chunks(carry, h, half)), (a1, state_f[h, :, half]))
        for t, (a, earlier) in enumerate(pairs):
            sums[t][k] = sums[t][k] + jnp.sum((a * earlier).reshape(WIDTH // 8, 8, 128), axis=0)
    up, down = adj.at[:, 0:2], adj.at[:, WIDE - 2 :]
    (whole,) = fetch(sems.at[2:3], (adj, adj_far))

    @pl.when(spot.core == 0)
    def _():
        fetch(sems, (up, to_chip), (down, to_core))

    @pl.when(spot.core == 1)
    def _():
        fetch(sems, (down, to_chip), (up, to_core))

    k0, k1 = (
        jnp.concatenate([jnp.sum(v, axis=0, keepdims=True) for v in pair], axis=1) * d
        for pair, d in zip(sums, (d0, d1))
    )
    rate_part = (k0 * table[2:3, :] + k1 * table[3:4, :]) * (-scale)
    s0 = jnp.sum(k0 * table[4:5, :], axis=1, keepdims=True) * (-step_scale)
    s1 = jnp.sum(k1 * table[4:5, :], axis=1, keepdims=True) * (-step_scale)
    lane = lax.broadcasted_iota(jnp.int32, (1, CHANS), 1)
    at = spot.place * FRAMES
    steps = jnp.where(lane == at, s0, jnp.where(lane == at + 1, s1, 0.0))
    small[0], small[1] = spread(rate_part, steps, skip[...] * scale)

    @pl.when(spot.core == 0)
    def _():
        (copy,) = fetch(sems.at[3:4], (out_part, payload))
        copy.wait()

    @pl.when(spot.core == 1)
    def _():
        in_grad(scale, adj, small, flat_mid, flat_edge, payload)

    fetch_wait(sems, (up, to_chip), (down, to_core))
    whole.wait()


def even_grad_body(scale, adj, small, flat_mid, flat_edge, out_part, mine, sems):
    spot = Spot()

    @pl.when(spot.core == 0)
    def _():
        in_grad(scale, adj, small, flat_mid, flat_edge, mine)

    @pl.when(spot.core == 1)
    def _():
        (copy,) = fetch(sems, (out_part, mine))
        copy.wait()


def grad_inputs_body(
    adj_far, core_far, chip_far, weight_far, direct_far,
    out_far, adj, from_core, from_chip, weight, direct, out, above, below, sems,
):
    spot = Spot()
    copies = fetch(
        sems,
        (core_far, from_core),
        (chip_far, from_chip),
        (adj_far, adj),
        (weight_far, weight),
        (direct_far, direct),
    )
    for copy in copies:
        copy.wait()
    place_halos(spot, from_core, from_chip, above, below)
    for t in range(FRAMES):
        up = (adj[t, 0:2].astype(F32) + above[t].astype(F32)).astype(BF)
        down = (adj[t, WIDE - 2 :].astype(F32) + below[t].astype(F32)).astype(BF)
        rows = jnp.concatenate([up, adj[t, 2 : WIDE - 2], down], axis=0)
        grad = conv(rows, weight, True)
        for h, half in blocks(HEIGHT):
            own = direct[t, h, :, half].astype(F32)
            out[t, h, :, half] = (grad(h, half) + own).astype(BF)
    (copy,) = fetch(sems, (out, out_far))
    copy.wait()


def pair_sum_body(mine, got, send_far, send, sems):
    copies = []
    for k in range(GROUPS):
        send[k] = (mine[k].astype(F32) + got[k].astype(F32)).astype(BF)
        if k == 0:
            for lg in range(2):
                pairs = mine[0, lg, TAPS:PACK, :].astype(F32) + got[0, lg, TAPS:PACK, :].astype(F32)
                send[0, lg, TAPS:PACK, :] = split_pairs(joined(pairs)).astype(BF)
        if k % 8 == 7:
            part = slice(k - 7, k + 1)
            copies += fetch(sems.at[k // 8 : k // 8 + 1], (send.at[part], send_far.at[part]))
    for copy in copies:
        copy.wait()


def all_sum_body(got, send_far, send, sems):
    total = jnp.zeros((PACK, 128), F32)
    for k in range(CHIPS):
        total = total + got[k].astype(F32)
    extras = split_pairs(joined(total[TAPS:PACK]))
    total = jnp.concatenate([total[0:TAPS], extras], axis=0).astype(BF)
    send[...] = jnp.broadcast_to(total[None], send.shape)
    pairs = [(send, send_far.at[8 * k : 8 * k + 8]) for k in range(8)]
    for copy in fetch(sems, *pairs):
        copy.wait()


def write_grad(src, grad, stage, sems):
    copies = []
    for a in range(3):
        for b in range(3):
            tap = (3 * a + b) * 8
            for lg, half in enumerate(HALVES):
                part = src[:, lg, tap : tap + 8, :].astype(F32)
                stage[a, b, :, half] = part.reshape(CHANS, 128)
        copies += fetch(sems.at[a : a + 1], (stage.at[a], grad.at[a]))
    for copy in copies:
        copy.wait()


def unpack_own_body(own, grad_out, grad_in, stage, sems):
    core = Spot().core

    @pl.when(core == 0)
    def _():
        write_grad(own, grad_in, stage, sems)

    @pl.when(core == 1)
    def _():
        write_grad(own, grad_out, stage, sems)


def unpack_other_body(
    own, got, out_half, in_half, grad_out, grad_in, rate, skip, step, stage, sems
):
    del out_half, in_half
    spot = Spot()

    def smalls(src):
        for lg in range(2):
            extras = joined(src[0, lg, TAPS:PACK, :].astype(F32))
            rate[lg : lg + 1, :] = extras[0:1]
            skip[lg : lg + 1, :] = extras[2:3]
            if lg == 0:
                turned = pltpu.roll(extras, (128 - spot.place * FRAMES) % 128, 1)
                step[...] = turned[1:2, 0:FRAMES]

    @pl.when(spot.core == 0)
    def _():
        smalls(own)
        write_grad(got, grad_out, stage, sems)

    @pl.when(spot.core == 1)
    def _():
        smalls(got)
        write_grad(got, grad_in, stage, sems)


ROWS_AXES = ("z", "core")
TM_AXES = ("x", "y")
CORE_PAIRS = [(i, i ^ 1) for i in range(8)]
CHIP_PAIRS = [(i, (i + 1) % 8 if i % 2 else (i - 1) % 8) for i in range(8)]


def halos(to_core, to_chip):
    from_chip = lax.ppermute(to_chip, ROWS_AXES, CHIP_PAIRS)
    from_core = lax.ppermute(to_core, ROWS_AXES, CORE_PAIRS)
    return from_core, from_chip


def swap(chunks, axes):
    return lax.all_to_all(chunks, axes, 0, 0)


def vmem(shape, dtype=BF):
    return pltpu.VMEM(shape, dtype)


def sems(*shape):
    return pltpu.SemaphoreType.DMA(shape)


def on_device(inputs, in_weight, out_weight, skip_gain, rates, step_sizes, cotangent):
    scale = 1.0 / math.sqrt(32 * 32 * 128)
    step_scale = 1.0 / math.sqrt(1048576)
    core = lax.axis_index("core")
    field = (FRAMES, HEIGHT, WIDTH, CHANS)
    wide = (FRAMES, WIDE, WIDTH, CHANS)
    edge = (FRAMES, 2, WIDTH, CHANS)
    kernel = (3, 3, CHANS, CHANS)
    chunk = sds((BLOCKS, PLACES, CHANS), BF)
    packed = sds((GROUPS, 2, PACK, 128), BF)
    flat = sds((3 * CHANS, FRAMES * 4 * WIDTH), BF)
    params = jnp.concatenate([rates, skip_gain, jnp.pad(step_sizes, (0, CHANS - FRAMES))])
    params = params.reshape(3, CHANS)

    to_core = lax.dynamic_slice(inputs, (0, 2 - 2 * core, 0, 0), edge)
    to_chip = lax.dynamic_slice(inputs, (0, 2 * core, 0, 0), edge)
    from_core, from_chip = halos(to_core, to_chip)
    x, in_w, table, flat_mid = call(
        ready_body,
        [sds(field, BF), sds(kernel, BF), sds((8, CHANS), F32), flat],
        [far(inputs), far(in_weight), params],
        2 * ROW_FLOPS,
        [sems(2)],
    )
    local, send, flat_edge = call(
        drive_body,
        [sds(wide, F32), sds((BLOCKS, PLACES + NOTE, CHANS), BF), flat],
        [x, from_core, from_chip, in_w, table],
        WIDE * ROW_FLOPS,
        [vmem(edge), vmem(edge), vmem(field)],
    )
    got = swap(send, TM_AXES)
    send, block_decays = call(forward_scan_body, [chunk, sds((BLOCKS, CHANS), F32)], [got, table])
    carry = swap(send, TM_AXES)
    outputs, direct, gz, state, state_f, local_adj, send, skip = call(
        middle_body,
        [
            far(sds(field, BF)),
            far(sds(field, BF)),
            sds(field, BF),
            sds(wide, BF),
            sds(wide[1:], F32),
            sds(wide, F32),
            chunk,
            sds((1, CHANS), F32),
        ],
        [local, carry, x, cotangent, out_weight, table],
        (HEIGHT + WIDE) * ROW_FLOPS,
        [vmem(field), vmem(field), sems(FRAMES, 2)],
    )
    (out_part,) = call(
        functools.partial(out_grad_body, scale),
        [packed],
        [state, gz],
        HEIGHT * ROW_FLOPS,
        [vmem((3 * CHANS, FRAMES * WIDE * WIDTH))],
    )
    send, out_part = lax.optimization_barrier((send, out_part))
    got = swap(send, TM_AXES)
    (send,) = call(backward_scan_body, [chunk], [got, block_decays])
    incoming = swap(send, TM_AXES)
    payload, small, adj, adj_far, to_core, to_chip = call(
        functools.partial(odd_grad_body, scale, step_scale),
        [
            packed,
            sds((2, 8, 128), F32),
            sds(wide, BF),
            far(sds(wide, BF)),
            far(sds(edge, BF)),
            far(sds(edge, BF)),
        ],
        [local_adj, incoming, state_f, carry, table, skip, flat_mid, flat_edge, out_part],
        WIDE * ROW_FLOPS,
        [sems(4)],
    )
    got = lax.ppermute(payload, ROWS_AXES, CORE_PAIRS)
    (mine,) = call(
        functools.partial(even_grad_body, scale),
        [packed],
        [adj, small, flat_mid, flat_edge, out_part],
        WIDE * ROW_FLOPS,
        [sems(1)],
    )
    from_core, from_chip = halos(to_core, to_chip)
    (send,) = call(pair_sum_body, [far(packed)], [mine, got], 0, [vmem(packed.shape), sems(4)])
    got = swap(send.reshape(CHIPS, PACK, 128), ("x", "y", "z"))
    (send,) = call(
        all_sum_body,
        [far(sds((CHIPS, PACK, 128), BF))],
        [got],
        0,
        [vmem((8, PACK, 128)), sems(8)],
    )
    send, from_core, from_chip = lax.optimization_barrier((send, from_core, from_chip))
    own = swap(send, ("x", "y", "z"))
    (grad_inputs,) = call(
        grad_inputs_body,
        [far(sds(field, BF))],
        [far(a) for a in (adj_far, from_core, from_chip, in_weight, direct)],
        HEIGHT * ROW_FLOPS,
        [
            vmem(wide),
            vmem(edge),
            vmem(edge),
            vmem(kernel),
            vmem(field),
            vmem(field),
            vmem(edge),
            vmem(edge),
            sems(5),
        ],
        {4: 0},
    )
    own, grad_inputs = lax.optimization_barrier((own, grad_inputs))
    own = own.reshape(packed.shape)
    other = lax.ppermute(own, ROWS_AXES, CORE_PAIRS)
    weights = sds(kernel, F32)
    half = sds((2, 128), F32)
    stage = vmem(kernel, F32)
    grad_out_weight, grad_in_weight = call(
        unpack_own_body, [far(weights), far(weights)], [own], 0, [stage, sems(3)]
    )
    grad_out_weight, grad_in_weight, grad_rates, grad_skip, grad_steps = call(
        unpack_other_body,
        [far(weights), far(weights), half, half, sds((1, FRAMES), F32)],
        [own, other, far(grad_out_weight), far(grad_in_weight)],
        0,
        [stage, sems(3)],
        {2: 0, 3: 1},
    )
    return (
        outputs,
        grad_inputs,
        grad_in_weight,
        grad_out_weight,
        grad_skip.reshape(CHANS),
        grad_rates.reshape(CHANS),
        grad_steps.reshape(FRAMES),
    )


def solution(mesh):
    fine = Mesh(mesh.devices.reshape(4, 4, 4, 2), ("x", "y", "z", "core"))
    spread_out = P(TM_AXES, ROWS_AXES, None, None)
    placed = (spread_out, P(), P(), P(), P(), P(TM_AXES), spread_out)
    return jax.shard_map(
        on_device,
        mesh=fine,
        in_specs=placed,
        out_specs=(spread_out, spread_out, P(), P(), P(), P(), P(TM_AXES)),
        check_vma=False,
    )
```

```python
import functools
import math

import jax
import jax.numpy as jnp
from jax import lax
from jax.experimental import pallas as pl
from jax.experimental.pallas import tpu as pltpu
from jax.sharding import Mesh, PartitionSpec as P

BF, F32 = jnp.bfloat16, jnp.float32
VM = pl.BlockSpec(memory_space=pltpu.VMEM)
HB = pl.BlockSpec(memory_space=pltpu.HBM)
GRANT = 24 << 20
FRAMES, HEIGHT, WIDTH, CHANS = 2, 4, 128, 256
WIDE, WIDER = HEIGHT + 2, HEIGHT + 4
BLOCKS = 16
PLACES = WIDE * WIDTH // BLOCKS
NOTE = 8
CHIPS = 64
GROUPS = 32
TAPS = 72
PACK = TAPS + 8


def sds(shape, dtype):
    return jax.ShapeDtypeStruct(shape, dtype)


def call(body, outs, ins, flops=0, scratch=(), aliases=None):
    ins = [i if isinstance(i, tuple) else (i, VM) for i in ins]
    outs = [o if isinstance(o, tuple) else (o, VM) for o in outs]
    nbytes = sum(math.prod(a.shape) * a.dtype.itemsize for a, _ in ins + outs)
    return pl.pallas_call(
        body,
        out_shape=[o for o, _ in outs],
        in_specs=[s for _, s in ins],
        out_specs=[s for _, s in outs],
        scratch_shapes=list(scratch),
        input_output_aliases=aliases or {},
        compiler_params=pltpu.CompilerParams(vmem_limit_bytes=GRANT),
        cost_estimate=pl.CostEstimate(flops=flops, bytes_accessed=nbytes, transcendentals=0),
    )(*[i for i, _ in ins])


def far(array):
    return array, HB


def fetch(sems, *pairs):
    copies = [pltpu.make_async_copy(s, d, sems.at[i]) for i, (s, d) in enumerate(pairs)]
    for copy in copies:
        copy.start()
    return copies


class Spot:
    def __init__(self):
        z = lax.axis_index("z")
        self.core = lax.axis_index("core")
        self.top = jnp.logical_and(z == 0, self.core == 0)
        self.bottom = jnp.logical_and(z == 3, self.core == 1)
        self.place = lax.axis_index("x") * 4 + lax.axis_index("y")


ROW_FLOPS = 2 * 9 * FRAMES * WIDTH * CHANS * CHANS


def col_shift(v, by):
    turned = pltpu.roll(v, by % WIDTH, 0)
    at = lax.broadcasted_iota(jnp.int32, v.shape, 0)
    return jnp.where(at == (0 if by == 1 else WIDTH - 1), 0.0, turned)


HALVES = [slice(0, 128), slice(128, 256)]


def conv(rows, weight, flipped):
    height = rows.shape[0] - 2
    lhs = jnp.concatenate([rows[a : a + height] for a in range(3)], axis=-1)
    lhs = lhs.reshape(height * WIDTH, 3 * CHANS)
    parts = []
    for b in range(3):
        if flipped:
            rhs = jnp.concatenate([weight[2 - a, 2 - b] for a in range(3)], axis=1)
            y = lax.dot_general(lhs, rhs, (((1,), (1,)), ((), ())), preferred_element_type=F32)
        else:
            rhs = jnp.concatenate([weight[a, b] for a in range(3)], axis=0)
            y = jnp.dot(lhs, rhs, preferred_element_type=F32)
        parts.append(y.reshape(height, WIDTH, CHANS))

    def block(h, half):
        left, mid, right = (part[h, :, half] for part in parts)
        return mid + col_shift(left, 1) + col_shift(right, -1)

    return block


def spread_conv(field, weight):
    pieces = []
    for first, count, taps in ((0, 1, (2,)), (1, 1, (1, 2)), (2, 2, (0, 1, 2)), (4, 1, (0, 1)), (5, 1, (0,))):
        lhs = jnp.concatenate(
            [field[:, first + a - 2 : first + a - 2 + count] for a in taps], axis=-1
        ).reshape(FRAMES * count * WIDTH, len(taps) * CHANS)
        parts = []
        for b in range(3):
            rhs = jnp.concatenate([weight[2 - a, 2 - b] for a in taps], axis=1)
            y = lax.dot_general(lhs, rhs, (((1,), (1,)), ((), ())), preferred_element_type=F32)
            parts.append(y.reshape(FRAMES, count, WIDTH, CHANS))
        pieces += [(parts, k) for k in range(count)]

    def block(t, h, half):
        parts, k = pieces[h]
        left, mid, right = (part[t, k, :, half] for part in parts)
        return mid + col_shift(left, 1) + col_shift(right, -1)

    return block


def blocks(height):
    return [(h, half) for h in range(height) for half in HALVES]


def outer(spot, h, v):
    if h == 0:
        return jnp.where(spot.top, 0.0, v)
    if h == WIDE - 1:
        return jnp.where(spot.bottom, 0.0, v)
    return v


def put_chunks(send, h, half, v):
    for k in range(WIDTH // 16):
        place = h * WIDTH + k * 16
        send[place // PLACES, place % PLACES : place % PLACES + 16, half] = v[
            k * 16 : (k + 1) * 16
        ].astype(BF)


def take_chunks(ref, h, half):
    pieces = []
    for k in range(WIDTH // 16):
        place = h * WIDTH + k * 16
        pieces.append(ref[place // PLACES, place % PLACES : place % PLACES + 16, half])
    return jnp.concatenate(pieces, axis=0).astype(F32)


def transpose_rows(v_ref, out_ref, rows, at_row):
    lane = lax.broadcasted_iota(jnp.int32, (CHANS, WIDTH), 1)
    for t in range(FRAMES):
        for h in range(rows):
            flat = v_ref[t, h].astype(F32).T
            at = pl.ds(at_row(t, h) * WIDTH, WIDTH)
            left = jnp.where(lane == 0, 0.0, pltpu.roll(flat, 1, 1))
            right = jnp.where(lane == WIDTH - 1, 0.0, pltpu.roll(flat, WIDTH - 1, 1))
            out_ref[0:CHANS, at] = left.astype(BF)
            out_ref[CHANS : 2 * CHANS, at] = flat.astype(BF)
            out_ref[2 * CHANS : 3 * CHANS, at] = right.astype(BF)


def ready_body(x_far, in_far, params, x, in_weight, table, flat_mid, sems):
    copies = fetch(sems, (x_far, x), (in_far, in_weight))
    r = params[0:1, :]
    s0 = jnp.broadcast_to(params[2:3, 0:1], (1, CHANS))
    s1 = jnp.broadcast_to(params[2:3, 1:2], (1, CHANS))
    lines = [jnp.exp(-r * s0), jnp.exp(-r * s1), s0, s1, r, params[1:2, :], s0 + s1, r]
    for k, line in enumerate(lines):
        table[k : k + 1, :] = line
    copies[0].wait()
    transpose_rows(x, flat_mid, HEIGHT, lambda t, h: t * HEIGHT + h)
    copies[1].wait()


def place_halos(spot, from_core, from_chip, above, below):
    @pl.when(spot.core == 0)
    def _():
        above[...] = from_chip[...]
        below[...] = from_core[...]

    @pl.when(spot.core == 1)
    def _():
        above[...] = from_core[...]
        below[...] = from_chip[...]

    @pl.when(spot.top)
    def _():
        above[...] = jnp.zeros_like(above)

    @pl.when(spot.bottom)
    def _():
        below[...] = jnp.zeros_like(below)


def drive_body(
    x, from_core, from_chip, weight, table, local, send, flat_edge, above, below, edges
):
    spot = Spot()
    place_halos(spot, from_core, from_chip, above, below)
    for t in range(FRAMES):
        rows = jnp.concatenate([above[t], x[t], below[t]], axis=0)
        drive = conv(rows, weight, False)
        for h, half in blocks(WIDE):
            v = outer(spot, h, drive(h, half))
            if t == 1:
                v = table[1:2, half] * local[0, h, :, half] + v
                put_chunks(send, h, half, v)
            local[t, h, :, half] = v
    total = jnp.broadcast_to(table[6:7, :][None], (BLOCKS, NOTE, CHANS))
    row = lax.broadcasted_iota(jnp.int32, total.shape, 1)
    one = total.astype(BF).astype(F32)
    two = (total - one).astype(BF).astype(F32)
    three = total - one - two
    send[:, PLACES : PLACES + NOTE, :] = jnp.where(
        row == 0, one, jnp.where(row == 1, two, jnp.where(row == 2, three, 0.0))
    ).astype(BF)
    edges[:, 0:2] = above[...]
    edges[:, 2:4] = below[...]
    transpose_rows(edges, flat_edge, 4, lambda t, h: t * 4 + h)


def forward_scan_body(got, table, send, block_decays):
    carry = jnp.zeros((PLACES, CHANS), F32)
    for k in range(BLOCKS):
        send[k] = carry.astype(BF)
        span = jnp.sum(got[k, PLACES : PLACES + NOTE, :].astype(F32), axis=0, keepdims=True)
        d = jnp.exp(-table[4:5, :] * span)
        block_decays[pl.ds(k, 1), :] = d
        carry = d * carry + got[k, 0:PLACES, :].astype(F32)


def backward_scan_body(got, block_decays, send):
    carry = jnp.zeros((PLACES, CHANS), F32)
    for k in reversed(range(BLOCKS)):
        send[k] = carry.astype(BF)
        carry = block_decays[pl.ds(k, 1), :] * carry + got[k].astype(F32)


GELU_A = math.sqrt(2 / math.pi)


def small_rows(rate, skip, steps):
    row = lax.broadcasted_iota(jnp.int32, (8, 128), 0)
    halves = [v[:, half] for v in (rate, skip) for half in HALVES]
    lines = halves + [steps, steps] + halves[0:2]
    out = jnp.zeros((8, 128), F32)
    for k, line in enumerate(lines):
        out = jnp.where(row == k, jnp.broadcast_to(line, (8, 128)), out)
    top = out.astype(BF).astype(F32)
    return jnp.where(row < 5, top, out - top).astype(BF)


def middle_body(
    local, carry, x, cot, weight, table,
    out_far, direct_far, message, state_f, local_adj, send, skip, out, direct, sems,
):
    spot = Spot()
    state, gz = message.at[:, 0:WIDE], message.at[:, WIDE:]
    d0, d1 = table[0:1, :], table[1:2, :]
    for h, half in blocks(WIDE):
        c = take_chunks(carry, h, half)
        s0 = local[0, h, :, half] + d0[:, half] * c
        state_f[h, :, half] = s0
        state[0, h, :, half] = s0.astype(BF)
        s1 = local[1, h, :, half] + (d0 * d1)[:, half] * c
        state[1, h, :, half] = s1.astype(BF)
    totals = [jnp.zeros((8, 128), F32) for _ in HALVES]
    copies = []
    for t in (1, 0):
        pre_act = conv(state[t], weight, False)
        for h, half in blocks(HEIGHT):
            xt = x[t, h, :, half].astype(F32)
            z = pre_act(h, half) + table[5:6, half] * xt
            zz = z * z
            th = jnp.tanh(GELU_A * (z + 0.044715 * (zz * z)))
            gate = 0.5 * (1.0 + th)
            out[t, h, :, half] = (z * gate).astype(BF)
            slope = gate + 0.5 * z * (1.0 - th * th) * (GELU_A * (1.0 + 3 * 0.044715 * zz))
            g = cot[t, h, :, half].astype(F32) * slope
            gz[t, h, :, half] = g.astype(BF)
            direct[t, h, :, half] = (table[5:6, half] * g).astype(BF)
            k = HALVES.index(half)
            totals[k] = totals[k] + jnp.sum((g * xt).reshape(WIDTH // 8, 8, 128), axis=0)
        copies += fetch(sems.at[t], (out.at[t], out_far.at[t]), (direct.at[t], direct_far.at[t]))
    grad = spread_conv(gz, weight)
    for t in (1, 0):
        for h, half in blocks(WIDE):
            v = outer(spot, h, grad(t, h, half))
            if t == 0:
                v = v + d1[:, half] * local_adj[1, h, :, half]
                put_chunks(send, h, half, d0[:, half] * v)
            local_adj[t, h, :, half] = v
    total = jnp.concatenate([jnp.sum(v, axis=0, keepdims=True) for v in totals], axis=1)
    skip[...] = total
    for copy in copies:
        copy.wait()


def pack_grad(g, a, scale, out):
    for b in range(3):
        tap = (3 * a + b) * 8
        part = (g[b * CHANS : (b + 1) * CHANS] * scale).astype(BF)
        out[:, tap : tap + 8, :] = part.reshape(GROUPS, 8, CHANS)


def out_grad(state, gz, flat):
    transpose_rows(state, flat, WIDE, lambda t, h: t * WIDE + h)
    rhs = gz[...].reshape(FRAMES * HEIGHT * WIDTH, CHANS)
    for a in range(3):
        lhs = jnp.concatenate(
            [flat[:, pl.ds((t * WIDE + a) * WIDTH, HEIGHT * WIDTH)] for t in range(FRAMES)], axis=1
        )
        yield a, jnp.dot(lhs, rhs, preferred_element_type=F32)


def in_grad(adj, flat_mid, flat_edge):
    rhs = adj[...].reshape(FRAMES * WIDE * WIDTH, CHANS)
    for a in range(3):
        pieces = []
        for t in range(FRAMES):
            at = t * 4 * WIDTH
            if a < 2:
                pieces.append(flat_edge[:, at + a * WIDTH : at + 2 * WIDTH])
            pieces.append(flat_mid[:, at : at + 4 * WIDTH])
            if a > 0:
                pieces.append(flat_edge[:, at + 2 * WIDTH : at + (2 + a) * WIDTH])
        yield a, jnp.dot(jnp.concatenate(pieces, axis=1), rhs, preferred_element_type=F32)


def adjoint_stage(scales, spot, sources, adj, small):
    local, incoming, state_f, carry, table, skip = sources
    d0, d1 = table[0:1, :], table[1:2, :]
    sums = [[jnp.zeros((8, 128), F32) for _ in HALVES] for _ in range(FRAMES)]
    for h, half in blocks(WIDE):
        c = take_chunks(incoming, h, half)
        a0 = local[0, h, :, half] + d1[:, half] * c
        a1 = local[1, h, :, half] + c
        adj[0, h, :, half] = a0.astype(BF)
        adj[1, h, :, half] = a1.astype(BF)
        k = HALVES.index(half)
        pairs = ((a0, take_chunks(carry, h, half)), (a1, state_f[h, :, half]))
        for t, (a, earlier) in enumerate(pairs):
            sums[t][k] = sums[t][k] + jnp.sum((a * earlier).reshape(WIDTH // 8, 8, 128), axis=0)
    k0, k1 = (
        jnp.concatenate([jnp.sum(v, axis=0, keepdims=True) for v in pair], axis=1) * d
        for pair, d in zip(sums, (d0, d1))
    )
    rate = (k0 * table[2:3, :] + k1 * table[3:4, :]) * (-scales[0])
    s0 = jnp.sum(k0 * table[4:5, :], axis=1, keepdims=True) * (-scales[1])
    s1 = jnp.sum(k1 * table[4:5, :], axis=1, keepdims=True) * (-scales[1])
    lane = lax.broadcasted_iota(jnp.int32, (1, 128), 1)
    at = spot.place * FRAMES
    steps = jnp.where(lane == at, s0, jnp.where(lane == at + 1, s1, 0.0))
    small[...] = small_rows(rate, skip[...] * scales[0], steps)


def odd_grad_body(
    scales, local, incoming, state_f, carry, table, skip, flat_mid, flat_edge, message, flat_message,
    payload, out_part, adj, small, flat,
):
    spot = Spot()

    @pl.when(spot.core == 0)
    def _():
        payload[...] = flat_message[...]

    @pl.when(spot.core == 1)
    def _():
        adjoint_stage(scales, spot, (local, incoming, state_f, carry, table, skip), adj, small)
        for a, g in in_grad(adj, flat_mid, flat_edge):
            pack_grad(g, a, scales[0], payload)
        for a, g in out_grad(message.at[:, 0:WIDE], message.at[:, WIDE:], flat):
            pack_grad(g, a, scales[0], out_part)


def even_grad_body(
    scales, local, incoming, state_f, carry, table, skip, flat_mid, flat_edge, odd_adj, odd_small,
    mine, adj, to_core, to_chip, small,
):
    spot = Spot()

    @pl.when(spot.core == 0)
    def _():
        adjoint_stage(scales, spot, (local, incoming, state_f, carry, table, skip), adj, small)
        to_chip[...] = adj[:, 0:2]
        to_core[...] = adj[:, WIDE - 2 :]
        for a, g in in_grad(adj, flat_mid, flat_edge):
            pack_grad(g, a, scales[0], mine)

    @pl.when(spot.core == 1)
    def _():
        adj[...] = odd_adj[...]
        small[...] = odd_small[...]
        to_core[...] = odd_adj[:, 0:2]
        to_chip[...] = odd_adj[:, WIDE - 2 :]


def grad_inputs_body(
    adj_far, core_far, chip_far, weight_far, direct_far,
    out_far, adj, from_core, from_chip, weight, direct, out, above, below, sems,
):
    spot = Spot()
    copies = fetch(
        sems,
        (core_far, from_core),
        (chip_far, from_chip),
        (adj_far, adj),
        (weight_far, weight),
        (direct_far, direct),
    )
    for copy in copies:
        copy.wait()
    place_halos(spot, from_core, from_chip, above, below)
    for t in range(FRAMES):
        up = (adj[t, 0:2].astype(F32) + above[t].astype(F32)).astype(BF)
        down = (adj[t, WIDE - 2 :].astype(F32) + below[t].astype(F32)).astype(BF)
        rows = jnp.concatenate([up, adj[t, 2 : WIDE - 2], down], axis=0)
        grad = conv(rows, weight, True)
        for h, half in blocks(HEIGHT):
            own = direct[t, h, :, half].astype(F32)
            out[t, h, :, half] = (grad(h, half) + own).astype(BF)
    (copy,) = fetch(sems, (out, out_far))
    copy.wait()


def pair_sum_body(scale, mine, out_part, got, message, send_far, send, flat, sems):
    core = Spot().core

    @pl.when(core == 0)
    def _():
        copies = []
        for k in range(GROUPS):
            total = mine[k].astype(F32) + got[k, 0:TAPS, :].astype(F32)
            for lg, half in enumerate(HALVES):
                send[k, lg] = total[:, half].astype(BF)
            if k % 8 == 7:
                part = slice(k - 7, k + 1)
                copies += fetch(sems.at[k // 8 : k // 8 + 1], (send.at[part], send_far.at[part]))
        for copy in copies:
            copy.wait()

    @pl.when(core == 1)
    def _():
        copies = []
        for a, g in out_grad(message.at[:, 0:WIDE], message.at[:, WIDE:], flat):
            for b in range(3):
                tap = (3 * a + b) * 8
                own = out_part[:, tap : tap + 8, :].astype(F32)
                total = g[b * CHANS : (b + 1) * CHANS].reshape(GROUPS, 8, CHANS) * scale + own
                for lg, half in enumerate(HALVES):
                    send[:, lg, tap : tap + 8, :] = total[:, :, half].astype(BF)
            part = slice(24 * a, 24 * a + 24)
            copies += fetch(sems.at[a : a + 1], (send.at[:, :, part], send_far.at[:, :, part]))
        for copy in copies:
            copy.wait()


def all_sum_body(got, small, send_far, send, sems):
    total = jnp.zeros((TAPS, 128), F32)
    for k in range(CHIPS):
        total = total + got[k].astype(F32)
    total = jnp.concatenate([total.astype(BF), small[...]], axis=0)
    send[...] = jnp.broadcast_to(total[None], send.shape)
    pairs = [(send, send_far.at[8 * k : 8 * k + 8]) for k in range(8)]
    for copy in fetch(sems, *pairs):
        copy.wait()


def write_grad(src, grad, stage, sems):
    copies = []
    for tap in range(9):
        a, b = tap // 3, tap % 3
        for lg, half in enumerate(HALVES):
            part = src[:, lg, tap * 8 : tap * 8 + 8, :].astype(F32)
            stage[a, b, :, half] = part.reshape(CHANS, 128)
        copies += fetch(sems.at[tap : tap + 1], (stage.at[a, b], grad.at[a, b]))
    return copies


def unpack_own_body(own, grad_out, grad_in, stage, sems):
    core = Spot().core

    @pl.when(core == 0)
    def _():
        for copy in write_grad(own, grad_in, stage, sems):
            copy.wait()

    @pl.when(core == 1)
    def _():
        for copy in write_grad(own, grad_out, stage, sems):
            copy.wait()


def unpack_other_body(
    own, got, out_half, in_half, grad_out, grad_in, rate, skip, step, stage, sems
):
    del out_half, in_half
    spot = Spot()

    def smalls():
        total = jnp.zeros((8, 128), F32)
        for k in range(GROUPS):
            for lg in range(2):
                pair = own[k, lg, TAPS:PACK, :].astype(F32) + got[k, lg, TAPS:PACK, :].astype(F32)
                total = total + pair
        rate[...] = total[0:2] + total[6:8]
        skip[...] = total[2:4]
        steps = total + pltpu.roll(total, 7, 0)
        step[...] = pltpu.roll(steps, (128 - spot.place * FRAMES) % 128, 1)[4:5, 0:FRAMES]

    @pl.when(spot.core == 0)
    def _():
        copies = write_grad(got, grad_out, stage, sems)
        smalls()
        for copy in copies:
            copy.wait()

    @pl.when(spot.core == 1)
    def _():
        copies = write_grad(got, grad_in, stage, sems)
        smalls()
        for copy in copies:
            copy.wait()


ROWS_AXES = ("z", "core")
TM_AXES = ("x", "y")
CORE_PAIRS = [(i, i ^ 1) for i in range(8)]
CHIP_PAIRS = [(i, (i + 1) % 8 if i % 2 else (i - 1) % 8) for i in range(8)]


def halos(to_core, to_chip):
    from_chip = lax.ppermute(to_chip, ROWS_AXES, CHIP_PAIRS)
    from_core = lax.ppermute(to_core, ROWS_AXES, CORE_PAIRS)
    return from_core, from_chip


def swap(chunks, axes):
    return lax.all_to_all(chunks, axes, 0, 0)


def vmem(shape, dtype=BF):
    return pltpu.VMEM(shape, dtype)


def sems(*shape):
    return pltpu.SemaphoreType.DMA(shape)


def on_device(inputs, in_weight, out_weight, skip_gain, rates, step_sizes, cotangent):
    scale = 1.0 / math.sqrt(32 * 32 * 128)
    step_scale = 1.0 / math.sqrt(1048576)
    core = lax.axis_index("core")
    field = (FRAMES, HEIGHT, WIDTH, CHANS)
    wide = (FRAMES, WIDE, WIDTH, CHANS)
    message = (FRAMES, WIDE + HEIGHT, WIDTH, CHANS)
    edge = (FRAMES, 2, WIDTH, CHANS)
    kernel = (3, 3, CHANS, CHANS)
    chunk = sds((BLOCKS, PLACES, CHANS), BF)
    packed = sds((GROUPS, 2, PACK, 128), BF)
    part = sds((GROUPS, TAPS, CHANS), BF)
    scales = (scale, step_scale)
    flat = sds((3 * CHANS, FRAMES * 4 * WIDTH), BF)
    params = jnp.concatenate([rates, skip_gain, jnp.pad(step_sizes, (0, CHANS - FRAMES))])
    params = params.reshape(3, CHANS)

    to_core = lax.dynamic_slice(inputs, (0, 2 - 2 * core, 0, 0), edge)
    to_chip = lax.dynamic_slice(inputs, (0, 2 * core, 0, 0), edge)
    from_core, from_chip = halos(to_core, to_chip)
    x, in_w, table, flat_mid = call(
        ready_body,
        [sds(field, BF), sds(kernel, BF), sds((8, CHANS), F32), flat],
        [far(inputs), far(in_weight), params],
        2 * ROW_FLOPS,
        [sems(2)],
    )
    local, send, flat_edge = call(
        drive_body,
        [sds(wide, F32), sds((BLOCKS, PLACES + NOTE, CHANS), BF), flat],
        [x, from_core, from_chip, in_w, table],
        WIDE * ROW_FLOPS,
        [vmem(edge), vmem(edge), vmem(field)],
    )
    got = swap(send, TM_AXES)
    send, block_decays = call(forward_scan_body, [chunk, sds((BLOCKS, CHANS), F32)], [got, table])
    carry = swap(send, TM_AXES)
    outputs, direct, sent, state_f, local_adj, send, skip = call(
        middle_body,
        [
            far(sds(field, BF)),
            far(sds(field, BF)),
            sds(message, BF),
            sds(wide[1:], F32),
            sds(wide, F32),
            chunk,
            sds((1, CHANS), F32),
        ],
        [local, carry, x, cotangent, out_weight, table],
        (HEIGHT + WIDE) * ROW_FLOPS,
        [vmem(field), vmem(field), sems(FRAMES, 2)],
    )
    got = swap(send, TM_AXES)
    (send,) = call(backward_scan_body, [chunk], [got, block_decays])
    incoming = swap(send, TM_AXES)
    sources = [local_adj, incoming, state_f, carry, table, skip, flat_mid, flat_edge]
    flat_sent = sent.reshape(GROUPS, PACK, CHANS)
    payload, out_part, odd_adj, odd_small = call(
        functools.partial(odd_grad_body, scales),
        [sds(flat_sent.shape, BF), part, sds(wide, BF), sds((8, 128), BF)],
        [*sources, sent, flat_sent],
        WIDE * ROW_FLOPS,
        [vmem((3 * CHANS, FRAMES * WIDE * WIDTH))],
    )
    got = lax.ppermute(payload, ROWS_AXES, CORE_PAIRS)
    mine, adj, to_core, to_chip, small = call(
        functools.partial(even_grad_body, scales),
        [part, sds(wide, BF), sds(edge, BF), sds(edge, BF), sds((8, 128), BF)],
        [*sources, odd_adj, odd_small],
        WIDE * ROW_FLOPS,
    )
    from_core, from_chip = halos(to_core, to_chip)
    (send,) = call(
        functools.partial(pair_sum_body, scale),
        [far(sds((GROUPS, 2, TAPS, 128), BF))],
        [mine, out_part, got, got.reshape(message)],
        HEIGHT * ROW_FLOPS,
        [
            vmem((GROUPS, 2, TAPS, 128)),
            vmem((3 * CHANS, FRAMES * WIDE * WIDTH)),
            sems(4),
        ],
    )
    got = swap(send.reshape(CHIPS, TAPS, 128), ("x", "y", "z"))
    (send,) = call(
        all_sum_body,
        [far(sds((CHIPS, PACK, 128), BF))],
        [got, small],
        0,
        [vmem((8, PACK, 128)), sems(8)],
    )
    send, from_core, from_chip = lax.optimization_barrier((send, from_core, from_chip))
    own = swap(send, ("x", "y", "z"))
    (grad_inputs,) = call(
        grad_inputs_body,
        [far(sds(field, BF))],
        [far(a) for a in (adj, from_core, from_chip, in_weight, direct)],
        HEIGHT * ROW_FLOPS,
        [
            vmem(wide),
            vmem(edge),
            vmem(edge),
            vmem(kernel),
            vmem(field),
            vmem(field),
            vmem(edge),
            vmem(edge),
            sems(5),
        ],
        {4: 0},
    )
    own, grad_inputs = lax.optimization_barrier((own, grad_inputs))
    own = own.reshape(packed.shape)
    other = lax.ppermute(own, ROWS_AXES, CORE_PAIRS)
    weights = sds(kernel, F32)
    half = sds((2, 128), F32)
    stage = vmem(kernel, F32)
    grad_out_weight, grad_in_weight = call(
        unpack_own_body, [far(weights), far(weights)], [own], 0, [stage, sems(9)]
    )
    grad_out_weight, grad_in_weight, grad_rates, grad_skip, grad_steps = call(
        unpack_other_body,
        [far(weights), far(weights), half, half, sds((1, FRAMES), F32)],
        [own, other, far(grad_out_weight), far(grad_in_weight)],
        0,
        [stage, sems(9)],
        {2: 0, 3: 1},
    )
    return (
        outputs,
        grad_inputs,
        grad_in_weight,
        grad_out_weight,
        grad_skip.reshape(CHANS),
        grad_rates.reshape(CHANS),
        grad_steps.reshape(FRAMES),
    )


def solution(mesh):
    fine = Mesh(mesh.devices.reshape(4, 4, 4, 2), ("x", "y", "z", "core"))
    spread_out = P(TM_AXES, ROWS_AXES, None, None)
    placed = (spread_out, P(), P(), P(), P(), P(TM_AXES), spread_out)
    return jax.shard_map(
        on_device,
        mesh=fine,
        in_specs=placed,
        out_specs=(spread_out, spread_out, P(), P(), P(), P(), P(TM_AXES)),
        check_vma=False,
    )
```

```python
import functools
import math

import jax
import jax.numpy as jnp
from jax import lax
from jax.experimental import pallas as pl
from jax.experimental.pallas import tpu as pltpu
from jax.sharding import Mesh, PartitionSpec as P

BF, F32 = jnp.bfloat16, jnp.float32
VM = pl.BlockSpec(memory_space=pltpu.VMEM)
HB = pl.BlockSpec(memory_space=pltpu.HBM)
GRANT = 24 << 20
FRAMES, HEIGHT, WIDTH, CHANS = 2, 4, 128, 256
WIDE, WIDER = HEIGHT + 2, HEIGHT + 4
BLOCKS = 16
PLACES = WIDE * WIDTH // BLOCKS
NOTE = 8
CHIPS = 64
GROUPS = 32
TAPS = 72
PACK = TAPS + 8


def sds(shape, dtype):
    return jax.ShapeDtypeStruct(shape, dtype)


def call(body, outs, ins, flops=0, scratch=(), aliases=None):
    ins = [i if isinstance(i, tuple) else (i, VM) for i in ins]
    outs = [o if isinstance(o, tuple) else (o, VM) for o in outs]
    nbytes = sum(math.prod(a.shape) * a.dtype.itemsize for a, _ in ins + outs)
    return pl.pallas_call(
        body,
        out_shape=[o for o, _ in outs],
        in_specs=[s for _, s in ins],
        out_specs=[s for _, s in outs],
        scratch_shapes=list(scratch),
        input_output_aliases=aliases or {},
        compiler_params=pltpu.CompilerParams(vmem_limit_bytes=GRANT),
        cost_estimate=pl.CostEstimate(flops=flops, bytes_accessed=nbytes, transcendentals=0),
    )(*[i for i, _ in ins])


def far(array):
    return array, HB


def fetch(sems, *pairs):
    copies = [pltpu.make_async_copy(s, d, sems.at[i]) for i, (s, d) in enumerate(pairs)]
    for copy in copies:
        copy.start()
    return copies


class Spot:
    def __init__(self):
        z = lax.axis_index("z")
        self.core = lax.axis_index("core")
        self.top = jnp.logical_and(z == 0, self.core == 0)
        self.bottom = jnp.logical_and(z == 3, self.core == 1)
        self.place = lax.axis_index("x") * 4 + lax.axis_index("y")


ROW_FLOPS = 2 * 9 * FRAMES * WIDTH * CHANS * CHANS


def col_shift(v, by):
    turned = pltpu.roll(v, by % WIDTH, 0)
    at = lax.broadcasted_iota(jnp.int32, v.shape, 0)
    return jnp.where(at == (0 if by == 1 else WIDTH - 1), 0.0, turned)


HALVES = [slice(0, 128), slice(128, 256)]


def conv(rows, weight, flipped):
    height = rows.shape[0] - 2
    lhs = jnp.concatenate([rows[a : a + height] for a in range(3)], axis=-1)
    lhs = lhs.reshape(height * WIDTH, 3 * CHANS)
    parts = []
    for b in range(3):
        if flipped:
            rhs = jnp.concatenate([weight[2 - a, 2 - b] for a in range(3)], axis=1)
            y = lax.dot_general(lhs, rhs, (((1,), (1,)), ((), ())), preferred_element_type=F32)
        else:
            rhs = jnp.concatenate([weight[a, b] for a in range(3)], axis=0)
            y = jnp.dot(lhs, rhs, preferred_element_type=F32)
        parts.append(y.reshape(height, WIDTH, CHANS))

    def block(h, half):
        left, mid, right = (part[h, :, half] for part in parts)
        return mid + col_shift(left, 1) + col_shift(right, -1)

    return block


def spread_conv(field, weight):
    pieces = []
    for first, count, taps in ((0, 1, (2,)), (1, 1, (1, 2)), (2, 2, (0, 1, 2)), (4, 1, (0, 1)), (5, 1, (0,))):
        lhs = jnp.concatenate(
            [field[:, first + a - 2 : first + a - 2 + count] for a in taps], axis=-1
        ).reshape(FRAMES * count * WIDTH, len(taps) * CHANS)
        parts = []
        for b in range(3):
            rhs = jnp.concatenate([weight[2 - a, 2 - b] for a in taps], axis=1)
            y = lax.dot_general(lhs, rhs, (((1,), (1,)), ((), ())), preferred_element_type=F32)
            parts.append(y.reshape(FRAMES, count, WIDTH, CHANS))
        pieces += [(parts, k) for k in range(count)]

    def block(t, h, half):
        parts, k = pieces[h]
        left, mid, right = (part[t, k, :, half] for part in parts)
        return mid + col_shift(left, 1) + col_shift(right, -1)

    return block


def blocks(height):
    return [(h, half) for h in range(height) for half in HALVES]


def outer(spot, h, v):
    if h == 0:
        return jnp.where(spot.top, 0.0, v)
    if h == WIDE - 1:
        return jnp.where(spot.bottom, 0.0, v)
    return v


def put_chunks(send, h, half, v):
    for k in range(WIDTH // 16):
        place = h * WIDTH + k * 16
        send[place // PLACES, place % PLACES : place % PLACES + 16, half] = v[
            k * 16 : (k + 1) * 16
        ].astype(BF)


def take_chunks(ref, h, half):
    pieces = []
    for k in range(WIDTH // 16):
        place = h * WIDTH + k * 16
        pieces.append(ref[place // PLACES, place % PLACES : place % PLACES + 16, half])
    return jnp.concatenate(pieces, axis=0).astype(F32)


def transpose_rows(v_ref, out_ref, rows, at_row):
    lane = lax.broadcasted_iota(jnp.int32, (CHANS, WIDTH), 1)
    for t in range(FRAMES):
        for h in range(rows):
            flat = v_ref[t, h].astype(F32).T
            at = pl.ds(at_row(t, h) * WIDTH, WIDTH)
            left = jnp.where(lane == 0, 0.0, pltpu.roll(flat, 1, 1))
            right = jnp.where(lane == WIDTH - 1, 0.0, pltpu.roll(flat, WIDTH - 1, 1))
            out_ref[0:CHANS, at] = left.astype(BF)
            out_ref[CHANS : 2 * CHANS, at] = flat.astype(BF)
            out_ref[2 * CHANS : 3 * CHANS, at] = right.astype(BF)


def ready_body(x_far, in_far, params, x, in_weight, table, flat_mid, sems):
    copies = fetch(sems, (x_far, x), (in_far, in_weight))
    r = params[0:1, :]
    s0 = jnp.broadcast_to(params[2:3, 0:1], (1, CHANS))
    s1 = jnp.broadcast_to(params[2:3, 1:2], (1, CHANS))
    lines = [jnp.exp(-r * s0), jnp.exp(-r * s1), s0, s1, r, params[1:2, :], s0 + s1, r]
    for k, line in enumerate(lines):
        table[k : k + 1, :] = line
    copies[0].wait()
    transpose_rows(x, flat_mid, HEIGHT, lambda t, h: t * HEIGHT + h)
    copies[1].wait()


def place_halos(spot, from_core, from_chip, above, below):
    @pl.when(spot.core == 0)
    def _():
        above[...] = from_chip[...]
        below[...] = from_core[...]

    @pl.when(spot.core == 1)
    def _():
        above[...] = from_core[...]
        below[...] = from_chip[...]

    @pl.when(spot.top)
    def _():
        above[...] = jnp.zeros_like(above)

    @pl.when(spot.bottom)
    def _():
        below[...] = jnp.zeros_like(below)


def drive_body(
    x, from_core, from_chip, weight, table, local, send, edges, above, below
):
    spot = Spot()
    place_halos(spot, from_core, from_chip, above, below)
    for t in range(FRAMES):
        rows = jnp.concatenate([above[t], x[t], below[t]], axis=0)
        drive = conv(rows, weight, False)
        for h, half in blocks(WIDE):
            v = outer(spot, h, drive(h, half))
            if t == 1:
                v = table[1:2, half] * local[0, h, :, half] + v
                put_chunks(send, h, half, v)
            local[t, h, :, half] = v
    total = jnp.broadcast_to(table[6:7, :][None], (BLOCKS, NOTE, CHANS))
    row = lax.broadcasted_iota(jnp.int32, total.shape, 1)
    one = total.astype(BF).astype(F32)
    two = (total - one).astype(BF).astype(F32)
    three = total - one - two
    send[:, PLACES : PLACES + NOTE, :] = jnp.where(
        row == 0, one, jnp.where(row == 1, two, jnp.where(row == 2, three, 0.0))
    ).astype(BF)
    edges[:, 0:2] = above[...]
    edges[:, 2:4] = below[...]


def forward_scan_body(got, table, send, block_decays):
    carry = jnp.zeros((PLACES, CHANS), F32)
    for k in range(BLOCKS):
        send[k] = carry.astype(BF)
        span = jnp.sum(got[k, PLACES : PLACES + NOTE, :].astype(F32), axis=0, keepdims=True)
        d = jnp.exp(-table[4:5, :] * span)
        block_decays[pl.ds(k, 1), :] = d
        carry = d * carry + got[k, 0:PLACES, :].astype(F32)


def backward_scan_body(got, block_decays, send):
    carry = jnp.zeros((PLACES, CHANS), F32)
    for k in reversed(range(BLOCKS)):
        send[k] = carry.astype(BF)
        carry = block_decays[pl.ds(k, 1), :] * carry + got[k].astype(F32)


GELU_A = math.sqrt(2 / math.pi)


def small_rows(rate, skip, steps):
    row = lax.broadcasted_iota(jnp.int32, (8, 128), 0)
    halves = [v[:, half] for v in (rate, skip) for half in HALVES]
    lines = halves + [steps, steps] + halves[0:2]
    out = jnp.zeros((8, 128), F32)
    for k, line in enumerate(lines):
        out = jnp.where(row == k, jnp.broadcast_to(line, (8, 128)), out)
    top = out.astype(BF).astype(F32)
    return jnp.where(row < 5, top, out - top).astype(BF)


def middle_body(
    local, carry, x, cot, weight, table,
    out_far, direct_far, message, state_f, local_adj, send, skip, out, direct, sems,
):
    spot = Spot()
    state, gz = message.at[:, 0:WIDE], message.at[:, WIDE:]
    d0, d1 = table[0:1, :], table[1:2, :]
    for h, half in blocks(WIDE):
        c = take_chunks(carry, h, half)
        s0 = local[0, h, :, half] + d0[:, half] * c
        state_f[h, :, half] = s0
        state[0, h, :, half] = s0.astype(BF)
        s1 = local[1, h, :, half] + (d0 * d1)[:, half] * c
        state[1, h, :, half] = s1.astype(BF)
    totals = [jnp.zeros((8, 128), F32) for _ in HALVES]
    for t in (1, 0):
        pre_act = conv(state[t], weight, False)
        for h, half in blocks(HEIGHT):
            xt = x[t, h, :, half].astype(F32)
            z = pre_act(h, half) + table[5:6, half] * xt
            zz = z * z
            th = jnp.tanh(GELU_A * (z + 0.044715 * (zz * z)))
            gate = 0.5 * (1.0 + th)
            out[t, h, :, half] = (z * gate).astype(BF)
            slope = gate + 0.5 * z * (1.0 - th * th) * (GELU_A * (1.0 + 3 * 0.044715 * zz))
            g = cot[t, h, :, half].astype(F32) * slope
            gz[t, h, :, half] = g.astype(BF)
            direct[t, h, :, half] = (table[5:6, half] * g).astype(BF)
            k = HALVES.index(half)
            totals[k] = totals[k] + jnp.sum((g * xt).reshape(WIDTH // 8, 8, 128), axis=0)
    copies = fetch(sems, (out, out_far), (direct, direct_far))
    grad = spread_conv(gz, weight)
    for t in (1, 0):
        for h, half in blocks(WIDE):
            v = outer(spot, h, grad(t, h, half))
            if t == 0:
                v = v + d1[:, half] * local_adj[1, h, :, half]
                put_chunks(send, h, half, d0[:, half] * v)
            local_adj[t, h, :, half] = v
    total = jnp.concatenate([jnp.sum(v, axis=0, keepdims=True) for v in totals], axis=1)
    skip[...] = total
    for copy in copies:
        copy.wait()


def pack_grad(g, a, scale, out):
    for b in range(3):
        tap = (3 * a + b) * 8
        part = (g[b * CHANS : (b + 1) * CHANS] * scale).astype(BF)
        out[:, tap : tap + 8, :] = part.reshape(GROUPS, 8, CHANS)


def out_grad(state, gz, flat):
    transpose_rows(state, flat, WIDE, lambda t, h: t * WIDE + h)
    rhs = gz[...].reshape(FRAMES * HEIGHT * WIDTH, CHANS)
    for a in range(3):
        lhs = jnp.concatenate(
            [flat[:, pl.ds((t * WIDE + a) * WIDTH, HEIGHT * WIDTH)] for t in range(FRAMES)], axis=1
        )
        yield a, jnp.dot(lhs, rhs, preferred_element_type=F32)


def in_grad(adj, flat_mid, edges, flat_edge):
    transpose_rows(edges, flat_edge, 4, lambda t, h: t * 4 + h)
    rhs = adj[...].reshape(FRAMES * WIDE * WIDTH, CHANS)
    for a in range(3):
        pieces = []
        for t in range(FRAMES):
            at = t * 4 * WIDTH
            if a < 2:
                pieces.append(flat_edge[:, at + a * WIDTH : at + 2 * WIDTH])
            pieces.append(flat_mid[:, at : at + 4 * WIDTH])
            if a > 0:
                pieces.append(flat_edge[:, at + 2 * WIDTH : at + (2 + a) * WIDTH])
        yield a, jnp.dot(jnp.concatenate(pieces, axis=1), rhs, preferred_element_type=F32)


def adjoint_stage(scales, spot, sources, adj, small):
    local, incoming, state_f, carry, table, skip = sources
    d0, d1 = table[0:1, :], table[1:2, :]
    sums = [[jnp.zeros((8, 128), F32) for _ in HALVES] for _ in range(FRAMES)]
    for h, half in blocks(WIDE):
        c = take_chunks(incoming, h, half)
        a0 = local[0, h, :, half] + d1[:, half] * c
        a1 = local[1, h, :, half] + c
        adj[0, h, :, half] = a0.astype(BF)
        adj[1, h, :, half] = a1.astype(BF)
        k = HALVES.index(half)
        pairs = ((a0, take_chunks(carry, h, half)), (a1, state_f[h, :, half]))
        for t, (a, earlier) in enumerate(pairs):
            sums[t][k] = sums[t][k] + jnp.sum((a * earlier).reshape(WIDTH // 8, 8, 128), axis=0)
    k0, k1 = (
        jnp.concatenate([jnp.sum(v, axis=0, keepdims=True) for v in pair], axis=1) * d
        for pair, d in zip(sums, (d0, d1))
    )
    rate = (k0 * table[2:3, :] + k1 * table[3:4, :]) * (-scales[0])
    s0 = jnp.sum(k0 * table[4:5, :], axis=1, keepdims=True) * (-scales[1])
    s1 = jnp.sum(k1 * table[4:5, :], axis=1, keepdims=True) * (-scales[1])
    lane = lax.broadcasted_iota(jnp.int32, (1, 128), 1)
    at = spot.place * FRAMES
    steps = jnp.where(lane == at, s0, jnp.where(lane == at + 1, s1, 0.0))
    small[...] = small_rows(rate, skip[...] * scales[0], steps)


def odd_grad_body(
    scales, local, incoming, state_f, carry, table, skip, flat_mid, edges, message, flat_message,
    payload, out_part, adj, small, flat, flat_edge,
):
    spot = Spot()

    @pl.when(spot.core == 0)
    def _():
        payload[...] = flat_message[...]

    @pl.when(spot.core == 1)
    def _():
        adjoint_stage(scales, spot, (local, incoming, state_f, carry, table, skip), adj, small)
        for a, g in in_grad(adj, flat_mid, edges, flat_edge):
            pack_grad(g, a, scales[0], payload)
        for a, g in out_grad(message.at[:, 0:WIDE], message.at[:, WIDE:], flat):
            pack_grad(g, a, scales[0], out_part)


def even_grad_body(
    scales, local, incoming, state_f, carry, table, skip, flat_mid, edges, odd_adj, odd_small,
    mine, adj, to_core, to_chip, small, flat_edge,
):
    spot = Spot()

    @pl.when(spot.core == 0)
    def _():
        adjoint_stage(scales, spot, (local, incoming, state_f, carry, table, skip), adj, small)
        to_chip[...] = adj[:, 0:2]
        to_core[...] = adj[:, WIDE - 2 :]
        for a, g in in_grad(adj, flat_mid, edges, flat_edge):
            pack_grad(g, a, scales[0], mine)

    @pl.when(spot.core == 1)
    def _():
        adj[...] = odd_adj[...]
        small[...] = odd_small[...]
        to_core[...] = odd_adj[:, 0:2]
        to_chip[...] = odd_adj[:, WIDE - 2 :]


def grad_inputs_body(
    adj_far, core_far, chip_far, weight_far, direct_far,
    out_far, adj, from_core, from_chip, weight, direct, out, above, below, sems,
):
    spot = Spot()
    copies = fetch(
        sems,
        (core_far, from_core),
        (chip_far, from_chip),
        (adj_far, adj),
        (weight_far, weight),
        (direct_far, direct),
    )
    for copy in copies:
        copy.wait()
    place_halos(spot, from_core, from_chip, above, below)
    for t in range(FRAMES):
        up = (adj[t, 0:2].astype(F32) + above[t].astype(F32)).astype(BF)
        down = (adj[t, WIDE - 2 :].astype(F32) + below[t].astype(F32)).astype(BF)
        rows = jnp.concatenate([up, adj[t, 2 : WIDE - 2], down], axis=0)
        grad = conv(rows, weight, True)
        for h, half in blocks(HEIGHT):
            own = direct[t, h, :, half].astype(F32)
            out[t, h, :, half] = (grad(h, half) + own).astype(BF)
    (copy,) = fetch(sems, (out, out_far))
    copy.wait()


def pair_sum_body(scale, mine, out_part, got, message, send_far, send, flat, sems):
    core = Spot().core

    @pl.when(core == 0)
    def _():
        copies = []
        for k in range(GROUPS):
            total = mine[k].astype(F32) + got[k, 0:TAPS, :].astype(F32)
            for lg, half in enumerate(HALVES):
                send[k, lg] = total[:, half].astype(BF)
            if k % 8 == 7:
                part = slice(k - 7, k + 1)
                copies += fetch(sems.at[k // 8 : k // 8 + 1], (send.at[part], send_far.at[part]))
        for copy in copies:
            copy.wait()

    @pl.when(core == 1)
    def _():
        copies = []
        for a, g in out_grad(message.at[:, 0:WIDE], message.at[:, WIDE:], flat):
            for b in range(3):
                tap = (3 * a + b) * 8
                own = out_part[:, tap : tap + 8, :].astype(F32)
                total = g[b * CHANS : (b + 1) * CHANS].reshape(GROUPS, 8, CHANS) * scale + own
                for lg, half in enumerate(HALVES):
                    send[:, lg, tap : tap + 8, :] = total[:, :, half].astype(BF)
            part = slice(24 * a, 24 * a + 24)
            copies += fetch(sems.at[a : a + 1], (send.at[:, :, part], send_far.at[:, :, part]))
        for copy in copies:
            copy.wait()


def all_sum_body(got, small, send_far, send, sems):
    total = jnp.zeros((TAPS, 128), F32)
    for k in range(CHIPS):
        total = total + got[k].astype(F32)
    total = jnp.concatenate([total.astype(BF), small[...]], axis=0)
    send[...] = jnp.broadcast_to(total[None], send.shape)
    pairs = [(send, send_far.at[8 * k : 8 * k + 8]) for k in range(8)]
    for copy in fetch(sems, *pairs):
        copy.wait()


def write_grad(src, grad, stage, sems):
    copies = []
    for tap in range(9):
        a, b = tap // 3, tap % 3
        for lg, half in enumerate(HALVES):
            part = src[:, lg, tap * 8 : tap * 8 + 8, :].astype(F32)
            stage[a, b, :, half] = part.reshape(CHANS, 128)
        copies += fetch(sems.at[tap : tap + 1], (stage.at[a, b], grad.at[a, b]))
    return copies


def unpack_own_body(own, grad_out, grad_in, stage, sems):
    core = Spot().core

    @pl.when(core == 0)
    def _():
        for copy in write_grad(own, grad_in, stage, sems):
            copy.wait()

    @pl.when(core == 1)
    def _():
        for copy in write_grad(own, grad_out, stage, sems):
            copy.wait()


def unpack_other_body(
    own, got, out_half, in_half, grad_out, grad_in, rate_far, skip_far, step_far,
    stage, rate, skip, step, sems,
):
    del out_half, in_half
    spot = Spot()
    total = jnp.zeros((8, 128), F32)
    for k in range(GROUPS):
        for lg in range(2):
            pair = own[k, lg, TAPS:PACK, :].astype(F32) + got[k, lg, TAPS:PACK, :].astype(F32)
            total = total + pair
    rate[...] = total[0:2] + total[6:8]
    skip[...] = total[2:4]
    steps = total + pltpu.roll(total, 7, 0)
    step[...] = pltpu.roll(steps, (128 - spot.place * FRAMES) % 128, 1)[4:5, 0:FRAMES]
    smalls = fetch(sems.at[9:12], (rate, rate_far), (skip, skip_far), (step, step_far))

    @pl.when(spot.core == 0)
    def _():
        for copy in write_grad(got, grad_out, stage, sems):
            copy.wait()

    @pl.when(spot.core == 1)
    def _():
        for copy in write_grad(got, grad_in, stage, sems):
            copy.wait()

    for copy in smalls:
        copy.wait()


ROWS_AXES = ("z", "core")
TM_AXES = ("x", "y")
CORE_PAIRS = [(i, i ^ 1) for i in range(8)]
CHIP_PAIRS = [(i, (i + 1) % 8 if i % 2 else (i - 1) % 8) for i in range(8)]


def halos(to_core, to_chip):
    from_chip = lax.ppermute(to_chip, ROWS_AXES, CHIP_PAIRS)
    from_core = lax.ppermute(to_core, ROWS_AXES, CORE_PAIRS)
    return from_core, from_chip


def swap(chunks, axes):
    return lax.all_to_all(chunks, axes, 0, 0)


def vmem(shape, dtype=BF):
    return pltpu.VMEM(shape, dtype)


def sems(*shape):
    return pltpu.SemaphoreType.DMA(shape)


def on_device(inputs, in_weight, out_weight, skip_gain, rates, step_sizes, cotangent):
    scale = 1.0 / math.sqrt(32 * 32 * 128)
    step_scale = 1.0 / math.sqrt(1048576)
    core = lax.axis_index("core")
    field = (FRAMES, HEIGHT, WIDTH, CHANS)
    wide = (FRAMES, WIDE, WIDTH, CHANS)
    message = (FRAMES, WIDE + HEIGHT, WIDTH, CHANS)
    edge = (FRAMES, 2, WIDTH, CHANS)
    kernel = (3, 3, CHANS, CHANS)
    chunk = sds((BLOCKS, PLACES, CHANS), BF)
    packed = sds((GROUPS, 2, PACK, 128), BF)
    part = sds((GROUPS, TAPS, CHANS), BF)
    scales = (scale, step_scale)
    flat = sds((3 * CHANS, FRAMES * 4 * WIDTH), BF)
    params = jnp.concatenate([rates, skip_gain, jnp.pad(step_sizes, (0, CHANS - FRAMES))])
    params = params.reshape(3, CHANS)

    to_core = lax.dynamic_slice(inputs, (0, 2 - 2 * core, 0, 0), edge)
    to_chip = lax.dynamic_slice(inputs, (0, 2 * core, 0, 0), edge)
    from_core, from_chip = halos(to_core, to_chip)
    x, in_w, table, flat_mid = call(
        ready_body,
        [sds(field, BF), sds(kernel, BF), sds((8, CHANS), F32), flat],
        [far(inputs), far(in_weight), params],
        2 * ROW_FLOPS,
        [sems(2)],
    )
    local, send, edges = call(
        drive_body,
        [sds(wide, F32), sds((BLOCKS, PLACES + NOTE, CHANS), BF), sds(field, BF)],
        [x, from_core, from_chip, in_w, table],
        WIDE * ROW_FLOPS,
        [vmem(edge), vmem(edge)],
    )
    got = swap(send, TM_AXES)
    send, block_decays = call(forward_scan_body, [chunk, sds((BLOCKS, CHANS), F32)], [got, table])
    carry = swap(send, TM_AXES)
    outputs, direct, sent, state_f, local_adj, send, skip = call(
        middle_body,
        [
            far(sds(field, BF)),
            far(sds(field, BF)),
            sds(message, BF),
            sds(wide[1:], F32),
            sds(wide, F32),
            chunk,
            sds((1, CHANS), F32),
        ],
        [local, carry, x, cotangent, out_weight, table],
        (HEIGHT + WIDE) * ROW_FLOPS,
        [vmem(field), vmem(field), sems(2)],
    )
    got = swap(send, TM_AXES)
    (send,) = call(backward_scan_body, [chunk], [got, block_decays])
    incoming = swap(send, TM_AXES)
    sources = [local_adj, incoming, state_f, carry, table, skip, flat_mid, edges]
    flat_sent = sent.reshape(GROUPS, PACK, CHANS)
    payload, out_part, odd_adj, odd_small = call(
        functools.partial(odd_grad_body, scales),
        [sds(flat_sent.shape, BF), part, sds(wide, BF), sds((8, 128), BF)],
        [*sources, sent, flat_sent],
        WIDE * ROW_FLOPS,
        [vmem((3 * CHANS, FRAMES * WIDE * WIDTH)), vmem(flat.shape)],
    )
    got = lax.ppermute(payload, ROWS_AXES, CORE_PAIRS)
    mine, adj, to_core, to_chip, small = call(
        functools.partial(even_grad_body, scales),
        [part, sds(wide, BF), sds(edge, BF), sds(edge, BF), sds((8, 128), BF)],
        [*sources, odd_adj, odd_small],
        WIDE * ROW_FLOPS,
        [vmem(flat.shape)],
    )
    from_core, from_chip = halos(to_core, to_chip)
    (send,) = call(
        functools.partial(pair_sum_body, scale),
        [far(sds((GROUPS, 2, TAPS, 128), BF))],
        [mine, out_part, got, got.reshape(message)],
        HEIGHT * ROW_FLOPS,
        [
            vmem((GROUPS, 2, TAPS, 128)),
            vmem((3 * CHANS, FRAMES * WIDE * WIDTH)),
            sems(4),
        ],
    )
    got = swap(send.reshape(CHIPS, TAPS, 128), ("x", "y", "z"))
    (send,) = call(
        all_sum_body,
        [far(sds((CHIPS, PACK, 128), BF))],
        [got, small],
        0,
        [vmem((8, PACK, 128)), sems(8)],
    )
    send, from_core, from_chip = lax.optimization_barrier((send, from_core, from_chip))
    own = swap(send, ("x", "y", "z"))
    (grad_inputs,) = call(
        grad_inputs_body,
        [far(sds(field, BF))],
        [far(a) for a in (adj, from_core, from_chip, in_weight, direct)],
        HEIGHT * ROW_FLOPS,
        [
            vmem(wide),
            vmem(edge),
            vmem(edge),
            vmem(kernel),
            vmem(field),
            vmem(field),
            vmem(edge),
            vmem(edge),
            sems(5),
        ],
        {4: 0},
    )
    own, grad_inputs = lax.optimization_barrier((own, grad_inputs))
    own = own.reshape(packed.shape)
    other = lax.ppermute(own, ROWS_AXES, CORE_PAIRS)
    weights = sds(kernel, F32)
    half = sds((2, 128), F32)
    stage = vmem(kernel, F32)
    grad_out_weight, grad_in_weight = call(
        unpack_own_body, [far(weights), far(weights)], [own], 0, [stage, sems(9)]
    )
    grad_out_weight, grad_in_weight, grad_rates, grad_skip, grad_steps = call(
        unpack_other_body,
        [far(a) for a in (weights, weights, half, half, sds((1, FRAMES), F32))],
        [own, other, far(grad_out_weight), far(grad_in_weight)],
        0,
        [stage, vmem((2, 128), F32), vmem((2, 128), F32), vmem((1, FRAMES), F32), sems(12)],
        {2: 0, 3: 1},
    )
    return (
        outputs,
        grad_inputs,
        grad_in_weight,
        grad_out_weight,
        grad_skip.reshape(CHANS),
        grad_rates.reshape(CHANS),
        grad_steps.reshape(FRAMES),
    )


def solution(mesh):
    fine = Mesh(mesh.devices.reshape(4, 4, 4, 2), ("x", "y", "z", "core"))
    spread_out = P(TM_AXES, ROWS_AXES, None, None)
    placed = (spread_out, P(), P(), P(), P(), P(TM_AXES), spread_out)
    return jax.shard_map(
        on_device,
        mesh=fine,
        in_specs=placed,
        out_specs=(spread_out, spread_out, P(), P(), P(), P(), P(TM_AXES)),
        check_vma=False,
    )
```

```python
import functools
import math

import jax
import jax.numpy as jnp
from jax import lax
from jax.experimental import pallas as pl
from jax.experimental.pallas import tpu as pltpu
from jax.sharding import Mesh, PartitionSpec as P

BF, F32 = jnp.bfloat16, jnp.float32
VM = pl.BlockSpec(memory_space=pltpu.VMEM)
HB = pl.BlockSpec(memory_space=pltpu.HBM)
GRANT = 24 << 20
FRAMES, HEIGHT, WIDTH, CHANS = 2, 4, 128, 256
WIDE, WIDER = HEIGHT + 2, HEIGHT + 4
BLOCKS = 16
PLACES = WIDE * WIDTH // BLOCKS
NOTE = 8
CHIPS = 64
GROUPS = 32
TAPS = 72
PACK = TAPS + 8


def sds(shape, dtype):
    return jax.ShapeDtypeStruct(shape, dtype)


def call(body, outs, ins, flops=0, scratch=(), aliases=None, light=False):
    ins = [i if isinstance(i, tuple) else (i, VM) for i in ins]
    outs = [o if isinstance(o, tuple) else (o, VM) for o in outs]
    nbytes = sum(math.prod(a.shape) * a.dtype.itemsize for a, _ in ins + outs)
    return pl.pallas_call(
        body,
        out_shape=[o for o, _ in outs],
        in_specs=[s for _, s in ins],
        out_specs=[s for _, s in outs],
        scratch_shapes=list(scratch),
        input_output_aliases=aliases or {},
        compiler_params=pltpu.CompilerParams(vmem_limit_bytes=GRANT),
        cost_estimate=pl.CostEstimate(flops=flops, bytes_accessed=0 if light else nbytes, transcendentals=0),
    )(*[i for i, _ in ins])


def far(array):
    return array, HB


def fetch(sems, *pairs):
    copies = [pltpu.make_async_copy(s, d, sems.at[i]) for i, (s, d) in enumerate(pairs)]
    for copy in copies:
        copy.start()
    return copies


class Spot:
    def __init__(self):
        z = lax.axis_index("z")
        self.core = lax.axis_index("core")
        self.top = jnp.logical_and(z == 0, self.core == 0)
        self.bottom = jnp.logical_and(z == 3, self.core == 1)
        self.place = lax.axis_index("x") * 4 + lax.axis_index("y")


ROW_FLOPS = 2 * 9 * FRAMES * WIDTH * CHANS * CHANS


def col_shift(v, by):
    turned = pltpu.roll(v, by % WIDTH, 0)
    at = lax.broadcasted_iota(jnp.int32, v.shape, 0)
    return jnp.where(at == (0 if by == 1 else WIDTH - 1), 0.0, turned)


HALVES = [slice(0, 128), slice(128, 256)]


def conv(rows, weight, flipped):
    height = rows.shape[0] - 2
    lhs = jnp.concatenate([rows[a : a + height] for a in range(3)], axis=-1)
    lhs = lhs.reshape(height * WIDTH, 3 * CHANS)
    parts = []
    for b in range(3):
        if flipped:
            rhs = jnp.concatenate([weight[2 - a, 2 - b] for a in range(3)], axis=1)
            y = lax.dot_general(lhs, rhs, (((1,), (1,)), ((), ())), preferred_element_type=F32)
        else:
            rhs = jnp.concatenate([weight[a, b] for a in range(3)], axis=0)
            y = jnp.dot(lhs, rhs, preferred_element_type=F32)
        parts.append(y.reshape(height, WIDTH, CHANS))

    def block(h, half):
        left, mid, right = (part[h, :, half] for part in parts)
        return mid + col_shift(left, 1) + col_shift(right, -1)

    return block


def spread_conv(field, weight):
    pieces = []
    for first, count, taps in ((0, 1, (2,)), (1, 1, (1, 2)), (2, 2, (0, 1, 2)), (4, 1, (0, 1)), (5, 1, (0,))):
        lhs = jnp.concatenate(
            [field[:, first + a - 2 : first + a - 2 + count] for a in taps], axis=-1
        ).reshape(FRAMES * count * WIDTH, len(taps) * CHANS)
        parts = []
        for b in range(3):
            rhs = jnp.concatenate([weight[2 - a, 2 - b] for a in taps], axis=1)
            y = lax.dot_general(lhs, rhs, (((1,), (1,)), ((), ())), preferred_element_type=F32)
            parts.append(y.reshape(FRAMES, count, WIDTH, CHANS))
        pieces += [(parts, k) for k in range(count)]

    def block(t, h, half):
        parts, k = pieces[h]
        left, mid, right = (part[t, k, :, half] for part in parts)
        return mid + col_shift(left, 1) + col_shift(right, -1)

    return block


def blocks(height):
    return [(h, half) for h in range(height) for half in HALVES]


def outer(spot, h, v):
    if h == 0:
        return jnp.where(spot.top, 0.0, v)
    if h == WIDE - 1:
        return jnp.where(spot.bottom, 0.0, v)
    return v


def put_chunks(send, h, half, v):
    for k in range(WIDTH // 16):
        place = h * WIDTH + k * 16
        send[place // PLACES, place % PLACES : place % PLACES + 16, half] = v[
            k * 16 : (k + 1) * 16
        ].astype(BF)


def take_chunks(ref, h, half):
    pieces = []
    for k in range(WIDTH // 16):
        place = h * WIDTH + k * 16
        pieces.append(ref[place // PLACES, place % PLACES : place % PLACES + 16, half])
    return jnp.concatenate(pieces, axis=0).astype(F32)


def transpose_rows(v_ref, out_ref, rows, at_row):
    lane = lax.broadcasted_iota(jnp.int32, (CHANS, WIDTH), 1)
    for t in range(FRAMES):
        for h in range(rows):
            flat = v_ref[t, h].astype(F32).T
            at = pl.ds(at_row(t, h) * WIDTH, WIDTH)
            left = jnp.where(lane == 0, 0.0, pltpu.roll(flat, 1, 1))
            right = jnp.where(lane == WIDTH - 1, 0.0, pltpu.roll(flat, WIDTH - 1, 1))
            out_ref[0:CHANS, at] = left.astype(BF)
            out_ref[CHANS : 2 * CHANS, at] = flat.astype(BF)
            out_ref[2 * CHANS : 3 * CHANS, at] = right.astype(BF)


def ready_body(x_far, in_far, params, x, in_weight, table, flat_mid, sems):
    copies = fetch(sems, (x_far, x), (in_far, in_weight))
    r = params[0:1, :]
    s0 = jnp.broadcast_to(params[2:3, 0:1], (1, CHANS))
    s1 = jnp.broadcast_to(params[2:3, 1:2], (1, CHANS))
    lines = [jnp.exp(-r * s0), jnp.exp(-r * s1), s0, s1, r, params[1:2, :], s0 + s1, r]
    for k, line in enumerate(lines):
        table[k : k + 1, :] = line
    copies[0].wait()
    transpose_rows(x, flat_mid, HEIGHT, lambda t, h: t * HEIGHT + h)
    copies[1].wait()


def place_halos(spot, from_core, from_chip, above, below):
    @pl.when(spot.core == 0)
    def _():
        above[...] = from_chip[...]
        below[...] = from_core[...]

    @pl.when(spot.core == 1)
    def _():
        above[...] = from_core[...]
        below[...] = from_chip[...]

    @pl.when(spot.top)
    def _():
        above[...] = jnp.zeros_like(above)

    @pl.when(spot.bottom)
    def _():
        below[...] = jnp.zeros_like(below)


def drive_body(
    x, from_core, from_chip, weight, table, local, send, edges, above, below
):
    spot = Spot()
    place_halos(spot, from_core, from_chip, above, below)
    for t in range(FRAMES):
        rows = jnp.concatenate([above[t], x[t], below[t]], axis=0)
        drive = conv(rows, weight, False)
        for h, half in blocks(WIDE):
            v = outer(spot, h, drive(h, half))
            if t == 1:
                v = table[1:2, half] * local[0, h, :, half] + v
                put_chunks(send, h, half, v)
            local[t, h, :, half] = v
    total = jnp.broadcast_to(table[6:7, :][None], (BLOCKS, NOTE, CHANS))
    row = lax.broadcasted_iota(jnp.int32, total.shape, 1)
    one = total.astype(BF).astype(F32)
    two = (total - one).astype(BF).astype(F32)
    three = total - one - two
    send[:, PLACES : PLACES + NOTE, :] = jnp.where(
        row == 0, one, jnp.where(row == 1, two, jnp.where(row == 2, three, 0.0))
    ).astype(BF)
    edges[:, 0:2] = above[...]
    edges[:, 2:4] = below[...]


def forward_scan_body(got, table, send, block_decays):
    carry = jnp.zeros((PLACES, CHANS), F32)
    for k in range(BLOCKS):
        send[k] = carry.astype(BF)
        span = jnp.sum(got[k, PLACES : PLACES + NOTE, :].astype(F32), axis=0, keepdims=True)
        d = jnp.exp(-table[4:5, :] * span)
        block_decays[pl.ds(k, 1), :] = d
        carry = d * carry + got[k, 0:PLACES, :].astype(F32)


def backward_scan_body(got, block_decays, send):
    carry = jnp.zeros((PLACES, CHANS), F32)
    for k in reversed(range(BLOCKS)):
        send[k] = carry.astype(BF)
        carry = block_decays[pl.ds(k, 1), :] * carry + got[k].astype(F32)


GELU_A = math.sqrt(2 / math.pi)


def small_rows(rate, skip, steps):
    row = lax.broadcasted_iota(jnp.int32, (8, 128), 0)
    halves = [v[:, half] for v in (rate, skip) for half in HALVES]
    lines = halves + [steps, steps] + halves[0:2]
    out = jnp.zeros((8, 128), F32)
    for k, line in enumerate(lines):
        out = jnp.where(row == k, jnp.broadcast_to(line, (8, 128)), out)
    top = out.astype(BF).astype(F32)
    return jnp.where(row < 5, top, out - top).astype(BF)


def middle_body(
    local, carry, x, cot, weight, table,
    out_far, direct_far, message, state_f, local_adj, send, skip, out, direct, sems,
):
    spot = Spot()
    state, gz = message.at[:, 0:WIDE], message.at[:, WIDE:]
    d0, d1 = table[0:1, :], table[1:2, :]
    for h, half in blocks(WIDE):
        c = take_chunks(carry, h, half)
        s0 = local[0, h, :, half] + d0[:, half] * c
        state_f[h, :, half] = s0
        state[0, h, :, half] = s0.astype(BF)
        s1 = local[1, h, :, half] + (d0 * d1)[:, half] * c
        state[1, h, :, half] = s1.astype(BF)
    totals = [jnp.zeros((8, 128), F32) for _ in HALVES]
    for t in (1, 0):
        pre_act = conv(state[t], weight, False)
        for h, half in blocks(HEIGHT):
            xt = x[t, h, :, half].astype(F32)
            z = pre_act(h, half) + table[5:6, half] * xt
            zz = z * z
            th = jnp.tanh(GELU_A * (z + 0.044715 * (zz * z)))
            gate = 0.5 * (1.0 + th)
            out[t, h, :, half] = (z * gate).astype(BF)
            slope = gate + 0.5 * z * (1.0 - th * th) * (GELU_A * (1.0 + 3 * 0.044715 * zz))
            g = cot[t, h, :, half].astype(F32) * slope
            gz[t, h, :, half] = g.astype(BF)
            direct[t, h, :, half] = (table[5:6, half] * g).astype(BF)
            k = HALVES.index(half)
            totals[k] = totals[k] + jnp.sum((g * xt).reshape(WIDTH // 8, 8, 128), axis=0)
    copies = fetch(sems, (out, out_far), (direct, direct_far))
    grad = spread_conv(gz, weight)
    for t in (1, 0):
        for h, half in blocks(WIDE):
            v = outer(spot, h, grad(t, h, half))
            if t == 0:
                v = v + d1[:, half] * local_adj[1, h, :, half]
                put_chunks(send, h, half, d0[:, half] * v)
            local_adj[t, h, :, half] = v
    total = jnp.concatenate([jnp.sum(v, axis=0, keepdims=True) for v in totals], axis=1)
    skip[...] = total
    for copy in copies:
        copy.wait()


def pack_grad(g, a, scale, out):
    for b in range(3):
        tap = (3 * a + b) * 8
        part = (g[b * CHANS : (b + 1) * CHANS] * scale).astype(BF)
        out[:, tap : tap + 8, :] = part.reshape(GROUPS, 8, CHANS)


def out_grad(state, gz, flat):
    transpose_rows(state, flat, WIDE, lambda t, h: t * WIDE + h)
    rhs = gz[...].reshape(FRAMES * HEIGHT * WIDTH, CHANS)
    for a in range(3):
        lhs = jnp.concatenate(
            [flat[:, pl.ds((t * WIDE + a) * WIDTH, HEIGHT * WIDTH)] for t in range(FRAMES)], axis=1
        )
        yield a, jnp.dot(lhs, rhs, preferred_element_type=F32)


def in_grad(adj, flat_mid, edges, flat_edge):
    transpose_rows(edges, flat_edge, 4, lambda t, h: t * 4 + h)
    rhs = adj[...].reshape(FRAMES * WIDE * WIDTH, CHANS)
    for a in range(3):
        pieces = []
        for t in range(FRAMES):
            at = t * 4 * WIDTH
            if a < 2:
                pieces.append(flat_edge[:, at + a * WIDTH : at + 2 * WIDTH])
            pieces.append(flat_mid[:, at : at + 4 * WIDTH])
            if a > 0:
                pieces.append(flat_edge[:, at + 2 * WIDTH : at + (2 + a) * WIDTH])
        yield a, jnp.dot(jnp.concatenate(pieces, axis=1), rhs, preferred_element_type=F32)


def adjoint_stage(scales, spot, sources, adj, small):
    local, incoming, state_f, carry, table, skip = sources
    d0, d1 = table[0:1, :], table[1:2, :]
    sums = [[jnp.zeros((8, 128), F32) for _ in HALVES] for _ in range(FRAMES)]
    for h, half in blocks(WIDE):
        c = take_chunks(incoming, h, half)
        a0 = local[0, h, :, half] + d1[:, half] * c
        a1 = local[1, h, :, half] + c
        adj[0, h, :, half] = a0.astype(BF)
        adj[1, h, :, half] = a1.astype(BF)
        k = HALVES.index(half)
        pairs = ((a0, take_chunks(carry, h, half)), (a1, state_f[h, :, half]))
        for t, (a, earlier) in enumerate(pairs):
            sums[t][k] = sums[t][k] + jnp.sum((a * earlier).reshape(WIDTH // 8, 8, 128), axis=0)
    k0, k1 = (
        jnp.concatenate([jnp.sum(v, axis=0, keepdims=True) for v in pair], axis=1) * d
        for pair, d in zip(sums, (d0, d1))
    )
    rate = (k0 * table[2:3, :] + k1 * table[3:4, :]) * (-scales[0])
    s0 = jnp.sum(k0 * table[4:5, :], axis=1, keepdims=True) * (-scales[1])
    s1 = jnp.sum(k1 * table[4:5, :], axis=1, keepdims=True) * (-scales[1])
    lane = lax.broadcasted_iota(jnp.int32, (1, 128), 1)
    at = spot.place * FRAMES
    steps = jnp.where(lane == at, s0, jnp.where(lane == at + 1, s1, 0.0))
    small[...] = small_rows(rate, skip[...] * scales[0], steps)


def odd_grad_body(
    scales, local, incoming, state_f, carry, table, skip, flat_mid, edges, message, flat_message,
    payload, out_part, adj, small, flat, flat_edge,
):
    spot = Spot()

    @pl.when(spot.core == 0)
    def _():
        payload[...] = flat_message[...]

    @pl.when(spot.core == 1)
    def _():
        adjoint_stage(scales, spot, (local, incoming, state_f, carry, table, skip), adj, small)
        for a, g in in_grad(adj, flat_mid, edges, flat_edge):
            pack_grad(g, a, scales[0], payload)
        for a, g in out_grad(message.at[:, 0:WIDE], message.at[:, WIDE:], flat):
            pack_grad(g, a, scales[0], out_part)


def adjoint_body(
    scales, local, incoming, state_f, carry, table, skip, odd_adj, odd_small,
    adj, to_core, to_chip, small,
):
    spot = Spot()

    @pl.when(spot.core == 0)
    def _():
        adjoint_stage(scales, spot, (local, incoming, state_f, carry, table, skip), adj, small)
        to_chip[...] = adj[:, 0:2]
        to_core[...] = adj[:, WIDE - 2 :]

    @pl.when(spot.core == 1)
    def _():
        to_core[...] = odd_adj[:, 0:2]
        to_chip[...] = odd_adj[:, WIDE - 2 :]
        adj[...] = odd_adj[...]
        small[...] = odd_small[...]


def even_grad_body(scale, adj, flat_mid, edges, mine, flat_edge):
    @pl.when(Spot().core == 0)
    def _():
        for a, g in in_grad(adj, flat_mid, edges, flat_edge):
            pack_grad(g, a, scale, mine)


def grad_inputs_body(
    adj_far, core_far, chip_far, weight_far, direct_far,
    out_far, adj, from_core, from_chip, weight, direct, out, above, below, sems,
):
    spot = Spot()
    copies = fetch(
        sems,
        (core_far, from_core),
        (chip_far, from_chip),
        (adj_far, adj),
        (weight_far, weight),
        (direct_far, direct),
    )
    for copy in copies:
        copy.wait()
    place_halos(spot, from_core, from_chip, above, below)
    for t in range(FRAMES):
        up = (adj[t, 0:2].astype(F32) + above[t].astype(F32)).astype(BF)
        down = (adj[t, WIDE - 2 :].astype(F32) + below[t].astype(F32)).astype(BF)
        rows = jnp.concatenate([up, adj[t, 2 : WIDE - 2], down], axis=0)
        grad = conv(rows, weight, True)
        for h, half in blocks(HEIGHT):
            own = direct[t, h, :, half].astype(F32)
            out[t, h, :, half] = (grad(h, half) + own).astype(BF)
    (copy,) = fetch(sems, (out, out_far))
    copy.wait()


def pair_sum_body(scale, mine, out_part, got, message, send_far, send, flat, sems):
    core = Spot().core

    @pl.when(core == 0)
    def _():
        copies = []
        for k in range(GROUPS):
            total = mine[k].astype(F32) + got[k, 0:TAPS, :].astype(F32)
            for lg, half in enumerate(HALVES):
                send[k, lg] = total[:, half].astype(BF)
            if k % 8 == 7:
                part = slice(k - 7, k + 1)
                copies += fetch(sems.at[k // 8 : k // 8 + 1], (send.at[part], send_far.at[part]))
        for copy in copies:
            copy.wait()

    @pl.when(core == 1)
    def _():
        copies = []
        for a, g in out_grad(message.at[:, 0:WIDE], message.at[:, WIDE:], flat):
            for b in range(3):
                tap = (3 * a + b) * 8
                own = out_part[:, tap : tap + 8, :].astype(F32)
                total = g[b * CHANS : (b + 1) * CHANS].reshape(GROUPS, 8, CHANS) * scale + own
                for lg, half in enumerate(HALVES):
                    send[:, lg, tap : tap + 8, :] = total[:, :, half].astype(BF)
            part = slice(24 * a, 24 * a + 24)
            copies += fetch(sems.at[a : a + 1], (send.at[:, :, part], send_far.at[:, :, part]))
        for copy in copies:
            copy.wait()


def all_sum_body(got, small, send):
    total = jnp.zeros((TAPS, 128), F32)
    for k in range(CHIPS):
        total = total + got[k].astype(F32)
    total = jnp.concatenate([total.astype(BF), small[...]], axis=0)
    send[...] = jnp.broadcast_to(total[None], send.shape)


def write_grad(src, grad, stage, sems):
    copies = []
    for tap in range(9):
        a, b = tap // 3, tap % 3
        for lg, half in enumerate(HALVES):
            part = src[:, lg, tap * 8 : tap * 8 + 8, :].astype(F32)
            stage[a, b, :, half] = part.reshape(CHANS, 128)
        copies += fetch(sems.at[tap : tap + 1], (stage.at[a, b], grad.at[a, b]))
    return copies


def unpack_own_body(own, grad_out, grad_in, stage, sems):
    core = Spot().core

    @pl.when(core == 0)
    def _():
        for copy in write_grad(own, grad_in, stage, sems):
            copy.wait()

    @pl.when(core == 1)
    def _():
        for copy in write_grad(own, grad_out, stage, sems):
            copy.wait()


def unpack_other_body(
    own, got, out_half, in_half, grad_out, grad_in, rate_far, skip_far, step_far,
    stage, rate, skip, step, sems,
):
    del out_half, in_half
    spot = Spot()
    total = jnp.zeros((8, 128), F32)
    for k in range(GROUPS):
        for lg in range(2):
            pair = own[k, lg, TAPS:PACK, :].astype(F32) + got[k, lg, TAPS:PACK, :].astype(F32)
            total = total + pair
    rate[...] = total[0:2] + total[6:8]
    skip[...] = total[2:4]
    steps = total + pltpu.roll(total, 7, 0)
    step[...] = pltpu.roll(steps, (128 - spot.place * FRAMES) % 128, 1)[4:5, 0:FRAMES]
    smalls = fetch(sems.at[9:12], (rate, rate_far), (skip, skip_far), (step, step_far))

    @pl.when(spot.core == 0)
    def _():
        for copy in write_grad(got, grad_out, stage, sems):
            copy.wait()

    @pl.when(spot.core == 1)
    def _():
        for copy in write_grad(got, grad_in, stage, sems):
            copy.wait()

    for copy in smalls:
        copy.wait()


ROWS_AXES = ("z", "core")
TM_AXES = ("x", "y")
CORE_PAIRS = [(i, i ^ 1) for i in range(8)]
CHIP_PAIRS = [(i, (i + 1) % 8 if i % 2 else (i - 1) % 8) for i in range(8)]


def halos(to_core, to_chip):
    from_chip = lax.ppermute(to_chip, ROWS_AXES, CHIP_PAIRS)
    from_core = lax.ppermute(to_core, ROWS_AXES, CORE_PAIRS)
    return from_core, from_chip


def swap(chunks, axes):
    return lax.all_to_all(chunks, axes, 0, 0)


def vmem(shape, dtype=BF):
    return pltpu.VMEM(shape, dtype)


def sems(*shape):
    return pltpu.SemaphoreType.DMA(shape)


def on_device(inputs, in_weight, out_weight, skip_gain, rates, step_sizes, cotangent):
    scale = 1.0 / math.sqrt(32 * 32 * 128)
    step_scale = 1.0 / math.sqrt(1048576)
    core = lax.axis_index("core")
    field = (FRAMES, HEIGHT, WIDTH, CHANS)
    wide = (FRAMES, WIDE, WIDTH, CHANS)
    message = (FRAMES, WIDE + HEIGHT, WIDTH, CHANS)
    edge = (FRAMES, 2, WIDTH, CHANS)
    kernel = (3, 3, CHANS, CHANS)
    chunk = sds((BLOCKS, PLACES, CHANS), BF)
    packed = sds((GROUPS, 2, PACK, 128), BF)
    part = sds((GROUPS, TAPS, CHANS), BF)
    scales = (scale, step_scale)
    flat = sds((3 * CHANS, FRAMES * 4 * WIDTH), BF)
    params = jnp.concatenate([rates, skip_gain, jnp.pad(step_sizes, (0, CHANS - FRAMES))])
    params = params.reshape(3, CHANS)

    to_core = lax.dynamic_slice(inputs, (0, 2 - 2 * core, 0, 0), edge)
    to_chip = lax.dynamic_slice(inputs, (0, 2 * core, 0, 0), edge)
    from_core, from_chip = halos(to_core, to_chip)
    x, in_w, table, flat_mid = call(
        ready_body,
        [sds(field, BF), sds(kernel, BF), sds((8, CHANS), F32), flat],
        [far(inputs), far(in_weight), params],
        2 * ROW_FLOPS,
        [sems(2)],
    )
    local, send, edges = call(
        drive_body,
        [sds(wide, F32), sds((BLOCKS, PLACES + NOTE, CHANS), BF), sds(field, BF)],
        [x, from_core, from_chip, in_w, table],
        WIDE * ROW_FLOPS,
        [vmem(edge), vmem(edge)],
    )
    got = swap(send, TM_AXES)
    send, block_decays = call(forward_scan_body, [chunk, sds((BLOCKS, CHANS), F32)], [got, table])
    carry = swap(send, TM_AXES)
    outputs, direct, sent, state_f, local_adj, send, skip = call(
        middle_body,
        [
            far(sds(field, BF)),
            far(sds(field, BF)),
            sds(message, BF),
            sds(wide[1:], F32),
            sds(wide, F32),
            chunk,
            sds((1, CHANS), F32),
        ],
        [local, carry, x, cotangent, out_weight, table],
        (HEIGHT + WIDE) * ROW_FLOPS,
        [vmem(field), vmem(field), sems(2)],
    )
    got = swap(send, TM_AXES)
    (send,) = call(backward_scan_body, [chunk], [got, block_decays])
    incoming = swap(send, TM_AXES)
    sources = [local_adj, incoming, state_f, carry, table, skip, flat_mid, edges]
    flat_sent = sent.reshape(GROUPS, PACK, CHANS)
    payload, out_part, odd_adj, odd_small = call(
        functools.partial(odd_grad_body, scales),
        [sds(flat_sent.shape, BF), part, sds(wide, BF), sds((8, 128), BF)],
        [*sources, sent, flat_sent],
        WIDE * ROW_FLOPS,
        [vmem((3 * CHANS, FRAMES * WIDE * WIDTH)), vmem(flat.shape)],
    )
    got = lax.ppermute(payload, ROWS_AXES, CORE_PAIRS)
    adj, to_core, to_chip, small = call(
        functools.partial(adjoint_body, scales),
        [sds(wide, BF), sds(edge, BF), sds(edge, BF), sds((8, 128), BF)],
        [*sources[:6], odd_adj, odd_small],
    )
    from_core, from_chip = halos(to_core, to_chip)
    (mine,) = call(
        functools.partial(even_grad_body, scale),
        [part],
        [adj, flat_mid, edges],
        0,
        [vmem(flat.shape)],
        light=True,
    )
    (send,) = call(
        functools.partial(pair_sum_body, scale),
        [far(sds((GROUPS, 2, TAPS, 128), BF))],
        [mine, out_part, got, got.reshape(message)],
        0,
        [
            vmem((GROUPS, 2, TAPS, 128)),
            vmem((3 * CHANS, FRAMES * WIDE * WIDTH)),
            sems(4),
        ],
        light=True,
    )
    got = swap(send.reshape(CHIPS, TAPS, 128), ("x", "y", "z"))
    (grad_inputs,) = call(
        grad_inputs_body,
        [far(sds(field, BF))],
        [far(a) for a in (adj, from_core, from_chip, in_weight, direct)],
        4000 * ROW_FLOPS,
        [
            vmem(wide),
            vmem(edge),
            vmem(edge),
            vmem(kernel),
            vmem(field),
            vmem(field),
            vmem(edge),
            vmem(edge),
            sems(5),
        ],
        {4: 0},
    )
    small, grad_inputs = lax.optimization_barrier((small, grad_inputs))
    (send,) = call(all_sum_body, [sds((CHIPS, PACK, 128), BF)], [got, small])
    own = swap(send, ("x", "y", "z"))
    own = own.reshape(packed.shape)
    other = lax.ppermute(own, ROWS_AXES, CORE_PAIRS)
    weights = sds(kernel, F32)
    half = sds((2, 128), F32)
    stage = vmem(kernel, F32)
    grad_out_weight, grad_in_weight = call(
        unpack_own_body, [far(weights), far(weights)], [own], 0, [stage, sems(9)]
    )
    grad_out_weight, grad_in_weight, grad_rates, grad_skip, grad_steps = call(
        unpack_other_body,
        [far(a) for a in (weights, weights, half, half, sds((1, FRAMES), F32))],
        [own, other, far(grad_out_weight), far(grad_in_weight)],
        0,
        [stage, vmem((2, 128), F32), vmem((2, 128), F32), vmem((1, FRAMES), F32), sems(12)],
        {2: 0, 3: 1},
    )
    return (
        outputs,
        grad_inputs,
        grad_in_weight,
        grad_out_weight,
        grad_skip.reshape(CHANS),
        grad_rates.reshape(CHANS),
        grad_steps.reshape(FRAMES),
    )


def solution(mesh):
    fine = Mesh(mesh.devices.reshape(4, 4, 4, 2), ("x", "y", "z", "core"))
    spread_out = P(TM_AXES, ROWS_AXES, None, None)
    placed = (spread_out, P(), P(), P(), P(), P(TM_AXES), spread_out)
    return jax.shard_map(
        on_device,
        mesh=fine,
        in_specs=placed,
        out_specs=(spread_out, spread_out, P(), P(), P(), P(), P(TM_AXES)),
        check_vma=False,
    )
```

```python
import functools
import math

import jax
import jax.numpy as jnp
from jax import lax
from jax.experimental import pallas as pl
from jax.experimental.pallas import tpu as pltpu
from jax.sharding import Mesh, PartitionSpec as P

BF, F32 = jnp.bfloat16, jnp.float32
VM = pl.BlockSpec(memory_space=pltpu.VMEM)
HB = pl.BlockSpec(memory_space=pltpu.HBM)
GRANT = 24 << 20
FRAMES, HEIGHT, WIDTH, CHANS = 2, 4, 128, 256
WIDE, WIDER = HEIGHT + 2, HEIGHT + 4
BLOCKS = 16
PLACES = WIDE * WIDTH // BLOCKS
NOTE = 8
CHIPS = 64
GROUPS = 32
TAPS = 72
PACK = TAPS + 8


def sds(shape, dtype):
    return jax.ShapeDtypeStruct(shape, dtype)


def call(body, outs, ins, flops=0, scratch=(), aliases=None, light=False):
    ins = [i if isinstance(i, tuple) else (i, VM) for i in ins]
    outs = [o if isinstance(o, tuple) else (o, VM) for o in outs]
    nbytes = sum(math.prod(a.shape) * a.dtype.itemsize for a, _ in ins + outs)
    return pl.pallas_call(
        body,
        out_shape=[o for o, _ in outs],
        in_specs=[s for _, s in ins],
        out_specs=[s for _, s in outs],
        scratch_shapes=list(scratch),
        input_output_aliases=aliases or {},
        compiler_params=pltpu.CompilerParams(vmem_limit_bytes=GRANT),
        cost_estimate=pl.CostEstimate(flops=flops, bytes_accessed=0 if light else nbytes, transcendentals=0),
    )(*[i for i, _ in ins])


def far(array):
    return array, HB


def fetch(sems, *pairs):
    copies = [pltpu.make_async_copy(s, d, sems.at[i]) for i, (s, d) in enumerate(pairs)]
    for copy in copies:
        copy.start()
    return copies


class Spot:
    def __init__(self):
        z = lax.axis_index("z")
        self.core = lax.axis_index("core")
        self.top = jnp.logical_and(z == 0, self.core == 0)
        self.bottom = jnp.logical_and(z == 3, self.core == 1)
        self.place = lax.axis_index("x") * 4 + lax.axis_index("y")


ROW_FLOPS = 2 * 9 * FRAMES * WIDTH * CHANS * CHANS


def col_shift(v, by):
    turned = pltpu.roll(v, by % WIDTH, 0)
    at = lax.broadcasted_iota(jnp.int32, v.shape, 0)
    return jnp.where(at == (0 if by == 1 else WIDTH - 1), 0.0, turned)


HALVES = [slice(0, 128), slice(128, 256)]


def conv(rows, weight, flipped):
    height = rows.shape[0] - 2
    lhs = jnp.concatenate([rows[a : a + height] for a in range(3)], axis=-1)
    lhs = lhs.reshape(height * WIDTH, 3 * CHANS)
    parts = []
    for b in range(3):
        if flipped:
            rhs = jnp.concatenate([weight[2 - a, 2 - b] for a in range(3)], axis=1)
            y = lax.dot_general(lhs, rhs, (((1,), (1,)), ((), ())), preferred_element_type=F32)
        else:
            rhs = jnp.concatenate([weight[a, b] for a in range(3)], axis=0)
            y = jnp.dot(lhs, rhs, preferred_element_type=F32)
        parts.append(y.reshape(height, WIDTH, CHANS))

    def block(h, half):
        left, mid, right = (part[h, :, half] for part in parts)
        return mid + col_shift(left, 1) + col_shift(right, -1)

    return block


def spread_conv(field, weight):
    pieces = []
    for first, count, taps in ((0, 1, (2,)), (1, 1, (1, 2)), (2, 2, (0, 1, 2)), (4, 1, (0, 1)), (5, 1, (0,))):
        lhs = jnp.concatenate(
            [field[:, first + a - 2 : first + a - 2 + count] for a in taps], axis=-1
        ).reshape(FRAMES * count * WIDTH, len(taps) * CHANS)
        parts = []
        for b in range(3):
            rhs = jnp.concatenate([weight[2 - a, 2 - b] for a in taps], axis=1)
            y = lax.dot_general(lhs, rhs, (((1,), (1,)), ((), ())), preferred_element_type=F32)
            parts.append(y.reshape(FRAMES, count, WIDTH, CHANS))
        pieces += [(parts, k) for k in range(count)]

    def block(t, h, half):
        parts, k = pieces[h]
        left, mid, right = (part[t, k, :, half] for part in parts)
        return mid + col_shift(left, 1) + col_shift(right, -1)

    return block


def blocks(height):
    return [(h, half) for h in range(height) for half in HALVES]


def outer(spot, h, v):
    if h == 0:
        return jnp.where(spot.top, 0.0, v)
    if h == WIDE - 1:
        return jnp.where(spot.bottom, 0.0, v)
    return v


def put_chunks(send, h, half, v):
    for k in range(WIDTH // 16):
        place = h * WIDTH + k * 16
        send[place // PLACES, place % PLACES : place % PLACES + 16, half] = v[
            k * 16 : (k + 1) * 16
        ].astype(BF)


def take_chunks(ref, h, half):
    pieces = []
    for k in range(WIDTH // 16):
        place = h * WIDTH + k * 16
        pieces.append(ref[place // PLACES, place % PLACES : place % PLACES + 16, half])
    return jnp.concatenate(pieces, axis=0).astype(F32)


def transpose_rows(v_ref, out_ref, rows, at_row):
    lane = lax.broadcasted_iota(jnp.int32, (CHANS, WIDTH), 1)
    for t in range(FRAMES):
        for h in range(rows):
            flat = v_ref[t, h].astype(F32).T
            at = pl.ds(at_row(t, h) * WIDTH, WIDTH)
            left = jnp.where(lane == 0, 0.0, pltpu.roll(flat, 1, 1))
            right = jnp.where(lane == WIDTH - 1, 0.0, pltpu.roll(flat, WIDTH - 1, 1))
            out_ref[0:CHANS, at] = left.astype(BF)
            out_ref[CHANS : 2 * CHANS, at] = flat.astype(BF)
            out_ref[2 * CHANS : 3 * CHANS, at] = right.astype(BF)


def ready_body(x_far, in_far, params, x, in_weight, table, flat_mid, sems):
    copies = fetch(sems, (x_far, x), (in_far, in_weight))
    r = params[0:1, :]
    s0 = jnp.broadcast_to(params[2:3, 0:1], (1, CHANS))
    s1 = jnp.broadcast_to(params[2:3, 1:2], (1, CHANS))
    lines = [jnp.exp(-r * s0), jnp.exp(-r * s1), s0, s1, r, params[1:2, :], s0 + s1, r]
    for k, line in enumerate(lines):
        table[k : k + 1, :] = line
    copies[0].wait()
    transpose_rows(x, flat_mid, HEIGHT, lambda t, h: t * HEIGHT + h)
    copies[1].wait()


def place_halos(spot, from_core, from_chip, above, below):
    @pl.when(spot.core == 0)
    def _():
        above[...] = from_chip[...]
        below[...] = from_core[...]

    @pl.when(spot.core == 1)
    def _():
        above[...] = from_core[...]
        below[...] = from_chip[...]

    @pl.when(spot.top)
    def _():
        above[...] = jnp.zeros_like(above)

    @pl.when(spot.bottom)
    def _():
        below[...] = jnp.zeros_like(below)


def drive_body(
    x, from_core, from_chip, weight, table, local, send, edges, above, below
):
    spot = Spot()
    place_halos(spot, from_core, from_chip, above, below)
    for t in range(FRAMES):
        rows = jnp.concatenate([above[t], x[t], below[t]], axis=0)
        drive = conv(rows, weight, False)
        for h, half in blocks(WIDE):
            v = outer(spot, h, drive(h, half))
            if t == 1:
                v = table[1:2, half] * local[0, h, :, half] + v
                put_chunks(send, h, half, v)
            local[t, h, :, half] = v
    total = jnp.broadcast_to(table[6:7, :][None], (BLOCKS, NOTE, CHANS))
    row = lax.broadcasted_iota(jnp.int32, total.shape, 1)
    one = total.astype(BF).astype(F32)
    two = (total - one).astype(BF).astype(F32)
    three = total - one - two
    send[:, PLACES : PLACES + NOTE, :] = jnp.where(
        row == 0, one, jnp.where(row == 1, two, jnp.where(row == 2, three, 0.0))
    ).astype(BF)
    edges[:, 0:2] = above[...]
    edges[:, 2:4] = below[...]


def forward_scan_body(got, table, send, block_decays):
    carry = jnp.zeros((PLACES, CHANS), F32)
    for k in range(BLOCKS):
        send[k] = carry.astype(BF)
        span = jnp.sum(got[k, PLACES : PLACES + NOTE, :].astype(F32), axis=0, keepdims=True)
        d = jnp.exp(-table[4:5, :] * span)
        block_decays[pl.ds(k, 1), :] = d
        carry = d * carry + got[k, 0:PLACES, :].astype(F32)


def backward_scan_body(got, block_decays, send):
    carry = jnp.zeros((PLACES, CHANS), F32)
    for k in reversed(range(BLOCKS)):
        send[k] = carry.astype(BF)
        carry = block_decays[pl.ds(k, 1), :] * carry + got[k].astype(F32)


GELU_A = math.sqrt(2 / math.pi)


def small_rows(rate, skip, steps):
    row = lax.broadcasted_iota(jnp.int32, (8, 128), 0)
    halves = [v[:, half] for v in (rate, skip) for half in HALVES]
    lines = halves + [steps, steps] + halves[0:2]
    out = jnp.zeros((8, 128), F32)
    for k, line in enumerate(lines):
        out = jnp.where(row == k, jnp.broadcast_to(line, (8, 128)), out)
    top = out.astype(BF).astype(F32)
    return jnp.where(row < 5, top, out - top).astype(BF)


def middle_body(
    local, carry, x, cot, weight, table,
    out_far, direct_far, message, state_f, local_adj, send, skip, out, direct, sems,
):
    spot = Spot()
    state, gz = message.at[:, 0:WIDE], message.at[:, WIDE:]
    d0, d1 = table[0:1, :], table[1:2, :]
    for h, half in blocks(WIDE):
        c = take_chunks(carry, h, half)
        s0 = local[0, h, :, half] + d0[:, half] * c
        state_f[h, :, half] = s0
        state[0, h, :, half] = s0.astype(BF)
        s1 = local[1, h, :, half] + (d0 * d1)[:, half] * c
        state[1, h, :, half] = s1.astype(BF)
    totals = [jnp.zeros((8, 128), F32) for _ in HALVES]
    for t in (1, 0):
        pre_act = conv(state[t], weight, False)
        for h, half in blocks(HEIGHT):
            xt = x[t, h, :, half].astype(F32)
            z = pre_act(h, half) + table[5:6, half] * xt
            zz = z * z
            th = jnp.tanh(GELU_A * (z + 0.044715 * (zz * z)))
            gate = 0.5 * (1.0 + th)
            out[t, h, :, half] = (z * gate).astype(BF)
            slope = gate + 0.5 * z * (1.0 - th * th) * (GELU_A * (1.0 + 3 * 0.044715 * zz))
            g = cot[t, h, :, half].astype(F32) * slope
            gz[t, h, :, half] = g.astype(BF)
            direct[t, h, :, half] = (table[5:6, half] * g).astype(BF)
            k = HALVES.index(half)
            totals[k] = totals[k] + jnp.sum((g * xt).reshape(WIDTH // 8, 8, 128), axis=0)
    copies = fetch(sems, (out, out_far), (direct, direct_far))
    grad = spread_conv(gz, weight)
    for t in (1, 0):
        for h, half in blocks(WIDE):
            v = outer(spot, h, grad(t, h, half))
            if t == 0:
                v = v + d1[:, half] * local_adj[1, h, :, half]
                put_chunks(send, h, half, d0[:, half] * v)
            local_adj[t, h, :, half] = v
    total = jnp.concatenate([jnp.sum(v, axis=0, keepdims=True) for v in totals], axis=1)
    skip[...] = total
    for copy in copies:
        copy.wait()


def pack_grad(g, a, scale, out):
    for b in range(3):
        tap = (3 * a + b) * 8
        part = (g[b * CHANS : (b + 1) * CHANS] * scale).astype(BF)
        out[:, tap : tap + 8, :] = part.reshape(GROUPS, 8, CHANS)


def out_grad(state, gz, flat):
    transpose_rows(state, flat, WIDE, lambda t, h: t * WIDE + h)
    rhs = gz[...].reshape(FRAMES * HEIGHT * WIDTH, CHANS)
    for a in range(3):
        lhs = jnp.concatenate(
            [flat[:, pl.ds((t * WIDE + a) * WIDTH, HEIGHT * WIDTH)] for t in range(FRAMES)], axis=1
        )
        yield a, jnp.dot(lhs, rhs, preferred_element_type=F32)


def in_grad(adj, flat_mid, edges, flat_edge):
    transpose_rows(edges, flat_edge, 4, lambda t, h: t * 4 + h)
    rhs = adj[...].reshape(FRAMES * WIDE * WIDTH, CHANS)
    for a in range(3):
        pieces = []
        for t in range(FRAMES):
            at = t * 4 * WIDTH
            if a < 2:
                pieces.append(flat_edge[:, at + a * WIDTH : at + 2 * WIDTH])
            pieces.append(flat_mid[:, at : at + 4 * WIDTH])
            if a > 0:
                pieces.append(flat_edge[:, at + 2 * WIDTH : at + (2 + a) * WIDTH])
        yield a, jnp.dot(jnp.concatenate(pieces, axis=1), rhs, preferred_element_type=F32)


def adjoint_stage(scales, spot, sources, adj, small):
    local, incoming, state_f, carry, table, skip = sources
    d0, d1 = table[0:1, :], table[1:2, :]
    sums = [[jnp.zeros((8, 128), F32) for _ in HALVES] for _ in range(FRAMES)]
    for h, half in blocks(WIDE):
        c = take_chunks(incoming, h, half)
        a0 = local[0, h, :, half] + d1[:, half] * c
        a1 = local[1, h, :, half] + c
        adj[0, h, :, half] = a0.astype(BF)
        adj[1, h, :, half] = a1.astype(BF)
        k = HALVES.index(half)
        pairs = ((a0, take_chunks(carry, h, half)), (a1, state_f[h, :, half]))
        for t, (a, earlier) in enumerate(pairs):
            sums[t][k] = sums[t][k] + jnp.sum((a * earlier).reshape(WIDTH // 8, 8, 128), axis=0)
    k0, k1 = (
        jnp.concatenate([jnp.sum(v, axis=0, keepdims=True) for v in pair], axis=1) * d
        for pair, d in zip(sums, (d0, d1))
    )
    rate = (k0 * table[2:3, :] + k1 * table[3:4, :]) * (-scales[0])
    s0 = jnp.sum(k0 * table[4:5, :], axis=1, keepdims=True) * (-scales[1])
    s1 = jnp.sum(k1 * table[4:5, :], axis=1, keepdims=True) * (-scales[1])
    lane = lax.broadcasted_iota(jnp.int32, (1, 128), 1)
    at = spot.place * FRAMES
    steps = jnp.where(lane == at, s0, jnp.where(lane == at + 1, s1, 0.0))
    small[...] = small_rows(rate, skip[...] * scales[0], steps)


def odd_grad_body(
    scales, local, incoming, state_f, carry, table, skip, flat_mid, edges, message, flat_message,
    payload, out_part, adj, small, flat, flat_edge,
):
    spot = Spot()

    @pl.when(spot.core == 0)
    def _():
        payload[...] = flat_message[...]

    @pl.when(spot.core == 1)
    def _():
        adjoint_stage(scales, spot, (local, incoming, state_f, carry, table, skip), adj, small)
        for a, g in in_grad(adj, flat_mid, edges, flat_edge):
            pack_grad(g, a, scales[0], payload)
        for a, g in out_grad(message.at[:, 0:WIDE], message.at[:, WIDE:], flat):
            pack_grad(g, a, scales[0], out_part)


def adjoint_body(
    scales, local, incoming, state_f, carry, table, skip, odd_adj, odd_small,
    adj, to_core, to_chip, small,
):
    spot = Spot()

    @pl.when(spot.core == 0)
    def _():
        adjoint_stage(scales, spot, (local, incoming, state_f, carry, table, skip), adj, small)
        to_chip[...] = adj[:, 0:2]
        to_core[...] = adj[:, WIDE - 2 :]

    @pl.when(spot.core == 1)
    def _():
        to_core[...] = odd_adj[:, 0:2]
        to_chip[...] = odd_adj[:, WIDE - 2 :]
        adj[...] = odd_adj[...]
        small[...] = odd_small[...]


def even_grad_body(scale, adj, flat_mid, edges, mine, flat_edge):
    @pl.when(Spot().core == 0)
    def _():
        for a, g in in_grad(adj, flat_mid, edges, flat_edge):
            pack_grad(g, a, scale, mine)


def grad_inputs_body(
    adj_far, core_far, chip_far, weight_far, direct_far,
    out_far, adj, from_core, from_chip, weight, direct, out, above, below, sems,
):
    spot = Spot()
    copies = fetch(
        sems,
        (core_far, from_core),
        (chip_far, from_chip),
        (adj_far, adj),
        (weight_far, weight),
        (direct_far, direct),
    )
    for copy in copies:
        copy.wait()
    place_halos(spot, from_core, from_chip, above, below)
    for t in range(FRAMES):
        up = (adj[t, 0:2].astype(F32) + above[t].astype(F32)).astype(BF)
        down = (adj[t, WIDE - 2 :].astype(F32) + below[t].astype(F32)).astype(BF)
        rows = jnp.concatenate([up, adj[t, 2 : WIDE - 2], down], axis=0)
        grad = conv(rows, weight, True)
        for h, half in blocks(HEIGHT):
            own = direct[t, h, :, half].astype(F32)
            out[t, h, :, half] = (grad(h, half) + own).astype(BF)
    (copy,) = fetch(sems, (out, out_far))
    copy.wait()


def pair_sum_body(scale, mine, out_part, got, message, send_far, send, flat, sems):
    core = Spot().core

    @pl.when(core == 0)
    def _():
        copies = []
        for k in range(GROUPS):
            total = mine[k].astype(F32) + got[k, 0:TAPS, :].astype(F32)
            for lg, half in enumerate(HALVES):
                send[k, lg] = total[:, half].astype(BF)
            if k % 8 == 7:
                part = slice(k - 7, k + 1)
                copies += fetch(sems.at[k // 8 : k // 8 + 1], (send.at[part], send_far.at[part]))
        for copy in copies:
            copy.wait()

    @pl.when(core == 1)
    def _():
        copies = []
        for a, g in out_grad(message.at[:, 0:WIDE], message.at[:, WIDE:], flat):
            for b in range(3):
                tap = (3 * a + b) * 8
                own = out_part[:, tap : tap + 8, :].astype(F32)
                total = g[b * CHANS : (b + 1) * CHANS].reshape(GROUPS, 8, CHANS) * scale + own
                for lg, half in enumerate(HALVES):
                    send[:, lg, tap : tap + 8, :] = total[:, :, half].astype(BF)
            part = slice(24 * a, 24 * a + 24)
            copies += fetch(sems.at[a : a + 1], (send.at[:, :, part], send_far.at[:, :, part]))
        for copy in copies:
            copy.wait()


def all_sum_body(got, small, send):
    total = jnp.zeros((TAPS, 128), F32)
    for k in range(CHIPS):
        total = total + got[k].astype(F32)
    total = jnp.concatenate([total.astype(BF), small[...]], axis=0)
    send[...] = jnp.broadcast_to(total[None], send.shape)


def write_grad(src, grad, stage, sems):
    copies = []
    for tap in range(9):
        a, b = tap // 3, tap % 3
        for lg, half in enumerate(HALVES):
            part = src[:, lg, tap * 8 : tap * 8 + 8, :].astype(F32)
            stage[a, b, :, half] = part.reshape(CHANS, 128)
        copies += fetch(sems.at[tap : tap + 1], (stage.at[a, b], grad.at[a, b]))
    return copies


def unpack_own_body(own, grad_out, grad_in, stage, sems):
    core = Spot().core

    @pl.when(core == 0)
    def _():
        for copy in write_grad(own, grad_in, stage, sems):
            copy.wait()

    @pl.when(core == 1)
    def _():
        for copy in write_grad(own, grad_out, stage, sems):
            copy.wait()


def unpack_other_body(
    own, got, out_half, in_half, grad_out, grad_in, rate_far, skip_far, step_far,
    stage, rate, skip, step, sems,
):
    del out_half, in_half
    spot = Spot()
    total = jnp.zeros((8, 128), F32)
    for k in range(GROUPS):
        for lg in range(2):
            pair = own[k, lg, TAPS:PACK, :].astype(F32) + got[k, lg, TAPS:PACK, :].astype(F32)
            total = total + pair
    rate[...] = total[0:2] + total[6:8]
    skip[...] = total[2:4]
    steps = total + pltpu.roll(total, 7, 0)
    step[...] = pltpu.roll(steps, (128 - spot.place * FRAMES) % 128, 1)[4:5, 0:FRAMES]
    smalls = fetch(sems.at[9:12], (rate, rate_far), (skip, skip_far), (step, step_far))

    @pl.when(spot.core == 0)
    def _():
        for copy in write_grad(got, grad_out, stage, sems):
            copy.wait()

    @pl.when(spot.core == 1)
    def _():
        for copy in write_grad(got, grad_in, stage, sems):
            copy.wait()

    for copy in smalls:
        copy.wait()


ROWS_AXES = ("z", "core")
TM_AXES = ("x", "y")
CORE_PAIRS = [(i, i ^ 1) for i in range(8)]
CHIP_PAIRS = [(i, (i + 1) % 8 if i % 2 else (i - 1) % 8) for i in range(8)]


def halos(to_core, to_chip):
    from_chip = lax.ppermute(to_chip, ROWS_AXES, CHIP_PAIRS)
    from_core = lax.ppermute(to_core, ROWS_AXES, CORE_PAIRS)
    return from_core, from_chip


def swap(chunks, axes):
    return lax.all_to_all(chunks, axes, 0, 0)


def vmem(shape, dtype=BF):
    return pltpu.VMEM(shape, dtype)


def sems(*shape):
    return pltpu.SemaphoreType.DMA(shape)


def on_device(inputs, in_weight, out_weight, skip_gain, rates, step_sizes, cotangent):
    scale = 1.0 / math.sqrt(32 * 32 * 128)
    step_scale = 1.0 / math.sqrt(1048576)
    core = lax.axis_index("core")
    field = (FRAMES, HEIGHT, WIDTH, CHANS)
    wide = (FRAMES, WIDE, WIDTH, CHANS)
    message = (FRAMES, WIDE + HEIGHT, WIDTH, CHANS)
    edge = (FRAMES, 2, WIDTH, CHANS)
    kernel = (3, 3, CHANS, CHANS)
    chunk = sds((BLOCKS, PLACES, CHANS), BF)
    packed = sds((GROUPS, 2, PACK, 128), BF)
    part = sds((GROUPS, TAPS, CHANS), BF)
    scales = (scale, step_scale)
    flat = sds((3 * CHANS, FRAMES * 4 * WIDTH), BF)
    params = jnp.concatenate([rates, skip_gain, jnp.pad(step_sizes, (0, CHANS - FRAMES))])
    params = params.reshape(3, CHANS)

    to_core = lax.dynamic_slice(inputs, (0, 2 - 2 * core, 0, 0), edge)
    to_chip = lax.dynamic_slice(inputs, (0, 2 * core, 0, 0), edge)
    from_core, from_chip = halos(to_core, to_chip)
    x, in_w, table, flat_mid = call(
        ready_body,
        [sds(field, BF), sds(kernel, BF), sds((8, CHANS), F32), flat],
        [far(inputs), far(in_weight), params],
        2 * ROW_FLOPS,
        [sems(2)],
    )
    local, send, edges = call(
        drive_body,
        [sds(wide, F32), sds((BLOCKS, PLACES + NOTE, CHANS), BF), sds(field, BF)],
        [x, from_core, from_chip, in_w, table],
        WIDE * ROW_FLOPS,
        [vmem(edge), vmem(edge)],
    )
    got = swap(send, TM_AXES)
    send, block_decays = call(forward_scan_body, [chunk, sds((BLOCKS, CHANS), F32)], [got, table])
    carry = swap(send, TM_AXES)
    outputs, direct, sent, state_f, local_adj, send, skip = call(
        middle_body,
        [
            far(sds(field, BF)),
            far(sds(field, BF)),
            sds(message, BF),
            sds(wide[1:], F32),
            sds(wide, F32),
            chunk,
            sds((1, CHANS), F32),
        ],
        [local, carry, x, cotangent, out_weight, table],
        (HEIGHT + WIDE) * ROW_FLOPS,
        [vmem(field), vmem(field), sems(2)],
    )
    got = swap(send, TM_AXES)
    (send,) = call(backward_scan_body, [chunk], [got, block_decays])
    incoming = swap(send, TM_AXES)
    sources = [local_adj, incoming, state_f, carry, table, skip, flat_mid, edges]
    flat_sent = sent.reshape(GROUPS, PACK, CHANS)
    payload, out_part, odd_adj, odd_small = call(
        functools.partial(odd_grad_body, scales),
        [sds(flat_sent.shape, BF), part, sds(wide, BF), sds((8, 128), BF)],
        [*sources, sent, flat_sent],
        WIDE * ROW_FLOPS,
        [vmem((3 * CHANS, FRAMES * WIDE * WIDTH)), vmem(flat.shape)],
    )
    got = lax.ppermute(payload, ROWS_AXES, CORE_PAIRS)
    adj, to_core, to_chip, small = call(
        functools.partial(adjoint_body, scales),
        [sds(wide, BF), sds(edge, BF), sds(edge, BF), sds((8, 128), BF)],
        [*sources[:6], odd_adj, odd_small],
    )
    from_core, from_chip = halos(to_core, to_chip)
    (mine,) = call(
        functools.partial(even_grad_body, scale),
        [part],
        [adj, flat_mid, edges],
        0,
        [vmem(flat.shape)],
        light=True,
    )
    (send,) = call(
        functools.partial(pair_sum_body, scale),
        [far(sds((GROUPS, 2, TAPS, 128), BF))],
        [mine, out_part, got, got.reshape(message)],
        0,
        [
            vmem((GROUPS, 2, TAPS, 128)),
            vmem((3 * CHANS, FRAMES * WIDE * WIDTH)),
            sems(4),
        ],
        light=True,
    )
    got = swap(send.reshape(CHIPS, TAPS, 128), ("x", "y", "z"))
    (grad_inputs,) = call(
        grad_inputs_body,
        [far(sds(field, BF))],
        [far(a) for a in (adj, from_core, from_chip, in_weight, direct)],
        100 * ROW_FLOPS,
        [
            vmem(wide),
            vmem(edge),
            vmem(edge),
            vmem(kernel),
            vmem(field),
            vmem(field),
            vmem(edge),
            vmem(edge),
            sems(5),
        ],
        {4: 0},
    )
    small, grad_inputs = lax.optimization_barrier((small, grad_inputs))
    (send,) = call(all_sum_body, [sds((CHIPS, PACK, 128), BF)], [got, small])
    own = swap(send, ("x", "y", "z"))
    own = own.reshape(packed.shape)
    other = lax.ppermute(own, ROWS_AXES, CORE_PAIRS)
    weights = sds(kernel, F32)
    half = sds((2, 128), F32)
    stage = vmem(kernel, F32)
    grad_out_weight, grad_in_weight = call(
        unpack_own_body, [far(weights), far(weights)], [own], 0, [stage, sems(9)]
    )
    grad_out_weight, grad_in_weight, grad_rates, grad_skip, grad_steps = call(
        unpack_other_body,
        [far(a) for a in (weights, weights, half, half, sds((1, FRAMES), F32))],
        [own, other, far(grad_out_weight), far(grad_in_weight)],
        0,
        [stage, vmem((2, 128), F32), vmem((2, 128), F32), vmem((1, FRAMES), F32), sems(12)],
        {2: 0, 3: 1},
    )
    return (
        outputs,
        grad_inputs,
        grad_in_weight,
        grad_out_weight,
        grad_skip.reshape(CHANS),
        grad_rates.reshape(CHANS),
        grad_steps.reshape(FRAMES),
    )


def solution(mesh):
    fine = Mesh(mesh.devices.reshape(4, 4, 4, 2), ("x", "y", "z", "core"))
    spread_out = P(TM_AXES, ROWS_AXES, None, None)
    placed = (spread_out, P(), P(), P(), P(), P(TM_AXES), spread_out)
    return jax.shard_map(
        on_device,
        mesh=fine,
        in_specs=placed,
        out_specs=(spread_out, spread_out, P(), P(), P(), P(), P(TM_AXES)),
        check_vma=False,
    )
```

```python
import functools
import math

import jax
import jax.numpy as jnp
from jax import lax
from jax.experimental import pallas as pl
from jax.experimental.pallas import tpu as pltpu
from jax.sharding import Mesh, PartitionSpec as P

BF, F32 = jnp.bfloat16, jnp.float32
VM = pl.BlockSpec(memory_space=pltpu.VMEM)
HB = pl.BlockSpec(memory_space=pltpu.HBM)
GRANT = 16 << 20
FRAMES, HEIGHT, WIDTH, CHANS = 2, 4, 128, 256
WIDE, WIDER = HEIGHT + 2, HEIGHT + 4
BLOCKS = 16
PLACES = WIDE * WIDTH // BLOCKS
NOTE = 8
CHIPS = 64
GROUPS = 32
TAPS = 72
PACK = TAPS + 8


def sds(shape, dtype):
    return jax.ShapeDtypeStruct(shape, dtype)


def call(body, outs, ins, flops=0, scratch=(), aliases=None, light=False):
    ins = [i if isinstance(i, tuple) else (i, VM) for i in ins]
    outs = [o if isinstance(o, tuple) else (o, VM) for o in outs]
    nbytes = sum(math.prod(a.shape) * a.dtype.itemsize for a, _ in ins + outs)
    return pl.pallas_call(
        body,
        out_shape=[o for o, _ in outs],
        in_specs=[s for _, s in ins],
        out_specs=[s for _, s in outs],
        scratch_shapes=list(scratch),
        input_output_aliases=aliases or {},
        compiler_params=pltpu.CompilerParams(vmem_limit_bytes=GRANT),
        cost_estimate=pl.CostEstimate(flops=flops, bytes_accessed=0 if light else nbytes, transcendentals=0),
    )(*[i for i, _ in ins])


def far(array):
    return array, HB


def fetch(sems, *pairs):
    copies = [pltpu.make_async_copy(s, d, sems.at[i]) for i, (s, d) in enumerate(pairs)]
    for copy in copies:
        copy.start()
    return copies


class Spot:
    def __init__(self):
        z = lax.axis_index("z")
        self.core = lax.axis_index("core")
        self.top = jnp.logical_and(z == 0, self.core == 0)
        self.bottom = jnp.logical_and(z == 3, self.core == 1)
        self.place = lax.axis_index("x") * 4 + lax.axis_index("y")


ROW_FLOPS = 2 * 9 * FRAMES * WIDTH * CHANS * CHANS


def col_shift(v, by):
    turned = pltpu.roll(v, by % WIDTH, 0)
    at = lax.broadcasted_iota(jnp.int32, v.shape, 0)
    return jnp.where(at == (0 if by == 1 else WIDTH - 1), 0.0, turned)


HALVES = [slice(0, 128), slice(128, 256)]


def conv(rows, weight, flipped):
    height = rows.shape[0] - 2
    lhs = jnp.concatenate([rows[a : a + height] for a in range(3)], axis=-1)
    lhs = lhs.reshape(height * WIDTH, 3 * CHANS)
    parts = []
    for b in range(3):
        if flipped:
            rhs = jnp.concatenate([weight[2 - a, 2 - b] for a in range(3)], axis=1)
            y = lax.dot_general(lhs, rhs, (((1,), (1,)), ((), ())), preferred_element_type=F32)
        else:
            rhs = jnp.concatenate([weight[a, b] for a in range(3)], axis=0)
            y = jnp.dot(lhs, rhs, preferred_element_type=F32)
        parts.append(y.reshape(height, WIDTH, CHANS))

    def block(h, half):
        left, mid, right = (part[h, :, half] for part in parts)
        return mid + col_shift(left, 1) + col_shift(right, -1)

    return block


def spread_conv(field, weight):
    pieces = []
    for first, count, taps in ((0, 1, (2,)), (1, 1, (1, 2)), (2, 2, (0, 1, 2)), (4, 1, (0, 1)), (5, 1, (0,))):
        lhs = jnp.concatenate(
            [field[:, first + a - 2 : first + a - 2 + count] for a in taps], axis=-1
        ).reshape(FRAMES * count * WIDTH, len(taps) * CHANS)
        parts = []
        for b in range(3):
            rhs = jnp.concatenate([weight[2 - a, 2 - b] for a in taps], axis=1)
            y = lax.dot_general(lhs, rhs, (((1,), (1,)), ((), ())), preferred_element_type=F32)
            parts.append(y.reshape(FRAMES, count, WIDTH, CHANS))
        pieces += [(parts, k) for k in range(count)]

    def block(t, h, half):
        parts, k = pieces[h]
        left, mid, right = (part[t, k, :, half] for part in parts)
        return mid + col_shift(left, 1) + col_shift(right, -1)

    return block


def blocks(height):
    return [(h, half) for h in range(height) for half in HALVES]


def outer(spot, h, v):
    if h == 0:
        return jnp.where(spot.top, 0.0, v)
    if h == WIDE - 1:
        return jnp.where(spot.bottom, 0.0, v)
    return v


def put_chunks(send, h, half, v):
    for k in range(WIDTH // 16):
        place = h * WIDTH + k * 16
        send[place // PLACES, place % PLACES : place % PLACES + 16, half] = v[
            k * 16 : (k + 1) * 16
        ].astype(BF)


def take_chunks(ref, h, half):
    pieces = []
    for k in range(WIDTH // 16):
        place = h * WIDTH + k * 16
        pieces.append(ref[place // PLACES, place % PLACES : place % PLACES + 16, half])
    return jnp.concatenate(pieces, axis=0).astype(F32)


def transpose_rows(v_ref, out_ref, rows, at_row):
    lane = lax.broadcasted_iota(jnp.int32, (CHANS, WIDTH), 1)
    for t in range(FRAMES):
        for h in range(rows):
            flat = v_ref[t, h].astype(F32).T
            at = pl.ds(at_row(t, h) * WIDTH, WIDTH)
            left = jnp.where(lane == 0, 0.0, pltpu.roll(flat, 1, 1))
            right = jnp.where(lane == WIDTH - 1, 0.0, pltpu.roll(flat, WIDTH - 1, 1))
            out_ref[0:CHANS, at] = left.astype(BF)
            out_ref[CHANS : 2 * CHANS, at] = flat.astype(BF)
            out_ref[2 * CHANS : 3 * CHANS, at] = right.astype(BF)


def ready_body(x_far, in_far, params, x, in_weight, table, flat_mid, sems):
    copies = fetch(sems, (x_far, x), (in_far, in_weight))
    r = params[0:1, :]
    s0 = jnp.broadcast_to(params[2:3, 0:1], (1, CHANS))
    s1 = jnp.broadcast_to(params[2:3, 1:2], (1, CHANS))
    lines = [jnp.exp(-r * s0), jnp.exp(-r * s1), s0, s1, r, params[1:2, :], s0 + s1, r]
    for k, line in enumerate(lines):
        table[k : k + 1, :] = line
    copies[0].wait()
    transpose_rows(x, flat_mid, HEIGHT, lambda t, h: t * HEIGHT + h)
    copies[1].wait()


def place_halos(spot, from_core, from_chip, above, below):
    @pl.when(spot.core == 0)
    def _():
        above[...] = from_chip[...]
        below[...] = from_core[...]

    @pl.when(spot.core == 1)
    def _():
        above[...] = from_core[...]
        below[...] = from_chip[...]

    @pl.when(spot.top)
    def _():
        above[...] = jnp.zeros_like(above)

    @pl.when(spot.bottom)
    def _():
        below[...] = jnp.zeros_like(below)


def drive_body(
    x, from_core, from_chip, weight, table, local, send, edges, above, below
):
    spot = Spot()
    place_halos(spot, from_core, from_chip, above, below)
    for t in range(FRAMES):
        rows = jnp.concatenate([above[t], x[t], below[t]], axis=0)
        drive = conv(rows, weight, False)
        for h, half in blocks(WIDE):
            v = outer(spot, h, drive(h, half))
            if t == 1:
                v = table[1:2, half] * local[0, h, :, half] + v
                put_chunks(send, h, half, v)
            local[t, h, :, half] = v
    total = jnp.broadcast_to(table[6:7, :][None], (BLOCKS, NOTE, CHANS))
    row = lax.broadcasted_iota(jnp.int32, total.shape, 1)
    one = total.astype(BF).astype(F32)
    two = (total - one).astype(BF).astype(F32)
    three = total - one - two
    send[:, PLACES : PLACES + NOTE, :] = jnp.where(
        row == 0, one, jnp.where(row == 1, two, jnp.where(row == 2, three, 0.0))
    ).astype(BF)
    edges[:, 0:2] = above[...]
    edges[:, 2:4] = below[...]


def forward_scan_body(got, table, send, block_decays):
    carry = jnp.zeros((PLACES, CHANS), F32)
    for k in range(BLOCKS):
        send[k] = carry.astype(BF)
        span = jnp.sum(got[k, PLACES : PLACES + NOTE, :].astype(F32), axis=0, keepdims=True)
        d = jnp.exp(-table[4:5, :] * span)
        block_decays[pl.ds(k, 1), :] = d
        carry = d * carry + got[k, 0:PLACES, :].astype(F32)


def backward_scan_body(got, block_decays, send):
    carry = jnp.zeros((PLACES, CHANS), F32)
    for k in reversed(range(BLOCKS)):
        send[k] = carry.astype(BF)
        carry = block_decays[pl.ds(k, 1), :] * carry + got[k].astype(F32)


GELU_A = math.sqrt(2 / math.pi)


def small_rows(rate, skip, steps):
    row = lax.broadcasted_iota(jnp.int32, (8, 128), 0)
    halves = [v[:, half] for v in (rate, skip) for half in HALVES]
    lines = halves + [steps, steps] + halves[0:2]
    out = jnp.zeros((8, 128), F32)
    for k, line in enumerate(lines):
        out = jnp.where(row == k, jnp.broadcast_to(line, (8, 128)), out)
    top = out.astype(BF).astype(F32)
    return jnp.where(row < 5, top, out - top).astype(BF)


def middle_body(
    local, carry, x, cot, weight, table,
    out_far, direct_far, message, state_f, local_adj, send, skip, out, direct, sems,
):
    spot = Spot()
    state, gz = message.at[:, 0:WIDE], message.at[:, WIDE:]
    d0, d1 = table[0:1, :], table[1:2, :]
    for h, half in blocks(WIDE):
        c = take_chunks(carry, h, half)
        s0 = local[0, h, :, half] + d0[:, half] * c
        state_f[h, :, half] = s0
        state[0, h, :, half] = s0.astype(BF)
        s1 = local[1, h, :, half] + (d0 * d1)[:, half] * c
        state[1, h, :, half] = s1.astype(BF)
    totals = [jnp.zeros((8, 128), F32) for _ in HALVES]
    for t in (1, 0):
        pre_act = conv(state[t], weight, False)
        for h, half in blocks(HEIGHT):
            xt = x[t, h, :, half].astype(F32)
            z = pre_act(h, half) + table[5:6, half] * xt
            zz = z * z
            th = jnp.tanh(GELU_A * (z + 0.044715 * (zz * z)))
            gate = 0.5 * (1.0 + th)
            out[t, h, :, half] = (z * gate).astype(BF)
            slope = gate + 0.5 * z * (1.0 - th * th) * (GELU_A * (1.0 + 3 * 0.044715 * zz))
            g = cot[t, h, :, half].astype(F32) * slope
            gz[t, h, :, half] = g.astype(BF)
            direct[t, h, :, half] = (table[5:6, half] * g).astype(BF)
            k = HALVES.index(half)
            totals[k] = totals[k] + jnp.sum((g * xt).reshape(WIDTH // 8, 8, 128), axis=0)
    copies = fetch(sems, (out, out_far), (direct, direct_far))
    grad = spread_conv(gz, weight)
    for t in (1, 0):
        for h, half in blocks(WIDE):
            v = outer(spot, h, grad(t, h, half))
            if t == 0:
                v = v + d1[:, half] * local_adj[1, h, :, half]
                put_chunks(send, h, half, d0[:, half] * v)
            local_adj[t, h, :, half] = v
    total = jnp.concatenate([jnp.sum(v, axis=0, keepdims=True) for v in totals], axis=1)
    skip[...] = total
    for copy in copies:
        copy.wait()


def pack_grad(g, a, scale, out):
    for b in range(3):
        tap = (3 * a + b) * 8
        part = (g[b * CHANS : (b + 1) * CHANS] * scale).astype(BF)
        out[:, tap : tap + 8, :] = part.reshape(GROUPS, 8, CHANS)


def out_grad(state, gz, flat):
    transpose_rows(state, flat, WIDE, lambda t, h: t * WIDE + h)
    rhs = gz[...].reshape(FRAMES * HEIGHT * WIDTH, CHANS)
    for a in range(3):
        lhs = jnp.concatenate(
            [flat[:, pl.ds((t * WIDE + a) * WIDTH, HEIGHT * WIDTH)] for t in range(FRAMES)], axis=1
        )
        yield a, jnp.dot(lhs, rhs, preferred_element_type=F32)


def in_grad(adj, flat_mid, edges, flat_edge):
    transpose_rows(edges, flat_edge, 4, lambda t, h: t * 4 + h)
    rhs = adj[...].reshape(FRAMES * WIDE * WIDTH, CHANS)
    for a in range(3):
        pieces = []
        for t in range(FRAMES):
            at = t * 4 * WIDTH
            if a < 2:
                pieces.append(flat_edge[:, at + a * WIDTH : at + 2 * WIDTH])
            pieces.append(flat_mid[:, at : at + 4 * WIDTH])
            if a > 0:
                pieces.append(flat_edge[:, at + 2 * WIDTH : at + (2 + a) * WIDTH])
        yield a, jnp.dot(jnp.concatenate(pieces, axis=1), rhs, preferred_element_type=F32)


def adjoint_stage(scales, spot, sources, adj, small):
    local, incoming, state_f, carry, table, skip = sources
    d0, d1 = table[0:1, :], table[1:2, :]
    sums = [[jnp.zeros((8, 128), F32) for _ in HALVES] for _ in range(FRAMES)]
    for h, half in blocks(WIDE):
        c = take_chunks(incoming, h, half)
        a0 = local[0, h, :, half] + d1[:, half] * c
        a1 = local[1, h, :, half] + c
        adj[0, h, :, half] = a0.astype(BF)
        adj[1, h, :, half] = a1.astype(BF)
        k = HALVES.index(half)
        pairs = ((a0, take_chunks(carry, h, half)), (a1, state_f[h, :, half]))
        for t, (a, earlier) in enumerate(pairs):
            sums[t][k] = sums[t][k] + jnp.sum((a * earlier).reshape(WIDTH // 8, 8, 128), axis=0)
    k0, k1 = (
        jnp.concatenate([jnp.sum(v, axis=0, keepdims=True) for v in pair], axis=1) * d
        for pair, d in zip(sums, (d0, d1))
    )
    rate = (k0 * table[2:3, :] + k1 * table[3:4, :]) * (-scales[0])
    s0 = jnp.sum(k0 * table[4:5, :], axis=1, keepdims=True) * (-scales[1])
    s1 = jnp.sum(k1 * table[4:5, :], axis=1, keepdims=True) * (-scales[1])
    lane = lax.broadcasted_iota(jnp.int32, (1, 128), 1)
    at = spot.place * FRAMES
    steps = jnp.where(lane == at, s0, jnp.where(lane == at + 1, s1, 0.0))
    small[...] = small_rows(rate, skip[...] * scales[0], steps)


def odd_grad_body(
    scales, local, incoming, state_f, carry, table, skip, flat_mid, edges, message, flat_message,
    payload, out_part, adj, small, flat, flat_edge,
):
    spot = Spot()

    @pl.when(spot.core == 0)
    def _():
        payload[...] = flat_message[...]

    @pl.when(spot.core == 1)
    def _():
        adjoint_stage(scales, spot, (local, incoming, state_f, carry, table, skip), adj, small)
        for a, g in in_grad(adj, flat_mid, edges, flat_edge):
            pack_grad(g, a, scales[0], payload)
        for a, g in out_grad(message.at[:, 0:WIDE], message.at[:, WIDE:], flat):
            pack_grad(g, a, scales[0], out_part)


def adjoint_body(
    scales, local, incoming, state_f, carry, table, skip, odd_adj, odd_small,
    adj, to_core, to_chip, small,
):
    spot = Spot()

    @pl.when(spot.core == 0)
    def _():
        adjoint_stage(scales, spot, (local, incoming, state_f, carry, table, skip), adj, small)
        to_chip[...] = adj[:, 0:2]
        to_core[...] = adj[:, WIDE - 2 :]

    @pl.when(spot.core == 1)
    def _():
        to_core[...] = odd_adj[:, 0:2]
        to_chip[...] = odd_adj[:, WIDE - 2 :]
        adj[...] = odd_adj[...]
        small[...] = odd_small[...]


def even_grad_body(scale, adj, flat_mid, edges, mine, flat_edge):
    @pl.when(Spot().core == 0)
    def _():
        for a, g in in_grad(adj, flat_mid, edges, flat_edge):
            pack_grad(g, a, scale, mine)


def grad_inputs_body(
    adj_far, core_far, chip_far, weight_far, direct_far,
    out_far, adj, from_core, from_chip, weight, direct, out, above, below, sems,
):
    spot = Spot()
    copies = fetch(
        sems,
        (core_far, from_core),
        (chip_far, from_chip),
        (adj_far, adj),
        (weight_far, weight),
        (direct_far, direct),
    )
    for copy in copies:
        copy.wait()
    place_halos(spot, from_core, from_chip, above, below)
    for t in range(FRAMES):
        up = (adj[t, 0:2].astype(F32) + above[t].astype(F32)).astype(BF)
        down = (adj[t, WIDE - 2 :].astype(F32) + below[t].astype(F32)).astype(BF)
        rows = jnp.concatenate([up, adj[t, 2 : WIDE - 2], down], axis=0)
        grad = conv(rows, weight, True)
        for h, half in blocks(HEIGHT):
            own = direct[t, h, :, half].astype(F32)
            out[t, h, :, half] = (grad(h, half) + own).astype(BF)
    (copy,) = fetch(sems, (out, out_far))
    copy.wait()


def pair_sum_body(scale, mine, out_part, got, message, send_far, send, flat, sems):
    core = Spot().core

    @pl.when(core == 0)
    def _():
        copies = []
        for k in range(GROUPS):
            total = mine[k].astype(F32) + got[k, 0:TAPS, :].astype(F32)
            for lg, half in enumerate(HALVES):
                send[k, lg] = total[:, half].astype(BF)
            if k % 8 == 7:
                part = slice(k - 7, k + 1)
                copies += fetch(sems.at[k // 8 : k // 8 + 1], (send.at[part], send_far.at[part]))
        for copy in copies:
            copy.wait()

    @pl.when(core == 1)
    def _():
        copies = []
        for a, g in out_grad(message.at[:, 0:WIDE], message.at[:, WIDE:], flat):
            for b in range(3):
                tap = (3 * a + b) * 8
                own = out_part[:, tap : tap + 8, :].astype(F32)
                total = g[b * CHANS : (b + 1) * CHANS].reshape(GROUPS, 8, CHANS) * scale + own
                for lg, half in enumerate(HALVES):
                    send[:, lg, tap : tap + 8, :] = total[:, :, half].astype(BF)
            part = slice(24 * a, 24 * a + 24)
            copies += fetch(sems.at[a : a + 1], (send.at[:, :, part], send_far.at[:, :, part]))
        for copy in copies:
            copy.wait()


def all_sum_body(got, small, send):
    total = jnp.zeros((TAPS, 128), F32)
    for k in range(CHIPS):
        total = total + got[k].astype(F32)
    total = jnp.concatenate([total.astype(BF), small[...]], axis=0)
    send[...] = jnp.broadcast_to(total[None], send.shape)


def write_grad(src, grad, stage, sems):
    copies = []
    for tap in range(9):
        a, b = tap // 3, tap % 3
        for lg, half in enumerate(HALVES):
            part = src[:, lg, tap * 8 : tap * 8 + 8, :].astype(F32)
            stage[a, b, :, half] = part.reshape(CHANS, 128)
        copies += fetch(sems.at[tap : tap + 1], (stage.at[a, b], grad.at[a, b]))
    return copies


def unpack_own_body(own, grad_out, grad_in, stage, sems):
    core = Spot().core

    @pl.when(core == 0)
    def _():
        for copy in write_grad(own, grad_in, stage, sems):
            copy.wait()

    @pl.when(core == 1)
    def _():
        for copy in write_grad(own, grad_out, stage, sems):
            copy.wait()


def unpack_other_body(
    own, got, out_half, in_half, grad_out, grad_in, rate_far, skip_far, step_far,
    stage, rate, skip, step, sems,
):
    del out_half, in_half
    spot = Spot()
    total = jnp.zeros((8, 128), F32)
    for k in range(GROUPS):
        for lg in range(2):
            pair = own[k, lg, TAPS:PACK, :].astype(F32) + got[k, lg, TAPS:PACK, :].astype(F32)
            total = total + pair
    rate[...] = total[0:2] + total[6:8]
    skip[...] = total[2:4]
    steps = total + pltpu.roll(total, 7, 0)
    step[...] = pltpu.roll(steps, (128 - spot.place * FRAMES) % 128, 1)[4:5, 0:FRAMES]
    smalls = fetch(sems.at[9:12], (rate, rate_far), (skip, skip_far), (step, step_far))

    @pl.when(spot.core == 0)
    def _():
        for copy in write_grad(got, grad_out, stage, sems):
            copy.wait()

    @pl.when(spot.core == 1)
    def _():
        for copy in write_grad(got, grad_in, stage, sems):
            copy.wait()

    for copy in smalls:
        copy.wait()


ROWS_AXES = ("z", "core")
TM_AXES = ("x", "y")
CORE_PAIRS = [(i, i ^ 1) for i in range(8)]
CHIP_PAIRS = [(i, (i + 1) % 8 if i % 2 else (i - 1) % 8) for i in range(8)]


def halos(to_core, to_chip):
    from_chip = lax.ppermute(to_chip, ROWS_AXES, CHIP_PAIRS)
    from_core = lax.ppermute(to_core, ROWS_AXES, CORE_PAIRS)
    return from_core, from_chip


def swap(chunks, axes):
    return lax.all_to_all(chunks, axes, 0, 0)


def vmem(shape, dtype=BF):
    return pltpu.VMEM(shape, dtype)


def sems(*shape):
    return pltpu.SemaphoreType.DMA(shape)


def on_device(inputs, in_weight, out_weight, skip_gain, rates, step_sizes, cotangent):
    scale = 1.0 / math.sqrt(32 * 32 * 128)
    step_scale = 1.0 / math.sqrt(1048576)
    core = lax.axis_index("core")
    field = (FRAMES, HEIGHT, WIDTH, CHANS)
    wide = (FRAMES, WIDE, WIDTH, CHANS)
    message = (FRAMES, WIDE + HEIGHT, WIDTH, CHANS)
    edge = (FRAMES, 2, WIDTH, CHANS)
    kernel = (3, 3, CHANS, CHANS)
    chunk = sds((BLOCKS, PLACES, CHANS), BF)
    packed = sds((GROUPS, 2, PACK, 128), BF)
    part = sds((GROUPS, TAPS, CHANS), BF)
    scales = (scale, step_scale)
    flat = sds((3 * CHANS, FRAMES * 4 * WIDTH), BF)
    params = jnp.concatenate([rates, skip_gain, jnp.pad(step_sizes, (0, CHANS - FRAMES))])
    params = params.reshape(3, CHANS)

    to_core = lax.dynamic_slice(inputs, (0, 2 - 2 * core, 0, 0), edge)
    to_chip = lax.dynamic_slice(inputs, (0, 2 * core, 0, 0), edge)
    from_core, from_chip = halos(to_core, to_chip)
    x, in_w, table, flat_mid = call(
        ready_body,
        [sds(field, BF), sds(kernel, BF), sds((8, CHANS), F32), flat],
        [far(inputs), far(in_weight), params],
        2 * ROW_FLOPS,
        [sems(2)],
    )
    local, send, edges = call(
        drive_body,
        [sds(wide, F32), sds((BLOCKS, PLACES + NOTE, CHANS), BF), sds(field, BF)],
        [x, from_core, from_chip, in_w, table],
        WIDE * ROW_FLOPS,
        [vmem(edge), vmem(edge)],
    )
    got = swap(send, TM_AXES)
    send, block_decays = call(forward_scan_body, [chunk, sds((BLOCKS, CHANS), F32)], [got, table])
    carry = swap(send, TM_AXES)
    outputs, direct, sent, state_f, local_adj, send, skip = call(
        middle_body,
        [
            far(sds(field, BF)),
            far(sds(field, BF)),
            sds(message, BF),
            sds(wide[1:], F32),
            sds(wide, F32),
            chunk,
            sds((1, CHANS), F32),
        ],
        [local, carry, x, cotangent, out_weight, table],
        (HEIGHT + WIDE) * ROW_FLOPS,
        [vmem(field), vmem(field), sems(2)],
    )
    got = swap(send, TM_AXES)
    (send,) = call(backward_scan_body, [chunk], [got, block_decays])
    incoming = swap(send, TM_AXES)
    sources = [local_adj, incoming, state_f, carry, table, skip, flat_mid, edges]
    flat_sent = sent.reshape(GROUPS, PACK, CHANS)
    payload, out_part, odd_adj, odd_small = call(
        functools.partial(odd_grad_body, scales),
        [sds(flat_sent.shape, BF), part, sds(wide, BF), sds((8, 128), BF)],
        [*sources, sent, flat_sent],
        WIDE * ROW_FLOPS,
        [vmem((3 * CHANS, FRAMES * WIDE * WIDTH)), vmem(flat.shape)],
    )
    got = lax.ppermute(payload, ROWS_AXES, CORE_PAIRS)
    adj, to_core, to_chip, small = call(
        functools.partial(adjoint_body, scales),
        [sds(wide, BF), sds(edge, BF), sds(edge, BF), sds((8, 128), BF)],
        [*sources[:6], odd_adj, odd_small],
    )
    from_core, from_chip = halos(to_core, to_chip)
    (mine,) = call(
        functools.partial(even_grad_body, scale),
        [part],
        [adj, flat_mid, edges],
        0,
        [vmem(flat.shape)],
        light=True,
    )
    (send,) = call(
        functools.partial(pair_sum_body, scale),
        [far(sds((GROUPS, 2, TAPS, 128), BF))],
        [mine, out_part, got, got.reshape(message)],
        0,
        [
            vmem((GROUPS, 2, TAPS, 128)),
            vmem((3 * CHANS, FRAMES * WIDE * WIDTH)),
            sems(4),
        ],
        light=True,
    )
    got = swap(send.reshape(CHIPS, TAPS, 128), ("x", "y", "z"))
    (grad_inputs,) = call(
        grad_inputs_body,
        [far(sds(field, BF))],
        [far(a) for a in (adj, from_core, from_chip, in_weight, direct)],
        100 * ROW_FLOPS,
        [
            vmem(wide),
            vmem(edge),
            vmem(edge),
            vmem(kernel),
            vmem(field),
            vmem(field),
            vmem(edge),
            vmem(edge),
            sems(5),
        ],
        {4: 0},
    )
    small, grad_inputs = lax.optimization_barrier((small, grad_inputs))
    (send,) = call(all_sum_body, [sds((CHIPS, PACK, 128), BF)], [got, small])
    own = swap(send, ("x", "y", "z"))
    own = own.reshape(packed.shape)
    other = lax.ppermute(own, ROWS_AXES, CORE_PAIRS)
    weights = sds(kernel, F32)
    half = sds((2, 128), F32)
    stage = vmem(kernel, F32)
    grad_out_weight, grad_in_weight = call(
        unpack_own_body, [far(weights), far(weights)], [own], 0, [stage, sems(9)]
    )
    grad_out_weight, grad_in_weight, grad_rates, grad_skip, grad_steps = call(
        unpack_other_body,
        [far(a) for a in (weights, weights, half, half, sds((1, FRAMES), F32))],
        [own, other, far(grad_out_weight), far(grad_in_weight)],
        0,
        [stage, vmem((2, 128), F32), vmem((2, 128), F32), vmem((1, FRAMES), F32), sems(12)],
        {2: 0, 3: 1},
    )
    return (
        outputs,
        grad_inputs,
        grad_in_weight,
        grad_out_weight,
        grad_skip.reshape(CHANS),
        grad_rates.reshape(CHANS),
        grad_steps.reshape(FRAMES),
    )


def solution(mesh):
    fine = Mesh(mesh.devices.reshape(4, 4, 4, 2), ("x", "y", "z", "core"))
    spread_out = P(TM_AXES, ROWS_AXES, None, None)
    placed = (spread_out, P(), P(), P(), P(), P(TM_AXES), spread_out)
    return jax.shard_map(
        on_device,
        mesh=fine,
        in_specs=placed,
        out_specs=(spread_out, spread_out, P(), P(), P(), P(), P(TM_AXES)),
        check_vma=False,
    )
```
